256 devices in a mesh: rad: 4 (over x), lat: 8 (over y, core), lon: 8 (over z).
Axes of the slice: x: 4, y: 4, z: 8, core: 2. Of those that a mesh axis runs over, the one named last changes fastest.
Arguments:
- forcing: float32 [3, 32, 256, 1024], P(None, 'rad', 'lat', 'lon'), may hold values from -6 to 6
- pressure: float32 [32, 256, 1024], P('rad', 'lat', 'lon'), may hold values from -6 to 6
- viscosity: float32 [32, 256, 1024], P('rad', 'lat', 'lon'), may hold values from 0.01 to 100
- forward_velocity: float32 [3, 32, 256, 1024], P(None, 'rad', 'lat', 'lon'), may hold values from -6 to 6
- coarse_owner: int32 [8, 64, 256], P('rad', 'lat', 'lon'), may hold values from 0 to 1023, as said below
Outputs:
- adjoint_velocity: float32 [3, 32, 256, 1024], P(None, 'rad', 'lat', 'lon')
- pressure_next: float32 [32, 256, 1024], P('rad', 'lat', 'lon')
- viscosity_gradient: float32 [32, 256, 1024], P('rad', 'lat', 'lon')
The draws below stay inside these ranges and needn't reach their ends.
Inputs may be any that keep to these rules, and one draw needn't show every extreme that they name: `coarse_owner`: aggregates are blocks of 2 x 8 level-two cells across the first two dimensions by one of 32 runs of varied lengths along the third; the runs are the same for all blocks, every aggregate has members, and a new run begins at every multiple of 32 along the third dimension. Aggregate numbers are (block along the first dimension times blocks along the second plus block along the second) times 32 plus the run's number, runs numbered in order along the third dimension starting at cell 0.
All inputs are finite; a program needn't handle non-finite values.
Results may differ from the reference program's by a relative error of at most 0.0003.
Values sent between devices are 32-bit elements; how exact they have to be, the bound alone decides.
A program may use at most 192 MiB of HBM per device.

```python
import math
import jax
import jax.numpy as jnp
from jax import lax

CZ = 128
AX = 2
AY = 8
ZSEG = 32
DEG = 3
CDEG = 8
NX = 32
NY = 256
NZ = 1024
NC = 1024


def draw_coarse_owner(key, part):
    key = jax.random.fold_in(key, 7)
    cells_x = NX // 4
    cells_y = NY // 4
    cells_z = NZ // 4
    device_cells = CZ // 4
    positions = jnp.arange(1, cells_z).astype(jnp.int32)
    ranking = jax.random.permutation(key, cells_z - 1).astype(jnp.int32)
    scores = ranking - jnp.where(positions % device_cells == 0, cells_z, 0).astype(jnp.int32)
    order = jnp.argsort(scores)
    cut_points = jnp.sort(positions[order[:ZSEG - 1]])
    position = jnp.arange(cells_z).astype(jnp.int32)
    segment = jnp.sum((position[:, None] >= cut_points[None, :]).astype(jnp.int32), axis=1)
    block_x = jnp.arange(cells_x) // AX
    block_y = jnp.arange(cells_y) // AY
    owners = (block_x[:, None, None] * (cells_y // AY) + block_y[None, :, None]) * ZSEG + segment[None, None, :]
    return owners.astype(jnp.int32)


def smooth_load(key):
    phase = jax.random.uniform(key, (3,), jnp.float32, 0.0, 6.283185)
    weight = jnp.array([1.0, 0.7, 0.5], jnp.float32)
    radial = (jnp.arange(NX).astype(jnp.float32) + 0.5) / NX
    along = jnp.arange(NZ).astype(jnp.float32) / NZ
    shape_x = 1.0 + 1.5 * jnp.cos(3.141593 * radial)
    shape_z = 1.0 + 0.5 * jnp.sin(6.283185 * along[None, :] + phase[:, None])
    return weight[:, None, None, None] * shape_x[None, :, None, None] * shape_z[:, None, None, :]


def draw_forcing(key, part):
    key = jax.random.fold_in(key, 11)
    noise_key, shape_key = jax.random.split(key)
    noise = jax.random.truncated_normal(noise_key, -2.0, 2.0, (3, NX, NY, NZ), jnp.float32)
    smooth = smooth_load(shape_key)
    return (noise + smooth).astype(jnp.float32)


def block_levels(key, dims, shards, least, top_value):
    def one(axis_at, shards_of):
        draws = jax.random.uniform(jax.random.fold_in(jax.random.fold_in(key, 6), axis_at), (shards_of,), jnp.float32, least / len(shards), top_value / len(shards))
        return jnp.repeat(jnp.exp(draws), dims[axis_at] // shards_of).reshape((-1,) + (1,) * (len(dims) - axis_at - 1))

    level = one(*shards[0])
    for cut in shards[1:]:
        level = level * one(*cut)
    return level


def centred(rng, dims, scale, bound, cuts=(), kind=jnp.bfloat16):
    entries = jax.random.normal(rng, dims, jnp.float32) * scale
    if len(cuts) > 0:
        entries = block_levels(rng, dims, cuts, -0.22, 0.18) * entries
    return jnp.clip(entries, min=-bound, max=bound).astype(kind)


def setup_inputs(seed: int = 0) -> dict:
    splits = jax.random.split(jax.random.key(seed), 6)
    return {
        "forcing": draw_forcing(jax.random.fold_in(splits[5], 71), 0),
        "pressure": centred(splits[1], (NX, NY, NZ), 1.0, 6.0, ((0, 4), (1, 8), (2, 8)), jnp.float32),
        "viscosity": jnp.clip(jnp.exp(math.log(100.0) - 9.2103404 * jax.random.uniform(splits[2], (NX, NY, NZ), jnp.float32) ** block_levels(splits[2], (NX, NY, NZ), ((0, 4), (1, 8), (2, 8)), -0.2, 0.2)), 0.01, 100.0),
        "forward_velocity": centred(splits[3], (3, NX, NY, NZ), 1.0, 6.0, ((1, 4), (2, 8), (3, 8)), jnp.float32),
        "coarse_owner": draw_coarse_owner(jax.random.fold_in(splits[5], 71), 0),
    }


FINE_LOW = 0.5
FINE_HIGH = 2.0
COARSE_LOW = 0.1
COARSE_HIGH = 2.0


def chebyshev(operate, inverse_diag, solution, residual, low, high, degree):
    middle = 0.5 * (high + low)
    spread = 0.5 * (high - low)
    factor = middle / spread
    carry_old = 1.0 / factor
    update = inverse_diag * residual / middle
    solution = solution + update
    for sweep in range(degree - 1):
        residual = residual - operate(update)
        carry_new = 1.0 / (2.0 * factor - carry_old)
        update = carry_new * carry_old * update + (2.0 * carry_new / spread) * inverse_diag * residual
        solution = solution + update
        carry_old = carry_new
    return solution, residual, update


def stencil(links, diagonal, vector):
    summed = diagonal * vector
    for direction in range(3):
        position = vector.ndim - 3 + direction
        summed = summed - links[2 * direction] * jnp.roll(vector, 1, position) - links[2 * direction + 1] * jnp.roll(vector, -1, position)
    return summed


def coarsen_face(values, direction, side):
    size_x, size_y, size_z = values.shape
    blocks = values.reshape(size_x // 2, 2, size_y // 2, 2, size_z // 2, 2)
    weights = []
    for other in range(3):
        if other == direction:
            weights.append(jnp.array([1.0 - side, float(side)], jnp.float32))
        else:
            weights.append(jnp.ones((2,), jnp.float32))
    scaled = blocks * weights[0][None, :, None, None, None, None] * weights[1][None, None, None, :, None, None] * weights[2][None, None, None, None, None, :]
    return scaled.sum(axis=(1, 3, 5))


def coarsen_level(faces, links):
    new_faces = jnp.stack([coarsen_face(faces[k], k // 2, k % 2) for k in range(6)])
    new_links = jnp.stack([coarsen_face(links[k], k // 2, k % 2) for k in range(6)])
    diagonal = new_faces[0] + new_faces[1] + new_faces[2] + new_faces[3] + new_faces[4] + new_faces[5]
    return new_faces, new_links, diagonal


def restrict(vector):
    comps, size_x, size_y, size_z = vector.shape
    return vector.reshape(comps, size_x // 2, 2, size_y // 2, 2, size_z // 2, 2).sum(axis=(2, 4, 6))


def prolong(vector):
    return jnp.repeat(jnp.repeat(jnp.repeat(vector, 2, axis=1), 2, axis=2), 2, axis=3)


def fine_faces(viscosity, neighbours, masks):
    lower_x, upper_x, lower_y, upper_y = masks
    prev_x, next_x, prev_y, next_y, prev_z, next_z = neighbours
    faces = jnp.stack([0.5 * (viscosity + lower_x * prev_x), 0.5 * (viscosity + upper_x * next_x),
                       0.5 * (viscosity + lower_y * prev_y), 0.5 * (viscosity + upper_y * next_y),
                       0.5 * (viscosity + prev_z), 0.5 * (viscosity + next_z)])
    links = jnp.stack([faces[0] * lower_x, faces[1] * upper_x, faces[2] * lower_y, faces[3] * upper_y, faces[4], faces[5]])
    diagonal = faces[0] + faces[1] + faces[2] + faces[3] + faces[4] + faces[5]
    return faces, links, diagonal


def galerkin_term(owners, owner_neighbours, links, diagonal, count):
    row_ids = owners.reshape(-1)
    key_list = [row_ids * count + row_ids]
    value_list = [diagonal.reshape(-1)]
    for k in range(6):
        key_list.append(row_ids * count + owner_neighbours[k].reshape(-1))
        value_list.append(-links[k].reshape(-1))
    summed = jax.ops.segment_sum(jnp.concatenate(value_list), jnp.concatenate(key_list), num_segments=count * count)
    return summed.reshape(count, count)


def aggregate_sums(residual, owners, count):
    flat = residual.reshape(residual.shape[0], -1).T
    return jax.ops.segment_sum(flat, owners.reshape(-1), num_segments=count).T


def strain_sum(forward_grads, adjoint_grads):
    summed = jnp.zeros_like(forward_grads[0][0])
    for d in range(3):
        for e in range(3):
            sym_forward = 0.5 * (forward_grads[e][d] + forward_grads[d][e])
            sym_adjoint = 0.5 * (adjoint_grads[e][d] + adjoint_grads[d][e])
            summed = summed + sym_forward * sym_adjoint
    return summed


def vcycle(levels, coarse, level, right):
    links, diagonal = levels[level]

    def operate(vector):
        return stencil(links, diagonal, vector)

    inverse = 1.0 / diagonal
    solution, residual, update = chebyshev(operate, inverse, jnp.zeros_like(right), right, FINE_LOW, FINE_HIGH, DEG)
    residual = residual - operate(update)
    if level == 2:
        correction = coarse(residual)
    else:
        correction = prolong(vcycle(levels, coarse, level + 1, restrict(residual)))
    solution = solution + correction
    residual = residual - operate(correction)
    solution, residual, update = chebyshev(operate, inverse, solution, residual, FINE_LOW, FINE_HIGH, DEG)
    return solution


def reference(forcing, pressure, viscosity, forward_velocity, coarse_owner):
    size_x, size_y, size_z = viscosity.shape
    gx = jnp.arange(size_x)
    gy = jnp.arange(size_y)
    lower_x = (gx > 0).astype(jnp.float32)[:, None, None]
    upper_x = (gx < size_x - 1).astype(jnp.float32)[:, None, None]
    lower_y = (gy > 0).astype(jnp.float32)[None, :, None]
    upper_y = (gy < size_y - 1).astype(jnp.float32)[None, :, None]
    neighbours = [jnp.roll(viscosity, 1, 0), jnp.roll(viscosity, -1, 0), jnp.roll(viscosity, 1, 1),
                  jnp.roll(viscosity, -1, 1), jnp.roll(viscosity, 1, 2), jnp.roll(viscosity, -1, 2)]
    faces, links, diagonal = fine_faces(viscosity, neighbours, (lower_x, upper_x, lower_y, upper_y))
    levels = [(links, diagonal)]
    for level in range(2):
        faces, links, diagonal = coarsen_level(faces, links)
        levels.append((links, diagonal))
    owner_neighbours = [jnp.roll(coarse_owner, 1, 0), jnp.roll(coarse_owner, -1, 0), jnp.roll(coarse_owner, 1, 1),
                        jnp.roll(coarse_owner, -1, 1), jnp.roll(coarse_owner, 1, 2), jnp.roll(coarse_owner, -1, 2)]
    matrix = galerkin_term(coarse_owner, owner_neighbours, levels[2][0], levels[2][1], NC)
    coarse_inverse = 1.0 / jnp.diagonal(matrix)

    def dense_apply(vector):
        return jnp.dot(vector, matrix, precision=lax.Precision.HIGHEST)

    def coarse(residual):
        right = aggregate_sums(residual, coarse_owner, NC)
        solution, last, update = chebyshev(dense_apply, coarse_inverse, jnp.zeros_like(right), right, COARSE_LOW, COARSE_HIGH, CDEG)
        return jnp.take(solution, coarse_owner, axis=1)

    pressure_grad = jnp.stack([jnp.roll(pressure, -1, 0) * upper_x - pressure,
                               jnp.roll(pressure, -1, 1) * upper_y - pressure,
                               jnp.roll(pressure, -1, 2) - pressure])
    right = forcing - pressure_grad
    adjoint = vcycle(levels, coarse, 0, right)
    divergence = (adjoint[0] - lower_x * jnp.roll(adjoint[0], 1, 0)) + (adjoint[1] - lower_y * jnp.roll(adjoint[1], 1, 1)) + (adjoint[2] - jnp.roll(adjoint[2], 1, 2))
    raw = pressure - viscosity * divergence
    pressure_next = raw - jnp.sum(raw) / (size_x * size_y * size_z)
    upper = [upper_x, upper_y, jnp.ones((1, 1, 1), jnp.float32)]

    def gradients(velocity):
        return [[jnp.roll(velocity[e], -1, d) * upper[d] - velocity[e] for d in range(3)] for e in range(3)]

    viscosity_gradient = 2.0 * viscosity * strain_sum(gradients(forward_velocity), gradients(adjoint))
    return adjoint, pressure_next, viscosity_gradient
```

```python
import functools

import jax
import jax.numpy as jnp
from jax import lax
from jax.experimental import pallas as pl
from jax.experimental.pallas import tpu as pltpu
from jax.sharding import PartitionSpec as P

AXES = ("rad", "lat", "lon")
SIZES = (4, 8, 8)
MESH = pl.DeviceIdType.MESH
F32 = jnp.float32
HI = lax.Precision.HIGHEST
CDEG = 8
CELLS = 32 * 256 * 1024
LEVELS = ((8, 32, 128), (4, 16, 64), (2, 8, 32))
TOP = 8


def cheb_constants(low, high, degree):
    middle, spread = 0.5 * (high + low), 0.5 * (high - low)
    factor = middle / spread
    old = 1.0 / factor
    steps = []
    for _ in range(degree - 1):
        new = 1.0 / (2.0 * factor - old)
        steps.append((new * old, 2.0 * new / spread))
        old = new
    return 1.0 / middle, steps


FIRST, STEPS = cheb_constants(0.5, 2.0, 3)
COARSE_FIRST, COARSE_STEPS = cheb_constants(0.1, 2.0, CDEG)


def lanes_of(shape):
    return lax.broadcasted_iota(jnp.int32, shape, len(shape) - 1)


def rows_of(shape):
    return lax.broadcasted_iota(jnp.int32, shape, len(shape) - 2)


def block(x, rows):
    return pl.ds(pl.multiple_of(x * rows, 8), rows)


def kernel(
    forcing, pressure, viscosity, forward, owner,
    adjoint, pnext, gradient,
    load, base, fwd, base_z, fwd_z,
    buf0, buf1, buf2, zbuf, faces0, faces1, faces2, links0, links1, links2,
    diag0, diag1, diag2, inv0, inv1, inv2, res0, res1, res2, sol0, sol1, sol2,
    tmp, flat, erows, tile, got1, got2,
    in_sem, send_sem, recv_sem, fsend, frecv, send1, recv1, send2, recv2,
):
    bufs = (buf0, buf1, buf2)
    faces, links = (faces0, faces1, faces2), (links0, links1, links2)
    diags, invs = (diag0, diag1, diag2), (inv0, inv1, inv2)
    ress, sols = (res0, res1, res2), (sol0, sol1, sol2)
    me = tuple(lax.axis_index(a) for a in AXES)
    rad, lat, lon = me

    def device(*steps):
        return tuple(
            lax.rem(m + (s % n), n) if s % n else m for m, s, n in zip(me, steps, SIZES)
        )

    up = [device(1, 0, 0), device(0, 1, 0), device(0, 0, 1)]
    down = [device(-1, 0, 0), device(0, -1, 0), device(0, 0, -1)]
    along = [device(0, 0, k) for k in range(1, 8)]
    across = [device(a, b, 0) for a in range(4) for b in range(8) if a or b]

    own_rows = pl.ds(TOP, 32)
    loads = [
        pltpu.make_async_copy(viscosity, base.at[0, pl.ds(1, 8), own_rows], in_sem.at[0]),
        pltpu.make_async_copy(pressure, base.at[1, pl.ds(1, 8), own_rows], in_sem.at[1]),
        pltpu.make_async_copy(forcing, load, in_sem.at[2]),
        pltpu.make_async_copy(forward, fwd.at[:, pl.ds(1, 8), own_rows], in_sem.at[3]),
    ]
    for copy in loads:
        copy.start()

    barrier = pltpu.get_barrier_semaphore()
    for target in along + across:
        pl.semaphore_signal(barrier, inc=1, device_id=target, device_id_type=MESH)

    def remote(src, dst, ssem, rsem, target):
        return pltpu.make_async_remote_copy(
            src_ref=src, dst_ref=dst, send_sem=ssem, recv_sem=rsem,
            device_id=target, device_id_type=MESH,
        )

    lane8 = lanes_of((8, 128))

    def pack(accs, plane, c, x, level, lows=True, highs=True):
        nx, ny, width = LEVELS[level]
        low, high = accs
        for g in range(ny // 8):
            q = (c * nx + x) * (ny // 8) + g
            turned = pltpu.roll(plane[8 * g : 8 * g + 8], q, 1)
            if lows:
                low = jnp.where(lane8 == q, turned, low)
            if highs:
                high = jnp.where(lane8 == lax.rem(q + width - 1, 128), turned, high)
        return low, high

    zero8 = jnp.zeros((8, 128), F32)

    def merged(level, before, after):
        width = LEVELS[level][2]
        if level == 0:
            return before, after
        left = pltpu.roll(before, 128 - width, 1)
        right = pltpu.roll(after, width, 1)
        return jnp.where((lane8 >= width) & (lane8 < width + 32), right, left)

    def shifted(level, v, halo, c, x):
        nx, ny, width = LEVELS[level]
        groups = ny // 8
        lane = lanes_of((ny, 128))
        q = (c * nx + x) * groups
        if level == 0:
            before, after = halo
            left = [pltpu.roll(before, lax.rem(257 - q - g, 128), 1) for g in range(groups)]
            right = [pltpu.roll(after, lax.rem(255 - q - g, 128), 1) for g in range(groups)]
            low = jnp.where(lane == 0, jnp.concatenate(left, 0), pltpu.roll(v, 1, 1))
            high = jnp.where(lane == 127, jnp.concatenate(right, 0), pltpu.roll(v, 127, 1))
            return low, high
        if halo.shape[0] == 8:
            rim = [pltpu.roll(halo, lax.rem(128 - q - g, 128), 1) for g in range(groups)]
            rim = jnp.concatenate(rim, 0) if groups > 1 else rim[0]
        else:
            rim = jnp.broadcast_to(halo[c : c + 1], (ny, 128))
        wide = jnp.where(lane < width, v, rim)
        return pltpu.roll(wide, 1, 1), pltpu.roll(wide, 127, 1)

    def sends(level, p, buf):
        nx, ny, _ = LEVELS[level]
        rows, planes = pl.ds(TOP, ny), pl.ds(1, nx)
        parts = [
            (buf.at[:, nx, rows], buf.at[:, 0, rows], up[0]),
            (buf.at[:, 1, rows], buf.at[:, nx + 1, rows], down[0]),
            (buf.at[:, planes, pl.ds(TOP + ny - 1, 1)], buf.at[:, planes, pl.ds(TOP - 1, 1)], up[1]),
            (buf.at[:, planes, pl.ds(TOP, 1)], buf.at[:, planes, pl.ds(TOP + ny, 1)], down[1]),
            (zbuf.at[p, 1], zbuf.at[p, 2], up[2]),
            (zbuf.at[p, 0], zbuf.at[p, 3], down[2]),
        ]
        return [
            remote(src, dst, send_sem.at[p, i], recv_sem.at[p, i], target)
            for i, (src, dst, target) in enumerate(parts)
        ]

    turn = [0]

    def exchange(level, accs, buf=None):
        p = turn[0] % 2
        turn[0] += 1
        zbuf[p, 0], zbuf[p, 1] = accs
        copies = sends(level, p, bufs[level].at[p] if buf is None else buf)
        for copy in copies:
            copy.start()

        def finish():
            for copy in copies:
                copy.wait()
            return merged(level, zbuf[p, 2], zbuf[p, 3])

        return finish

    def parity():
        return turn[0] % 2

    for copy in loads[:2]:
        copy.wait()

    def pack_base(x, accs):
        for c in range(2):
            accs = pack(accs, base[c, x + 1, own_rows, :], c, x, 0)
        return accs

    accs = lax.fori_loop(0, 8, pack_base, (zero8, zero8))
    pl.semaphore_wait(barrier, len(along) + len(across))
    finish = exchange(0, accs, base)
    loads[3].wait()

    def pack_fwd(x, accs):
        for c in range(3):
            accs = pack(accs, fwd[c, x + 1, own_rows, :], c, x, 0, highs=False)
        return accs

    fwd_z[0] = lax.fori_loop(0, 8, pack_fwd, (zero8, zero8))[0]
    fwd_parts = [
        (fwd.at[:, 1, own_rows], fwd.at[:, 9, own_rows], down[0]),
        (fwd.at[:, pl.ds(1, 8), pl.ds(TOP, 1)], fwd.at[:, pl.ds(1, 8), pl.ds(TOP + 32, 1)], down[1]),
        (fwd_z.at[0], fwd_z.at[1], down[2]),
    ]
    fwd_copies = [
        remote(src, dst, fsend.at[i], frecv.at[i], target)
        for i, (src, dst, target) in enumerate(fwd_parts)
    ]
    for copy in fwd_copies:
        copy.start()

    grid_row, grid_lane = rows_of((128, 128)), lanes_of((128, 128))
    pair = (grid_row // 2 == grid_lane).astype(F32)
    pick = [(grid_row == 2 * grid_lane + s).astype(F32) for s in range(2)]
    spread = (grid_row == grid_lane // 2).astype(F32)

    def times(a, b):
        return jnp.dot(a, b, precision=HI, preferred_element_type=F32)

    def edge(x, side, nx):
        at_edge = (rad == 0) & (x == 0) if side == 0 else (rad == 3) & (x == nx - 1)
        return jnp.where(at_edge, 0.0, 1.0).astype(F32)

    def edge_rows(side, ny):
        row = rows_of((ny, 128))
        at_edge = (lat == 0) & (row == 0) if side == 0 else (lat == 7) & (row == ny - 1)
        return jnp.where(at_edge, 0.0, 1.0).astype(F32)

    def finish_level(level, x, six):
        nx, ny, width = LEVELS[level]
        at = block(x, ny)
        for k in range(6):
            if k < 2:
                link = six[k] * edge(x, k, nx)
            elif k < 4:
                link = six[k] * edge_rows(k - 2, ny)
            else:
                link = six[k]
            links[level][k, at, :] = link
        total = six[0] + six[1] + six[2] + six[3] + six[4] + six[5]
        diags[level][at, :] = total
        lane = lanes_of((ny, 128))
        invs[level][at, :] = jnp.where(lane < width, 1.0 / jnp.where(lane < width, total, 1.0), 0.0)

    loads[2].wait()
    halo = finish()

    def setup_plane(x, accs):
        v = base[0, x + 1, own_rows, :]
        low_z, high_z = shifted(0, v, halo, 0, x)
        six = [
            0.5 * (v + edge(x, 0, 8) * base[0, x, own_rows, :]),
            0.5 * (v + edge(x, 1, 8) * base[0, x + 2, own_rows, :]),
            0.5 * (v + edge_rows(0, 32) * base[0, x + 1, pl.ds(TOP - 1, 32), :]),
            0.5 * (v + edge_rows(1, 32) * base[0, x + 1, pl.ds(TOP + 1, 32), :]),
            0.5 * (v + low_z),
            0.5 * (v + high_z),
        ]
        at = block(x, 32)
        for k in range(6):
            faces0[k, at, :] = six[k]
        finish_level(0, x, six)
        p = base[1, x + 1, own_rows, :]
        _, high_p = shifted(0, p, halo, 1, x)
        grads = [
            base[1, x + 2, own_rows, :] * edge(x, 1, 8) - p,
            base[1, x + 1, pl.ds(TOP + 1, 32), :] * edge_rows(1, 32) - p,
            high_p - p,
        ]
        for c in range(3):
            right = load[c, x] - grads[c]
            res0[c, at, :] = right
            update = inv0[at, :] * right * FIRST
            sol0[c, at, :] = update
            buf0[1, c, x + 1, own_rows, :] = update
            accs = pack(accs, update, c, x, 0)
        return accs

    start = lax.fori_loop(0, 8, setup_plane, (zero8, zero8))

    def coarsen(level):
        nx, ny, _ = LEVELS[level]
        half_x, half_y = nx // 2, ny // 2
        n = half_x * half_y
        fine = faces[level]
        for k in range(6):
            way, side = k // 2, k % 2

            def one(x, carry):
                if way == 0:
                    plane = fine[k, block(2 * x + side, ny), :]
                else:
                    plane = fine[k, block(2 * x, ny), :] + fine[k, block(2 * x + 1, ny), :]
                tmp[0, pl.ds(0, ny), :] = plane
                even = tmp[0, pl.ds(0, half_y, 2), :]
                odd = tmp[0, pl.ds(1, half_y, 2), :]
                both = (even, odd)[side] if way == 1 else even + odd
                flat[k, block(x, half_y), :] = both
                return carry

            lax.fori_loop(0, half_x, one, 0)
            along_z = pick[side] if way == 2 else pair
            faces[level + 1][k] = times(flat[k, :n, :], along_z)

        def store(x, carry):
            at = block(x, half_y)
            finish_level(level + 1, x, [faces[level + 1][k, at, :] for k in range(6)])
            return carry

        lax.fori_loop(0, half_x, store, 0)

    def sweep(level, p, halo, step, initial=False, emit=None, last=False):
        nx, ny, _ = LEVELS[level]
        buf, link, res, sol = bufs[level], links[level], ress[level], sols[level]

        def plane(x, accs):
            at = block(x, ny)
            diag, inv = diags[level][at, :], invs[level][at, :]
            ls = [link[k, at, :] for k in range(6)]
            for c in range(3):
                v = buf[p, c, x + 1, pl.ds(TOP, ny), :]
                low_z, high_z = shifted(level, v, halo, c, x)
                total = diag * v - ls[0] * buf[p, c, x, pl.ds(TOP, ny), :]
                total = total - ls[1] * buf[p, c, x + 2, pl.ds(TOP, ny), :]
                total = total - ls[2] * buf[p, c, x + 1, pl.ds(TOP - 1, ny), :]
                total = total - ls[3] * buf[p, c, x + 1, pl.ds(TOP + 1, ny), :]
                total = total - ls[4] * low_z - ls[5] * high_z
                r = res[c, at, :] - total
                if step is None:
                    res[c, at, :] = r
                    continue
                if initial:
                    update = FIRST * inv * r
                    after = sol[c, at, :] + v + update
                else:
                    update = step[0] * v + step[1] * inv * r
                    after = sol[c, at, :] + update
                sol[c, at, :] = after
                if last:
                    accs = emit(accs, after, c, x, at)
                else:
                    res[c, at, :] = r
                    buf[1 - p, c, x + 1, pl.ds(TOP, ny), :] = update
                    accs = pack(accs, update, c, x, level)
            return accs

        init = (zero8, zero8) if emit is None or not last else (zero8, zero8, zero8)
        return lax.fori_loop(0, nx, plane, init)

    def smooth_down(level, accs, between=None):
        for step in (STEPS[0], STEPS[1], None):
            p = parity()
            finish = exchange(level, accs)
            if between is not None:
                between()
                between = None
            accs = sweep(level, p, finish(), step)

    def restrict(level):
        nx, ny, _ = LEVELS[level]
        half_x, half_y = nx // 2, ny // 2
        n = half_x * half_y
        res = ress[level]
        for c in range(3):
            def one(x, carry):
                plane = res[c, block(2 * x, ny), :] + res[c, block(2 * x + 1, ny), :]
                tmp[0, pl.ds(0, ny), :] = plane
                even = tmp[0, pl.ds(0, half_y, 2), :]
                flat[c, block(x, half_y), :] = even + tmp[0, pl.ds(1, half_y, 2), :]
                return carry

            lax.fori_loop(0, half_x, one, 0)
            ress[level + 1][c] = times(flat[c, :n, :], pair)
        p = parity()

        def first(x, accs):
            at = block(x, half_y)
            for c in range(3):
                update = FIRST * invs[level + 1][at, :] * ress[level + 1][c, at, :]
                sols[level + 1][c, at, :] = update
                bufs[level + 1][p, c, x + 1, pl.ds(TOP, half_y), :] = update
                accs = pack(accs, update, c, x, level + 1)
            return accs

        return lax.fori_loop(0, half_x, first, (zero8, zero8))

    def prolong(level):
        nx, ny, _ = LEVELS[level]
        half_x, half_y = nx // 2, ny // 2
        p = parity()
        buf = bufs[level]
        for c in range(3):
            flat[c, : half_x * half_y, :] = times(sols[level + 1][c], spread)

        def one(x, accs):
            for c in range(3):
                coarse = flat[c, block(x, half_y), :]
                tmp[0, pl.ds(0, half_y, 2), :] = coarse
                tmp[0, pl.ds(1, half_y, 2), :] = coarse
                fine = tmp[0, pl.ds(0, ny), :]
                for s in range(2):
                    buf[p, c, 2 * x + 1 + s, pl.ds(TOP, ny), :] = fine
                    accs = pack(accs, fine, c, 2 * x + s, level)
            return accs

        return lax.fori_loop(0, half_x, one, (zero8, zero8))

    def gather(use):
        first = [
            remote(tile.at[use, 0], got1.at[use, lon], send1.at[use, i], recv1.at[use, i], target)
            for i, target in enumerate(along)
        ]
        second = [
            remote(tile.at[use, 1], got2.at[use, rad, block(lat, 8)], send2.at[use, i], recv2.at[use, i], target)
            for i, target in enumerate(across)
        ]

        def begin(value):
            tile[use, 0] = value
            got1[use, lon] = value
            for copy in first:
                copy.start()

        def middle():
            for copy in first:
                copy.wait()
            total = got1[use, 0]
            for k in range(1, 8):
                total = total + got1[use, k]
            tile[use, 1] = total
            got2[use, rad, block(lat, 8), :] = total
            for copy in second:
                copy.start()

        def end():
            for copy in second:
                copy.wait()

        return begin, middle, end

    runs = jnp.bitwise_and(owner[0:1, :], 31)
    lane1 = lanes_of((1, 128))
    place = jnp.where(lane1 < 32, runs + 32 * rad, -1)
    member = (grid_row == jnp.broadcast_to(place, (128, 128))).astype(F32)

    def to_runs(rows):
        return lax.dot_general(
            rows, member, (((1,), (1,)), ((), ())), precision=HI, preferred_element_type=F32
        )

    def stacked(rows):
        out = zero8
        row8 = rows_of((8, 128))
        for i, row in enumerate(rows):
            out = jnp.where(row8 == i, jnp.broadcast_to(row, (8, 128)), out)
        return out

    def rowsum(plane):
        return jnp.sum(plane, axis=0, keepdims=True)

    def coarse_solve():
        begin, middle, end = gather(0)
        f = faces2
        here = jnp.where(lane1 < 32, runs, -1)
        first_cell = (lane1 == 0) | (here != pltpu.roll(jnp.broadcast_to(here, (8, 128)), 1, 1)[0:1])
        last_cell = (lane1 == 31) | (here != pltpu.roll(jnp.broadcast_to(here, (8, 128)), 127, 1)[0:1])
        sides = [
            rowsum(f[0, 0:8, :]),
            rowsum(f[1, 8:16, :]),
            f[2, 0:1, :] + f[2, 8:9, :],
            f[3, 7:8, :] + f[3, 15:16, :],
            jnp.where(first_cell, rowsum(f[4, 0:8, :] + f[4, 8:16, :]), 0.0),
            jnp.where(last_cell, rowsum(f[5, 0:8, :] + f[5, 8:16, :]), 0.0),
        ]
        whole = sides[0] + sides[1] + sides[2] + sides[3] + sides[4] + sides[5]
        rights = [rowsum(res2[c, 0:8, :] + res2[c, 8:16, :]) for c in range(3)]
        begin(to_runs(stacked(rights + [sides[0], sides[2], sides[4], whole])))
        middle()
        end()

        def all_of(i):
            out = got2[0, 0, pl.ds(i, 8, 8), :]
            for k in range(1, 4):
                out = out + got2[0, k, pl.ds(i, 8, 8), :]
            return out

        row8 = rows_of((8, 128))
        wrap = jnp.bitwise_and(lane8, 31)

        def lower_z(v):
            return jnp.where(wrap == 0, pltpu.roll(v, 97, 1), pltpu.roll(v, 1, 1))

        def upper_z(v):
            return jnp.where(wrap == 31, pltpu.roll(v, 31, 1), pltpu.roll(v, 127, 1))

        link_x = jnp.where(lane8 < 32, 0.0, all_of(3))
        link_y = jnp.where(row8 == 0, 0.0, all_of(4))
        link_z = all_of(5)
        link_xu, link_yu, link_zu = pltpu.roll(link_x, 96, 1), pltpu.roll(link_y, 7, 0), upper_z(link_z)
        diagonal = all_of(6)
        inverse = 1.0 / diagonal

        def operate(v):
            out = diagonal * v - link_x * pltpu.roll(v, 32, 1) - link_xu * pltpu.roll(v, 96, 1)
            out = out - link_y * pltpu.roll(v, 1, 0) - link_yu * pltpu.roll(v, 7, 0)
            return out - link_z * lower_z(v) - link_zu * upper_z(v)

        rs = [all_of(c) for c in range(3)]
        ds = [inverse * r * COARSE_FIRST for r in rs]
        es = list(ds)
        for a, b in COARSE_STEPS:
            rs = [r - operate(d) for r, d in zip(rs, ds)]
            ds = [a * d + b * inverse * r for r, d in zip(rs, ds)]
            es = [e + d for e, d in zip(es, ds)]
        for c in range(3):
            erows[c] = es[c]
            erows[3 + c] = lower_z(es[c])
            erows[6 + c] = upper_z(es[c])

        def row_of(i, at):
            return erows[i, pl.ds(at, 1), :]

        below, above = lax.rem(lat + 7, 8), lax.rem(lat + 1, 8)
        kinds = []
        for c in range(3):
            mid = row_of(c, lat)
            wide = jnp.broadcast_to(mid, (8, 128))
            kinds.append(to_columns(stacked([
                mid, row_of(3 + c, lat), row_of(6 + c, lat), row_of(c, below), row_of(c, above),
                pltpu.roll(wide, 32, 1)[0:1], pltpu.roll(wide, 96, 1)[0:1],
            ])))
        p = parity()
        rims = []
        for c in range(3):
            k = kinds[c]
            own = jnp.broadcast_to(k[0:1], (8, 128))
            for x in range(2):
                buf2[p, c, 1 + x, pl.ds(TOP, 8), :] = own
                buf2[p, c, 1 + x, pl.ds(TOP - 1, 1), :] = k[3:4]
                buf2[p, c, 1 + x, pl.ds(TOP + 8, 1), :] = k[4:5]
            buf2[p, c, 0, pl.ds(TOP, 8), :] = jnp.broadcast_to(k[5:6], (8, 128))
            buf2[p, c, 3, pl.ds(TOP, 8), :] = jnp.broadcast_to(k[6:7], (8, 128))
            left = pltpu.roll(jnp.broadcast_to(k[1:2], (8, 128)), 127, 1)
            right = pltpu.roll(jnp.broadcast_to(k[2:3], (8, 128)), 1, 1)
            rims.append(jnp.where(lane1 == 127, left[0:1], right[0:1]))
        return p, jnp.concatenate(rims, 0)

    def to_columns(rows):
        return times(rows, member)

    def smooth_up(level, accs, emit=None):
        for i, step in enumerate(STEPS):
            p = parity()
            last = i == len(STEPS) - 1
            halo = exchange(level, accs)()
            accs = sweep(level, p, halo, step, emit=emit, last=last)
        return accs

    def nothing(accs, after, c, x, at):
        return accs

    def coarsen_all():
        coarsen(0)
        coarsen(1)

    smooth_down(0, start, coarsen_all)
    smooth_down(1, restrict(0))
    smooth_down(2, restrict(1))
    p, rim = coarse_solve()
    turn[0] += 1
    accs = sweep(2, p, rim, True, initial=True)
    smooth_up(2, accs, nothing)
    for level in (1, 0):
        accs = prolong(level)
        p = parity()
        halo = exchange(level, accs)()
        accs = sweep(level, p, halo, True, initial=True)
        if level == 1:
            smooth_up(1, accs, nothing)
    final = parity()

    def emit(accs, after, c, x, at):
        adjoint[c, x] = after
        buf0[final, c, x + 1, own_rows, :] = after
        low, high, total = accs
        low, high = pack((low, high), after, c, x, 0)
        v = base[0, x + 1, own_rows, :]
        part = 2.0 * (faces0[2 * c + 1, at, :] - v) * after
        if c == 0:
            part = part + base[1, x + 1, own_rows, :]
        total = total + (part[0:8] + part[8:16] + part[16:24] + part[24:32])
        return low, high, total

    low, high, partial = smooth_up(0, accs, emit)

    begin, middle, end = gather(1)
    finish = exchange(0, (low, high))
    begin(partial)
    for copy in fwd_copies:
        copy.wait()
    middle()
    halo = finish()
    fwd_halo = fwd_z[1]
    lane32 = lanes_of((32, 128))

    def outputs(x, carry):
        at = block(x, 32)
        v = base[0, x + 1, own_rows, :]
        keep_x, keep_y = edge(x, 1, 8), edge_rows(1, 32)
        ga, gf = [], []
        us = []
        for c in range(3):
            u = buf0[final, c, x + 1, own_rows, :]
            low_z, high_z = shifted(0, u, halo, c, x)
            ga.append([
                buf0[final, c, x + 2, own_rows, :] * keep_x - u,
                buf0[final, c, x + 1, pl.ds(TOP + 1, 32), :] * keep_y - u,
                high_z - u,
            ])
            us.append((u, low_z))
            w = fwd[c, x + 1, own_rows, :]
            q = (c * 8 + x) * 4
            right = [pltpu.roll(fwd_halo, lax.rem(255 - q - g, 128), 1) for g in range(4)]
            high_w = jnp.where(lane32 == 127, jnp.concatenate(right, 0), pltpu.roll(w, 127, 1))
            gf.append([
                fwd[c, x + 2, own_rows, :] * keep_x - w,
                fwd[c, x + 1, pl.ds(TOP + 1, 32), :] * keep_y - w,
                high_w - w,
            ])
        divergence = (
            us[0][0] - edge(x, 0, 8) * buf0[final, 0, x, own_rows, :]
            + (us[1][0] - edge_rows(0, 32) * buf0[final, 1, x + 1, pl.ds(TOP - 1, 32), :])
            + (us[2][0] - us[2][1])
        )
        pnext[x] = base[1, x + 1, own_rows, :] - v * divergence
        summed = gf[0][0] * ga[0][0] + gf[1][1] * ga[1][1] + gf[2][2] * ga[2][2]
        for d, e in ((0, 1), (0, 2), (1, 2)):
            summed = summed + 0.5 * (gf[e][d] + gf[d][e]) * (ga[e][d] + ga[d][e])
        gradient[x] = 2.0 * v * summed
        return carry

    lax.fori_loop(0, 8, outputs, 0)
    end()
    total = zero8
    for a in range(4):
        for b in range(8):
            total = total + got2[1, a, 8 * b : 8 * b + 8, :]
    mean = jnp.sum(total) / CELLS

    def shift(x, carry):
        pnext[x] = pnext[x] - mean
        return carry

    lax.fori_loop(0, 8, shift, 0)


def per_device(forcing, pressure, viscosity, forward, owner):
    vmem, anywhere = pl.BlockSpec(memory_space=pltpu.VMEM), pl.BlockSpec(memory_space=pl.ANY)
    first_row = jnp.pad(owner[0, 0:1, :], ((0, 0), (0, 96)))
    f32 = lambda *shape: pltpu.VMEM(shape, F32)
    padded = [f32(2, 3, nx + 2, ny + 16, 128) for nx, ny, _ in LEVELS]
    six = [f32(6, nx * ny, 128) for nx, ny, _ in LEVELS]
    one = [f32(nx * ny, 128) for nx, ny, _ in LEVELS]
    three = [f32(3, nx * ny, 128) for nx, ny, _ in LEVELS]
    dma = lambda *shape: pltpu.SemaphoreType.DMA(shape)
    return pl.pallas_call(
        kernel,
        out_shape=(
            jax.ShapeDtypeStruct((3, 8, 32, 128), F32),
            jax.ShapeDtypeStruct((8, 32, 128), F32),
            jax.ShapeDtypeStruct((8, 32, 128), F32),
        ),
        in_specs=[anywhere] * 4 + [vmem],
        out_specs=(vmem, vmem, vmem),
        scratch_shapes=[
            f32(3, 8, 32, 128), f32(2, 10, 48, 128), f32(3, 10, 48, 128), f32(1, 8, 128), f32(2, 8, 128),
            *padded, f32(2, 4, 8, 128), *six, *six, *one, *one, *three, *three,
            f32(1, 32, 128), f32(6, 64, 128), f32(9, 8, 128), f32(2, 2, 8, 128),
            f32(2, 8, 8, 128), f32(2, 4, 64, 128),
            dma(4), dma(2, 6), dma(2, 6), dma(3), dma(3), dma(2, 7), dma(2, 7), dma(2, 31), dma(2, 31),
        ],
        compiler_params=pltpu.CompilerParams(
            collective_id=0, has_side_effects=True, vmem_limit_bytes=40 * 1024 * 1024
        ),
    )(forcing, pressure, viscosity, forward, first_row)


def solution(mesh):
    placed = (
        P(None, "rad", "lat", "lon"),
        P("rad", "lat", "lon"),
        P("rad", "lat", "lon"),
        P(None, "rad", "lat", "lon"),
        P("rad", "lat", "lon"),
    )
    return jax.shard_map(
        per_device,
        mesh=mesh,
        in_specs=placed,
        out_specs=(P(None, "rad", "lat", "lon"), P("rad", "lat", "lon"), P("rad", "lat", "lon")),
        check_vma=False,
    )
```

```python
import jax
import jax.numpy as jnp
from jax import lax
from jax.experimental import pallas as pl
from jax.experimental.pallas import tpu as pltpu
from jax.sharding import PartitionSpec as P

AXES = ("rad", "lat", "lon")
SIZES = (4, 8, 8)
MESH = pl.DeviceIdType.MESH
F32 = jnp.float32
HI = lax.Precision.HIGHEST
CDEG = 8
CELLS = 32 * 256 * 1024
LEVELS = ((8, 32, 128), (4, 16, 64), (2, 8, 32))
TOP = 8
DEEP_ROWS = {1: 48, 2: 40}
OWN1, OWN2 = pl.ds(16, 16), pl.ds(16, 8)


def cheb_constants(low, high, degree):
    middle, spread = 0.5 * (high + low), 0.5 * (high - low)
    factor = middle / spread
    old = 1.0 / factor
    steps = []
    for _ in range(degree - 1):
        new = 1.0 / (2.0 * factor - old)
        steps.append((new * old, 2.0 * new / spread))
        old = new
    return 1.0 / middle, steps


FIRST, STEPS = cheb_constants(0.5, 2.0, 3)
COARSE_FIRST, COARSE_STEPS = cheb_constants(0.1, 2.0, CDEG)


def lanes_of(shape):
    return lax.broadcasted_iota(jnp.int32, shape, len(shape) - 1)


def rows_of(shape):
    return lax.broadcasted_iota(jnp.int32, shape, len(shape) - 2)


def block(x, rows):
    return pl.ds(pl.multiple_of(x * rows, 8), rows)


def kernel(
    forcing, pressure, viscosity, forward, owner,
    adjoint, pnext, gradient,
    load, base, fwd, base_z, fwd_z,
    buf0, zbuf, faces0, faces1, faces2, links0, diag0, inv0, res0, sol0, rim0, hbuf, hz, applied,
    coef1, coef2, inv1, inv2, right1, left1, right2, deep1, deep2, sol1, sol2,
    zsend1, zgot1, dense2, dgot2,
    tmp, flat, erows, tile, got1, got2, got3,
    in_sem, send_sem, recv_sem, fsend, frecv, send1, recv1, send2, recv2, send3, recv3,
    dsend1, drecv1, dsend2, drecv2, hsend, hrecv,
):
    me = tuple(lax.axis_index(a) for a in AXES)
    rad, lat, lon = me

    def device(*steps):
        return tuple(
            lax.rem(m + (s % n), n) if s % n else m for m, s, n in zip(me, steps, SIZES)
        )

    up = [device(1, 0, 0), device(0, 1, 0), device(0, 0, 1)]
    down = [device(-1, 0, 0), device(0, -1, 0), device(0, 0, -1)]
    along = [device(0, 0, k) for k in range(1, 8)]
    across = [device(0, k, 0) for k in range(1, 8)]
    through = [device(k, 0, 0) for k in range(1, 4)]
    near1 = [
        (a, b, c) for a in (0, 1, -1) for b in (0, 1, -1) for c in (0, 1, -1) if a or b or c
    ]
    near2 = [
        (a, b, c) for a in range(4) for b in (0, 1, -1) for c in (0, 1, -1) if a or b or c
    ]
    peers = [device(*o) for o in near2] + along[1:6] + across[1:6]

    own_rows = pl.ds(TOP, 32)
    loads = [
        pltpu.make_async_copy(viscosity, base.at[0, pl.ds(1, 8), own_rows], in_sem.at[0]),
        pltpu.make_async_copy(pressure, base.at[1, pl.ds(1, 8), own_rows], in_sem.at[1]),
        pltpu.make_async_copy(forcing, load, in_sem.at[2]),
        pltpu.make_async_copy(forward, fwd.at[:, pl.ds(1, 8), own_rows], in_sem.at[3]),
    ]
    for copy in loads:
        copy.start()

    def clear(ref, *at):
        ref[at] = jnp.zeros(ref[at].shape, F32)

    every, low_rows, high_rows = slice(None), slice(8, 16), slice(32, 40)
    for plane in (0, 9):
        clear(buf0, every, every, plane, slice(8, 40))
        clear(base, every, plane, slice(8, 40))
        clear(fwd, every, plane, slice(8, 40))
        clear(hbuf, every, plane, slice(8, 40))
    clear(coef1, every, slice(0, 12), low_rows)
    clear(coef1, every, slice(0, 12), slice(32, 48))
    for planes in (slice(0, 4), slice(8, 12)):
        clear(coef1, every, planes, slice(16, 32))
        clear(right1, every, planes, slice(16, 32))
        clear(left1, every, planes, slice(16, 32))
    for ref in (right1, left1):
        clear(ref, every, every, low_rows)
        clear(ref, every, every, high_rows)
    clear(deep1, every, every, every, slice(0, 8))
    clear(deep1, every, every, every, slice(40, 48))
    clear(deep2, every, every, every, slice(0, 8))
    clear(deep2, every, every, every, slice(32, 40))
    for plane in (1, 10):
        clear(coef2, every, plane)
        clear(deep2, every, every, plane)
    clear(coef2, every, every, slice(32, 40))
    for plane in (0, 1, 10, 11):
        clear(sol2, every, plane, slice(8, 32))
    for side in (0, 2):
        clear(zgot1, every, side)

    barrier = pltpu.get_barrier_semaphore()
    for target in peers:
        pl.semaphore_signal(barrier, inc=1, device_id=target, device_id_type=MESH)

    def remote(src, dst, ssem, rsem, target):
        return pltpu.make_async_remote_copy(
            src_ref=src, dst_ref=dst, send_sem=ssem, recv_sem=rsem,
            device_id=target, device_id_type=MESH,
        )

    lane8 = lanes_of((8, 128))

    zero8 = jnp.zeros((8, 128), F32)

    def pack(accs, planes, x, lows=True, highs=True):
        parts = [p[8 * g : 8 * g + 8] for p in planes for g in range(4)]
        n = len(parts)
        low = high = zero8
        for j, part in enumerate(parts):
            turned = pltpu.roll(part, j, 1) if j else part
            if lows:
                low = jnp.where(lane8 == j, turned, low)
            if highs:
                high = jnp.where(lane8 == (127 + j) % 128, turned, high)
        return (
            accs[0] + pltpu.roll(low, n * x, 1) if lows else accs[0],
            accs[1] + pltpu.roll(high, n * x, 1) if highs else accs[1],
        )

    def merged(before, after):
        before, after = pltpu.roll(before, 1, 1), pltpu.roll(after, 127, 1)
        even = jnp.bitwise_and(lane8, 1) == 0
        return jnp.where(even, before, after), jnp.where(even, after, before)

    def rims_of(halo, n, x):
        turn_back = lax.rem(128 - n * x, 128)
        halo = [pltpu.roll(h, turn_back, 1) for h in halo]
        return [pltpu.roll(halo[j % 2], 128 - j, 1) if j else halo[0] for j in range(n)]

    lane32, lane16 = lanes_of((32, 128)), lanes_of((16, 128))

    def shifted(v, rims):
        rim = jnp.concatenate(rims, 0) if isinstance(rims, list) else rims
        low = jnp.where(lane32 == 0, rim, pltpu.roll(v, 1, 1))
        high = jnp.where(lane32 == 127, rim, pltpu.roll(v, 127, 1))
        return low, high

    def guarded(copy, step):
        sends_it, gets_it = (rad < 3, rad > 0) if step == 1 else (rad > 0, rad < 3)

        def start():
            pl.when(sends_it)(copy.start)

        def wait():
            pl.when(sends_it)(copy.wait_send)
            pl.when(gets_it)(copy.wait_recv)

        return start, wait

    def plain(copy):
        return copy.start, copy.wait

    def sends(buf, zref, ssem, rsem):
        rows, planes = pl.ds(TOP, 32), pl.ds(1, 8)
        parts = [
            (buf.at[:, 8, rows], buf.at[:, 0, rows], up[0]),
            (buf.at[:, 1, rows], buf.at[:, 9, rows], down[0]),
            (buf.at[:, planes, pl.ds(TOP + 31, 1)], buf.at[:, planes, pl.ds(TOP - 1, 1)], up[1]),
            (buf.at[:, planes, pl.ds(TOP, 1)], buf.at[:, planes, pl.ds(TOP + 32, 1)], down[1]),
            (zref.at[1], zref.at[2], up[2]),
            (zref.at[0], zref.at[3], down[2]),
        ]
        copies = [
            remote(src, dst, ssem.at[i], rsem.at[i], target)
            for i, (src, dst, target) in enumerate(parts)
        ]
        return [guarded(copies[0], 1), guarded(copies[1], -1)] + [plain(copy) for copy in copies[2:]]

    turn = [0]

    def send_all(accs, buf, zref, ssem, rsem):
        zref[0], zref[1] = accs
        copies = sends(buf, zref, ssem, rsem)
        for start, _ in copies:
            start()

        def finish():
            for _, wait in copies:
                wait()
            return merged(zref[2], zref[3])

        return finish

    def exchange(accs, buf=None):
        p = turn[0] % 2
        turn[0] += 1
        return send_all(accs, buf0.at[p] if buf is None else buf, zbuf.at[p], send_sem.at[p], recv_sem.at[p])

    for copy in loads[:2]:
        copy.wait()

    def pack_base(x, accs):
        return pack(accs, [base[c, x + 1, own_rows, :] for c in range(2)], x)

    accs = lax.fori_loop(0, 8, pack_base, (zero8, zero8), unroll=2)
    pl.semaphore_wait(barrier, len(peers))
    finish = exchange(accs, base)
    loads[3].wait()

    def pack_fwd(x, accs):
        return pack(accs, [fwd[c, x + 1, own_rows, :] for c in range(3)], x, highs=False)

    fwd_z[0] = lax.fori_loop(0, 8, pack_fwd, (zero8, zero8), unroll=2)[0]
    fwd_parts = [
        (fwd.at[:, 1, own_rows], fwd.at[:, 9, own_rows], down[0]),
        (fwd.at[:, pl.ds(1, 8), pl.ds(TOP, 1)], fwd.at[:, pl.ds(1, 8), pl.ds(TOP + 32, 1)], down[1]),
        (fwd_z.at[0], fwd_z.at[1], down[2]),
    ]
    fwd_copies = [
        remote(src, dst, fsend.at[i], frecv.at[i], target)
        for i, (src, dst, target) in enumerate(fwd_parts)
    ]
    fwd_copies = [guarded(fwd_copies[0], -1)] + [plain(copy) for copy in fwd_copies[1:]]
    for begin, _ in fwd_copies:
        begin()

    grid_row, grid_lane = rows_of((128, 128)), lanes_of((128, 128))
    pair = (grid_row // 2 == grid_lane).astype(F32)
    own_pair = jnp.where(grid_row < 64, pair, 0.0)
    pick = [(grid_row == 2 * grid_lane + s).astype(F32) for s in range(2)]
    spread0 = (grid_row == grid_lane // 2).astype(F32)
    spread1 = (grid_row == jnp.where(grid_lane < 96, 0, 64) + grid_lane // 2).astype(F32)

    def times(a, b):
        return jnp.dot(a, b, precision=HI, preferred_element_type=F32)

    def edge(x, side, nx):
        at_edge = (rad == 0) & (x == 0) if side == 0 else (rad == 3) & (x == nx - 1)
        return jnp.where(at_edge, 0.0, 1.0).astype(F32)

    def edge_rows(side, ny):
        row = rows_of((ny, 128))
        at_edge = (lat == 0) & (row == 0) if side == 0 else (lat == 7) & (row == ny - 1)
        return jnp.where(at_edge, 0.0, 1.0).astype(F32)

    loads[2].wait()
    halo = finish()

    def setup_plane(x, accs):
        v = base[0, x + 1, own_rows, :]
        rims = rims_of(halo, 8, x)
        low_z, high_z = shifted(v, rims[:4])
        lower_x, upper_x, lower_y, upper_y = edge(x, 0, 8), edge(x, 1, 8), edge_rows(0, 32), edge_rows(1, 32)
        six = [
            0.5 * (v + lower_x * base[0, x, own_rows, :]),
            0.5 * (v + upper_x * base[0, x + 2, own_rows, :]),
            0.5 * (v + lower_y * base[0, x + 1, pl.ds(TOP - 1, 32), :]),
            0.5 * (v + upper_y * base[0, x + 1, pl.ds(TOP + 1, 32), :]),
            0.5 * (v + low_z),
            0.5 * (v + high_z),
        ]
        at = block(x, 32)
        for k in range(6):
            faces0[k, at, :] = six[k]
        masks = (lower_x, upper_x, lower_y, upper_y)
        for k in range(6):
            links0[k, at, :] = six[k] * masks[k] if k < 4 else six[k]
        diag = six[0] + six[1] + six[2] + six[3] + six[4] + six[5]
        inv = 1.0 / diag
        diag0[at, :] = diag
        inv0[at, :] = inv
        p = base[1, x + 1, own_rows, :]
        _, high_p = shifted(p, rims[4:])
        grads = [
            base[1, x + 2, own_rows, :] * upper_x - p,
            base[1, x + 1, pl.ds(TOP + 1, 32), :] * upper_y - p,
            high_p - p,
        ]
        updates = []
        for c in range(3):
            right = load[c, x] - grads[c]
            res0[c, at, :] = right
            update = inv * right * FIRST
            sol0[c, at, :] = update
            buf0[1, c, x + 1, own_rows, :] = update
            updates.append(update)
        return pack(accs, updates, x)

    start = lax.fori_loop(0, 8, setup_plane, (zero8, zero8))

    def coarsen(level, fine, coarse):
        nx, ny, _ = LEVELS[level]
        half_x, half_y = nx // 2, ny // 2
        n = half_x * half_y

        def one(x, carry):
            for k in range(6):
                way, side = k // 2, k % 2
                if way == 0:
                    plane = fine[k, block(2 * x + side, ny), :]
                else:
                    plane = fine[k, block(2 * x, ny), :] + fine[k, block(2 * x + 1, ny), :]
                tmp[k, pl.ds(0, ny), :] = plane
            for k in range(6):
                way, side = k // 2, k % 2
                if way == 1:
                    both = tmp[k, pl.ds(side, half_y, 2), :]
                else:
                    both = tmp[k, pl.ds(0, half_y, 2), :] + tmp[k, pl.ds(1, half_y, 2), :]
                flat[k, block(x, half_y), :] = both
            return carry

        lax.fori_loop(0, half_x, one, 0)
        sums = times(flat[0:4, :n, :].reshape(4 * n, 128), pair).reshape(4, n, 128)
        for k in range(4):
            coarse[k] = sums[k]
        for k in range(4, 6):
            coarse[k] = times(flat[k, :n, :], pick[k - 4])

    def coefficients(level, faces, x):
        nx, ny, _ = LEVELS[level]
        six = [faces[k, pl.ds(x * ny, ny), :] for k in range(6)]
        total = six[0] + six[1] + six[2] + six[3] + six[4] + six[5]
        return [total, six[0] * edge(x, 0, nx), six[2] * edge_rows(0, ny), six[4]]

    def invert(coef, inv, planes):
        def one(x, carry):
            d = coef[0, x]
            inv[x] = jnp.where(d > 0.0, 1.0 / jnp.where(d > 0.0, d, 1.0), 0.0)
            return carry

        lax.fori_loop(0, planes, one, 0)

    side_lanes = (lane8 < 68) | (lane8 >= 124)

    def exchange1(use, ref, depth_up, depth_down):
        n = ref.shape[0]
        zlow = zhigh = zero8
        for x in range(4):
            for a in range(n):
                for g in range(2):
                    at = 4 * ((x * n + a) * 2 + g)
                    part = ref[a, 4 + x, pl.ds(16 + 8 * g, 8), :]
                    turned = pltpu.roll(part, at, 1) if at else part
                    zlow = jnp.where((lane8 >= at) & (lane8 < at + 4), turned, zlow)
                    top = (60 + at) % 128
                    zhigh = jnp.where((lane8 >= top) & (lane8 < top + 4), turned, zhigh)
        zsend1[use, 0] = zlow
        zsend1[use, 1] = zhigh
        copies = []
        for i, (a, b, c) in enumerate(near1):
            if c:
                src = zsend1.at[use, (c + 1) // 2]
                dst = zgot1.at[use, 1 - a, 1 - b, (1 - c) // 2]
            else:
                from_x, to_x, from_y, to_y = pl.ds(4, 4), pl.ds(4, 4), OWN1, OWN1
                if a == 1:
                    from_x, to_x = pl.ds(8 - depth_up, depth_up), pl.ds(4 - depth_up, depth_up)
                if a == -1:
                    from_x, to_x = pl.ds(4, depth_down), pl.ds(8, depth_down)
                if b == 1:
                    from_y, to_y = pl.ds(28, 4), pl.ds(12, 4)
                if b == -1:
                    from_y, to_y = pl.ds(16, 4), pl.ds(32, 4)
                src, dst = ref.at[:, from_x, from_y], ref.at[:, to_x, to_y]
            copy = remote(src, dst, dsend1.at[use, i], drecv1.at[use, i], device(a, b, c))
            copies.append((a, copy))

        def each(way, do):
            group = [copy for a, copy in copies if a == way]
            for copy in group:
                do(copy)

        for way, there in ((1, rad < 3), (-1, rad > 0)):
            pl.when(there)(lambda way=way: each(way, lambda copy: copy.start()))
        each(0, lambda copy: copy.start())

        def finish(low_plane, high_plane):
            for way, sends_it, gets_it in ((1, rad < 3, rad > 0), (-1, rad > 0, rad < 3)):
                pl.when(sends_it)(lambda way=way: each(way, lambda copy: copy.wait_send()))
                pl.when(gets_it)(lambda way=way: each(way, lambda copy: copy.wait_recv()))
            each(0, lambda copy: copy.wait())

            def one(plane, carry):
                dx, x = lax.div(plane, 4), lax.rem(plane, 4)
                back = lax.rem(192 - 8 * n * x, 128)
                for dy, groups in ((0, (1,)), (1, (2, 3)), (2, (4,))):
                    above = pltpu.roll(zgot1[use, dx, dy, 1], back, 1)
                    below = pltpu.roll(zgot1[use, dx, dy, 0], back, 1)
                    both = jnp.where((lane8 >= 64) & (lane8 < 96), above, below)
                    for a in range(n):
                        for group in groups:
                            g = (1, group - 2, 0)[dy]
                            at = (128 - 4 * (2 * a + g)) % 128
                            side = pltpu.roll(both, at, 1) if at else both
                            rows = pl.ds(8 * group, 8)
                            own = ref[a, plane, rows, :]
                            side = jnp.where(side_lanes, side, 0.0)
                            ref[a, plane, rows, :] = jnp.where(lane8 < 64, own, side)
                return carry

            lax.fori_loop(low_plane, high_plane, one, 0)

        return finish

    def exchange2(use, tiles):
        n = len(tiles)
        for i, t in enumerate(tiles):
            dense2[use, i] = t
            dgot2[use, rad, 1, 1, i] = t
        copies = []
        for i, (a, b, c) in enumerate(near2):
            src = dense2.at[use, pl.ds(0, n)]
            dst = dgot2.at[use, rad, 1 - b, 1 - c, pl.ds(0, n)]
            copies.append(remote(src, dst, dsend2.at[use, i], drecv2.at[use, i], device(a, b, c)))
        for copy in copies:
            copy.start()

        def finish():
            for copy in copies:
                copy.wait()

        return finish

    def packed2(parts):
        tiles = []
        for i in range(0, len(parts), 4):
            out = zero8
            for j, part in enumerate(parts[i : i + 4]):
                part = pltpu.roll(part, 32 * j, 1) if j else part
                out = jnp.where((lane8 >= 32 * j) & (lane8 < 32 * j + 32), part, out)
            tiles.append(out)
        return tiles

    def turned2(use, source, dy, dz, tile_at, lanes):
        t = dgot2[use, source, dy, dz, tile_at]
        return pltpu.roll(t, lanes % 128, 1) if lanes % 128 else t

    def joined2(use, source, dy, part):
        i, at = part // 4, 32 * (part % 4)
        own = turned2(use, source, dy, 1, i, -at)
        after = turned2(use, source, dy, 2, i, 32 - at)
        before = turned2(use, source, dy, 0, i, 96 - at)
        out = jnp.where(lane8 < 32, own, jnp.where(lane8 < 64, after, before))
        return jnp.where((lane8 < 64) | (lane8 >= 96), out, 0.0)

    def unpack2(use, ref):
        n = ref.shape[0]

        def one(source, carry):
            for a in range(n):
                for x in range(2):
                    for dy in range(3):
                        ref[a, 2 + 2 * source + x, pl.ds(8 + 8 * dy, 8), :] = joined2(use, source, dy, 2 * a + x)
            return carry

        lax.fori_loop(0, 4, one, 0)

    coefs, invs = (None, coef1, coef2), (None, inv1, inv2)
    deeps, sols = (None, deep1, deep2), (None, sol1, sol2)

    def begin_deep(level, res, planes, keep):
        rows = pl.ds(8, DEEP_ROWS[level] - 16)

        def one(x, carry):
            for c in range(3):
                update = FIRST * invs[level][x, rows, :] * res[c, x, rows, :]
                deeps[level][0, c, x, rows, :] = update
                sols[level][c, x, rows, :] = update
            return carry

        lax.fori_loop(planes[0], planes[1], one, 0, unroll=2)

    def sweep_deep(level, p, res, out, planes, step, initial=False, rows=None):
        coef, inv, deep, sol = coefs[level], invs[level], deeps[level], sols[level]
        first, count = (8, DEEP_ROWS[level] - 16) if rows is None else rows
        here, under, over = pl.ds(first, count), pl.ds(first - 1, count), pl.ds(first + 1, count)

        def one(x, carry):
            diag, lower_x, upper_x = coef[0, x, here, :], coef[1, x, here, :], coef[1, x + 1, here, :]
            lower_y, upper_y, lower_z = coef[2, x, here, :], coef[2, x, over, :], coef[3, x, here, :]
            upper_z = pltpu.roll(lower_z, 127, 1)
            for c in range(3):
                v = deep[p, c, x, here, :]
                total = diag * v - lower_x * deep[p, c, x - 1, here, :] - upper_x * deep[p, c, x + 1, here, :]
                total = total - lower_y * deep[p, c, x, under, :] - upper_y * deep[p, c, x, over, :]
                total = total - lower_z * pltpu.roll(v, 1, 1) - upper_z * pltpu.roll(v, 127, 1)
                r = res[c, x, here, :] - total
                out[c, x, here, :] = r
                if step is None:
                    continue
                if initial:
                    update = FIRST * inv[x, here, :] * r
                    sol[c, x, here, :] = sol[c, x, here, :] + v + update
                else:
                    update = step[0] * v + step[1] * inv[x, here, :] * r
                    sol[c, x, here, :] = sol[c, x, here, :] + update
                deep[1 - p, c, x, here, :] = update
            return carry

        lax.fori_loop(planes[0], planes[1], one, 0, unroll=2)

    def sweep(p, halo, step, initial=False, emit=None):
        def plane(x, accs):
            at = block(x, 32)
            diag, inv = diag0[at, :], inv0[at, :]
            ls = [links0[k, at, :] for k in range(6)]
            rims = rims_of(halo, 12, x) if halo is not None else None
            packs = []
            for c in range(3):
                v = buf0[p, c, x + 1, own_rows, :]
                low_z, high_z = shifted(v, rims[4 * c : 4 * c + 4] if rims else rim0[c, x])
                total = diag * v - ls[0] * buf0[p, c, x, own_rows, :]
                total = total - ls[1] * buf0[p, c, x + 2, own_rows, :]
                total = total - ls[2] * buf0[p, c, x + 1, pl.ds(TOP - 1, 32), :]
                total = total - ls[3] * buf0[p, c, x + 1, pl.ds(TOP + 1, 32), :]
                total = total - ls[4] * low_z - ls[5] * high_z
                r = res0[c, at, :] - total
                if step is None:
                    res0[c, at, :] = r
                    continue
                if initial:
                    update = FIRST * inv * r
                    after = sol0[c, at, :] + v + update
                else:
                    update = step[0] * v + step[1] * inv * r
                    after = sol0[c, at, :] + update
                if emit is None:
                    sol0[c, at, :] = after
                    res0[c, at, :] = r
                    buf0[1 - p, c, x + 1, own_rows, :] = update
                    packs.append(update)
                else:
                    packs.append(after)
            if step is None:
                return accs
            low, high = pack(accs, packs, x)
            if emit is not None:
                emit(packs, x)
            return low, high

        return lax.fori_loop(0, 8, plane, (zero8, zero8), unroll=2)

    def restrict(source, rows, level, matrix):
        nx, ny, _ = LEVELS[level]
        half_x, half_y = nx // 2, ny // 2
        n = half_x * half_y

        def one(x, carry):
            for c in range(3):
                tmp[c, pl.ds(0, ny), :] = source(c, 2 * x) + source(c, 2 * x + 1)
            for c in range(3):
                flat[c, block(x, half_y), :] = tmp[c, pl.ds(0, half_y, 2), :] + tmp[c, pl.ds(1, half_y, 2), :]
            return carry

        lax.fori_loop(0, half_x, one, 0)
        return times(flat[0:3, :n, :].reshape(3 * n, 128), matrix)

    def gather(use):
        first = [
            remote(tile.at[use, 0], got1.at[use, lon], send1.at[use, i], recv1.at[use, i], target)
            for i, target in enumerate(along)
        ]
        second = [
            remote(tile.at[use, 1], got2.at[use, block(lat, 8)], send2.at[use, i], recv2.at[use, i], target)
            for i, target in enumerate(across)
        ]

        def begin(value):
            tile[use, 0] = value
            got1[use, lon] = value
            for copy in first:
                copy.start()

        def middle():
            for copy in first:
                copy.wait()
            total = got1[use, 0]
            for k in range(1, 8):
                total = total + got1[use, k]
            tile[use, 1] = total
            got2[use, block(lat, 8), :] = total
            for copy in second:
                copy.start()

        def end():
            for copy in second:
                copy.wait()

        return begin, middle, end

    lane1 = lanes_of((1, 128))
    runs = jnp.bitwise_and(owner[0, 0:1, :], 31)
    runs = jnp.concatenate([runs, jnp.full((1, 96), -1, jnp.int32)], 1)

    def member_of(columns):
        return (grid_row == jnp.broadcast_to(columns, (128, 128))).astype(F32)

    own_member = member_of(runs)

    def to_runs(rows):
        return lax.dot_general(
            rows, own_member, (((1,), (1,)), ((), ())), precision=HI, preferred_element_type=F32
        )

    def stacked(rows, count=8):
        out = jnp.zeros((count, 128), F32)
        at = rows_of((count, 128))
        for i, row in enumerate(rows):
            out = jnp.where(at == i, jnp.broadcast_to(row, (count, 128)), out)
        return out

    def rowsum(plane):
        return jnp.sum(plane, axis=0, keepdims=True)

    def run_sides():
        f = faces2
        wide = jnp.broadcast_to(runs, (8, 128))
        first_cell = (lane1 == 0) | (runs != pltpu.roll(wide, 1, 1)[0:1])
        last_cell = (lane1 == 31) | (runs != pltpu.roll(wide, 127, 1)[0:1])
        sides = [
            rowsum(f[0, 0:8, :]),
            rowsum(f[1, 8:16, :]),
            f[2, 0:1, :] + f[2, 8:9, :],
            f[3, 7:8, :] + f[3, 15:16, :],
            jnp.where(first_cell, rowsum(f[4, 0:8, :] + f[4, 8:16, :]), 0.0),
            jnp.where(last_cell, rowsum(f[5, 0:8, :] + f[5, 8:16, :]), 0.0),
        ]
        whole = sides[0] + sides[1] + sides[2] + sides[3] + sides[4] + sides[5]
        return to_runs(stacked([sides[0], sides[2], sides[4], whole]))

    def coarse_solve(meanwhile):
        begin, middle, end = gather(0)
        rows = []
        for block_x in range(4):
            for c in range(3):
                both = right2[c, 2 + 2 * block_x, OWN2, :] + right2[c, 3 + 2 * block_x, OWN2, :]
                rows.append(rowsum(both))
        sums = to_runs(stacked(rows, 16))
        row8 = rows_of((8, 128))
        value = zero8
        for block_x in range(4):
            part = jnp.where(row8 < 3, 0.0, pltpu.roll(dgot2[0, block_x, 1, 1, 2], 2, 0))
            for c in range(3):
                row = jnp.broadcast_to(sums[3 * block_x + c : 3 * block_x + c + 1], (8, 128))
                part = jnp.where(row8 == c, row, part)
            value = value + (pltpu.roll(part, 32 * block_x, 1) if block_x else part)
        begin(value)
        meanwhile()
        middle()
        end()

        def all_of(i):
            return got2[0, pl.ds(i, 8, 8), :]

        wrap = jnp.bitwise_and(lane8, 31)

        def lower_z(v):
            return jnp.where(wrap == 0, pltpu.roll(v, 97, 1), pltpu.roll(v, 1, 1))

        def upper_z(v):
            return jnp.where(wrap == 31, pltpu.roll(v, 31, 1), pltpu.roll(v, 127, 1))

        link_x = jnp.where(lane8 < 32, 0.0, all_of(3))
        link_y = jnp.where(row8 == 0, 0.0, all_of(4))
        link_z = all_of(5)
        link_xu, link_yu, link_zu = pltpu.roll(link_x, 96, 1), pltpu.roll(link_y, 7, 0), upper_z(link_z)
        diagonal = all_of(6)
        inverse = 1.0 / diagonal

        def operate(v):
            out = diagonal * v - link_x * pltpu.roll(v, 32, 1) - link_xu * pltpu.roll(v, 96, 1)
            out = out - link_y * pltpu.roll(v, 1, 0) - link_yu * pltpu.roll(v, 7, 0)
            return out - link_z * lower_z(v) - link_zu * upper_z(v)

        rs = [all_of(c) for c in range(3)]
        ds = [inverse * r * COARSE_FIRST for r in rs]
        es = list(ds)
        for a, b in COARSE_STEPS:
            rs = [r - operate(d) for r, d in zip(rs, ds)]
            ds = [a * d + b * inverse * r for r, d in zip(rs, ds)]
            es = [e + d for e, d in zip(es, ds)]
        for c in range(3):
            erows[c] = es[c]
        lats = [lax.rem(lat + 7, 8), lat, lax.rem(lat + 1, 8)]
        rows = [erows[c, pl.ds(at, 1), :] for c in range(3) for at in lats]
        rows = stacked(rows, 16)
        rows = [rows if k == 0 else pltpu.roll(rows, 128 - 32 * k, 1) for k in range(4)]
        spans = times(jnp.concatenate(rows, 0), region_member())
        for block_x in range(4):
            for c in range(3):
                for dy in range(3):
                    i = 16 * block_x + 3 * c + dy
                    row = jnp.broadcast_to(spans[i : i + 1], (8, 128))
                    for x in range(2):
                        deep2[1, c, 2 + 2 * block_x + x, pl.ds(8 + 8 * dy, 8), :] = row

    def region_member():
        own, before, after = (turned2(0, rad, 1, k, 2, t)[0:1] for k, t in ((1, 0), (0, 96), (2, 32)))
        columns = jnp.where(lane1 < 32, own, jnp.where(lane1 < 64, after, before))
        columns = jnp.where((lane1 < 64) | (lane1 >= 96), columns, -1.0).astype(jnp.int32)
        return member_of(columns)

    pending = {}

    def while_first():
        coarsen(0, faces0, faces1)
        for x in range(4):
            for k, value in enumerate(coefficients(1, faces1, x)):
                coef1[k, 4 + x, OWN1, :] = value
        pending["coef1"] = exchange1(0, coef1, 3, 4)

    def while_second():
        coarsen(1, faces1, faces2)
        values = [coefficients(2, faces2, x) for x in range(2)]
        last = jnp.where(rows_of((8, 128)) == 0, runs.astype(F32), pltpu.roll(run_sides(), 1, 0))
        parts = packed2([values[x][k] for k in range(4) for x in range(2)])
        pending["coef2"] = exchange2(0, parts + [last])

        def weigh(x, accs):
            v, inv = base[0, x + 1, own_rows, :], inv0[block(x, 32), :]
            parts = [2.0 * inv * (v - faces0[2 * c + 1, block(x, 32), :]) for c in range(3)]
            for c in range(3):
                hbuf[c, x + 1, own_rows, :] = parts[c]
            return pack(accs, parts, x)

        accs = lax.fori_loop(0, 8, weigh, (zero8, zero8), unroll=2)
        pending["h"] = send_all(accs, hbuf, hz, hsend, hrecv)

    def apply_to_h():
        halo = pending["h"]()

        def one(x, carry):
            at = block(x, 32)
            rims = rims_of(halo, 12, x)
            for c in range(3):
                v = hbuf[c, x + 1, own_rows, :]
                low_z, high_z = shifted(v, rims[4 * c : 4 * c + 4])
                total = diag0[at, :] * v - links0[0, at, :] * hbuf[c, x, own_rows, :]
                total = total - links0[1, at, :] * hbuf[c, x + 2, own_rows, :]
                total = total - links0[2, at, :] * hbuf[c, x + 1, pl.ds(TOP - 1, 32), :]
                total = total - links0[3, at, :] * hbuf[c, x + 1, pl.ds(TOP + 1, 32), :]
                applied[c, at, :] = total - links0[4, at, :] * low_z - links0[5, at, :] * high_z
            return carry

        lax.fori_loop(0, 8, one, 0, unroll=2)

    def while_third():
        pending["coef1"](0, 12)
        invert(coef1, inv1, 12)

    accs = start
    for step, meanwhile in ((STEPS[0], while_first), (STEPS[1], while_second), (None, while_third)):
        p = turn[0] % 2
        finish = exchange(accs)
        meanwhile()
        accs = sweep(p, finish(), step)

    sums = restrict(lambda c, x: res0[c, block(x, 32), :], 32, 0, pair)
    for c in range(3):
        for x in range(4):
            right1[c, 4 + x, OWN1, :] = sums[64 * c + 16 * x : 64 * c + 16 * x + 16]
    finish = exchange1(1, right1, 3, 3)
    pending["coef2"]()
    unpack2(0, coef2)
    invert(coef2, inv2, 12)
    finish(1, 11)
    begin_deep(1, right1, (1, 11), None)
    sweep_deep(1, 0, right1, right1, (2, 10), STEPS[0])
    sweep_deep(1, 1, right1, right1, (3, 9), STEPS[1])
    sweep_deep(1, 0, right1, left1, (4, 8), None, rows=(16, 16))

    sums = restrict(lambda c, x: left1[c, 4 + x, OWN1, :], 16, 1, own_pair)
    finish2 = exchange2(1, packed2([sums[16 * c + 8 * x : 16 * c + 8 * x + 8] for c in range(3) for x in range(2)]))
    finish1 = exchange1(2, left1, 3, 3)
    apply_to_h()
    finish2()
    unpack2(1, right2)
    all2 = (2, 10)
    begin_deep(2, right2, all2, None)
    sweep_deep(2, 0, right2, right2, all2, STEPS[0])
    sweep_deep(2, 1, right2, right2, all2, STEPS[1])
    sweep_deep(2, 0, right2, right2, all2, None)
    coarse_solve(lambda: finish1(1, 11))
    sweep_deep(2, 1, right2, right2, all2, STEPS[0], initial=True)
    sweep_deep(2, 0, right2, right2, all2, STEPS[0])
    sweep_deep(2, 1, right2, right2, all2, STEPS[1])

    def gather_rows(k, carry):
        for c in range(3):
            flat[c, block(k, 16), :] = sol2[c, 2 * rad + k, pl.ds(12, 16), :]
        return carry

    lax.fori_loop(0, 6, gather_rows, 0)
    for c in range(3):
        flat[c, 0:96, :] = times(flat[c, 0:96, :], spread1)

    def to_level1(k, carry):
        for c in range(3):
            value = flat[c, block(k, 16), :]
            for s in range(2):
                for t in range(2):
                    deep1[1, c, 2 * k + s, pl.ds(8 + t, 16, 2), :] = value
        return carry

    lax.fori_loop(0, 6, to_level1, 0)
    sweep_deep(1, 1, left1, left1, (1, 11), STEPS[0], initial=True)
    sweep_deep(1, 0, left1, left1, (2, 10), STEPS[0])
    sweep_deep(1, 1, left1, left1, (3, 9), STEPS[1])

    p = turn[0] % 2
    turn[0] += 1
    for c in range(3):
        flat[c] = times(sol1[c, 3:9, 12:36, :].reshape(144, 128), spread0)

    for k in range(6):
        for c in range(3):
            value = flat[c, 24 * k : 24 * k + 24, :]
            tmp[c, pl.ds(0, 24, 2), :] = value
            tmp[c, pl.ds(1, 24, 2), :] = value
            if 1 <= k <= 4:
                coarse = sol1[c, 3 + k, OWN1, :]
                rim = jnp.where(lane16 == 0, pltpu.roll(coarse, 1, 1), pltpu.roll(coarse, 63, 1))
                tmp[3 + c, pl.ds(0, 16, 2), :] = rim
                tmp[3 + c, pl.ds(1, 16, 2), :] = rim
        for c in range(3):
            for at in (2 * k - 1, 2 * k):
                if 0 <= at <= 9:
                    buf0[p, c, at] = tmp[c, pl.ds(0, 48), :]
                if 1 <= at <= 8:
                    rim0[c, at - 1] = tmp[3 + c, pl.ds(0, 32), :]

    accs = sweep(p, None, STEPS[0], initial=True)
    p = turn[0] % 2
    accs = sweep(p, exchange(accs)(), STEPS[0])
    p = turn[0] % 2
    finish = exchange(accs)
    begin, middle, end = gather(1)

    def add_up(x, total):
        at = block(x, 32)
        v = base[0, x + 1, own_rows, :]
        part = base[1, x + 1, own_rows, :]
        for c in range(3):
            update = buf0[p, c, x + 1, own_rows, :]
            weight = 2.0 * (v - faces0[2 * c + 1, at, :])
            h = hbuf[c, x + 1, own_rows, :]
            part = part - weight * (sol0[c, at, :] + STEPS[1][0] * update)
            part = part - STEPS[1][1] * (h * res0[c, at, :] - applied[c, at, :] * update)
        return total + (part[0:8] + part[8:16] + part[16:24] + part[24:32])

    begin(lax.fori_loop(0, 8, add_up, zero8, unroll=2))
    final = 1 - p

    def emit(afters, x):
        for c, after in enumerate(afters):
            adjoint[c, x] = after
            buf0[final, c, x + 1, own_rows, :] = after

    accs = sweep(p, finish(), STEPS[1], emit=emit)

    finish = exchange(accs)
    for _, wait in fwd_copies:
        wait()
    middle()
    halo = finish()
    fwd_halo = merged(zero8, fwd_z[1])

    def outputs(x, carry):
        v = base[0, x + 1, own_rows, :]
        keep_x, keep_y = edge(x, 1, 8), edge_rows(1, 32)
        ga, gf = [], []
        us = []
        rims, fwd_rims = rims_of(halo, 12, x), rims_of(fwd_halo, 12, x)
        for c in range(3):
            u = buf0[final, c, x + 1, own_rows, :]
            low_z, high_z = shifted(u, rims[4 * c : 4 * c + 4])
            ga.append([
                buf0[final, c, x + 2, own_rows, :] * keep_x - u,
                buf0[final, c, x + 1, pl.ds(TOP + 1, 32), :] * keep_y - u,
                high_z - u,
            ])
            us.append((u, low_z))
            w = fwd[c, x + 1, own_rows, :]
            _, high_w = shifted(w, fwd_rims[4 * c : 4 * c + 4])
            gf.append([
                fwd[c, x + 2, own_rows, :] * keep_x - w,
                fwd[c, x + 1, pl.ds(TOP + 1, 32), :] * keep_y - w,
                high_w - w,
            ])
        divergence = (
            us[0][0] - edge(x, 0, 8) * buf0[final, 0, x, own_rows, :]
            + (us[1][0] - edge_rows(0, 32) * buf0[final, 1, x + 1, pl.ds(TOP - 1, 32), :])
            + (us[2][0] - us[2][1])
        )
        pnext[x] = base[1, x + 1, own_rows, :] - v * divergence
        summed = gf[0][0] * ga[0][0] + gf[1][1] * ga[1][1] + gf[2][2] * ga[2][2]
        for d, e in ((0, 1), (0, 2), (1, 2)):
            summed = summed + 0.5 * (gf[e][d] + gf[d][e]) * (ga[e][d] + ga[d][e])
        gradient[x] = 2.0 * v * summed
        return carry

    end()
    total = zero8
    for b in range(8):
        total = total + got2[1, 8 * b : 8 * b + 8, :]
    tile[1, 2] = total
    got3[rad] = total
    last = [
        remote(tile.at[1, 2], got3.at[rad], send3.at[i], recv3.at[i], target)
        for i, target in enumerate(through)
    ]
    for copy in last:
        copy.start()
    lax.fori_loop(0, 8, outputs, 0, unroll=2)
    for copy in last:
        copy.wait()
    mean = jnp.sum(got3[0] + got3[1] + got3[2] + got3[3]) / CELLS

    def shift(x, carry):
        pnext[x] = pnext[x] - mean
        return carry

    lax.fori_loop(0, 8, shift, 0)


def per_device(forcing, pressure, viscosity, forward, owner):
    vmem, anywhere = pl.BlockSpec(memory_space=pltpu.VMEM), pl.BlockSpec(memory_space=pl.ANY)
    f32 = lambda *shape: pltpu.VMEM(shape, F32)
    dma = lambda *shape: pltpu.SemaphoreType.DMA(shape)
    return pl.pallas_call(
        kernel,
        out_shape=(
            jax.ShapeDtypeStruct((3, 8, 32, 128), F32),
            jax.ShapeDtypeStruct((8, 32, 128), F32),
            jax.ShapeDtypeStruct((8, 32, 128), F32),
        ),
        in_specs=[anywhere] * 4 + [vmem],
        out_specs=(vmem, vmem, vmem),
        scratch_shapes=[
            f32(3, 8, 32, 128), f32(2, 10, 48, 128), f32(3, 10, 48, 128), f32(1, 8, 128), f32(2, 8, 128),
            f32(2, 3, 10, 48, 128), f32(2, 4, 8, 128), f32(6, 256, 128), f32(6, 64, 128), f32(6, 16, 128),
            f32(6, 256, 128), f32(256, 128), f32(256, 128), f32(3, 256, 128), f32(3, 256, 128), f32(3, 8, 32, 128),
            f32(3, 10, 48, 128), f32(4, 8, 128), f32(3, 256, 128),
            f32(4, 13, 48, 128), f32(4, 12, 40, 128), f32(12, 48, 128), f32(12, 40, 128),
            f32(3, 12, 48, 128), f32(3, 12, 48, 128), f32(3, 12, 40, 128),
            f32(2, 3, 12, 48, 128), f32(2, 3, 12, 40, 128), f32(3, 12, 48, 128), f32(3, 12, 40, 128),
            f32(3, 2, 8, 128), f32(3, 3, 3, 2, 8, 128), f32(2, 3, 8, 128), f32(2, 4, 3, 3, 3, 8, 128),
            f32(6, 48, 128), f32(6, 144, 128), f32(3, 8, 128), f32(2, 3, 8, 128),
            f32(2, 8, 8, 128), f32(2, 64, 128), f32(4, 8, 128),
            dma(4), dma(2, 6), dma(2, 6), dma(3), dma(3), dma(2, 7), dma(2, 7), dma(2, 7), dma(2, 7), dma(3), dma(3),
            dma(3, 26), dma(3, 26), dma(2, 35), dma(2, 35), dma(6), dma(6),
        ],
        compiler_params=pltpu.CompilerParams(
            collective_id=0, has_side_effects=True, vmem_limit_bytes=60 * 1024 * 1024
        ),
    )(forcing, pressure, viscosity, forward, owner)


def solution(mesh):
    placed = (
        P(None, "rad", "lat", "lon"),
        P("rad", "lat", "lon"),
        P("rad", "lat", "lon"),
        P(None, "rad", "lat", "lon"),
        P("rad", "lat", "lon"),
    )
    return jax.shard_map(
        per_device,
        mesh=mesh,
        in_specs=placed,
        out_specs=(P(None, "rad", "lat", "lon"), P("rad", "lat", "lon"), P("rad", "lat", "lon")),
        check_vma=False,
    )
```

```python
import jax
import jax.numpy as jnp
from jax import lax
from jax.experimental import pallas as pl
from jax.experimental.pallas import tpu as pltpu
from jax.sharding import PartitionSpec as P

AXES = ("rad", "lat", "lon")
SIZES = (4, 8, 8)
MESH = pl.DeviceIdType.MESH
F32 = jnp.float32
HI = lax.Precision.HIGHEST
CDEG = 8
CELLS = 32 * 256 * 1024
LEVELS = ((8, 32, 128), (4, 16, 64), (2, 8, 32))
TOP = 8
DEEP_ROWS = {1: 48, 2: 40}
OWN1, OWN2 = pl.ds(16, 16), pl.ds(16, 8)


def cheb_constants(low, high, degree):
    middle, spread = 0.5 * (high + low), 0.5 * (high - low)
    factor = middle / spread
    old = 1.0 / factor
    steps = []
    for _ in range(degree - 1):
        new = 1.0 / (2.0 * factor - old)
        steps.append((new * old, 2.0 * new / spread))
        old = new
    return 1.0 / middle, steps


FIRST, STEPS = cheb_constants(0.5, 2.0, 3)
COARSE_FIRST, COARSE_STEPS = cheb_constants(0.1, 2.0, CDEG)


def lanes_of(shape):
    return lax.broadcasted_iota(jnp.int32, shape, len(shape) - 1)


def rows_of(shape):
    return lax.broadcasted_iota(jnp.int32, shape, len(shape) - 2)


def block(x, rows):
    return pl.ds(pl.multiple_of(x * rows, 8), rows)


def kernel(
    forcing, pressure, viscosity, forward, owner,
    adjoint, pnext, gradient,
    load, base, fwd, base_z, fwd_z,
    buf0, zbuf, faces0, faces1, faces2, links0, diag0, inv0, res0, sol0, rim0, hbuf, hz, applied, mbuf, mz,
    coef1, coef2, inv1, inv2, right1, left1, right2, deep1, deep2, sol1, sol2,
    zsend1, zgot1, cz, dgot2,
    tmp, flat, erows, tile, got1, got2, summed, layers, rings,
    in_sem, send_sem, recv_sem, fsend, frecv, send1, recv1, send2, recv2, sum_send1, sum_recv1, sum_send2, sum_recv2,
    dsend1, drecv1, dsend2, drecv2, hsend, hrecv, msend, mrecv, csend1, crecv1, csend2, crecv2,
):
    me = tuple(lax.axis_index(a) for a in AXES)
    rad, lat, lon = me

    def device(*steps):
        return tuple(
            lax.rem(m + (s % n), n) if s % n else m for m, s, n in zip(me, steps, SIZES)
        )

    up = [device(1, 0, 0), device(0, 1, 0), device(0, 0, 1)]
    down = [device(-1, 0, 0), device(0, -1, 0), device(0, 0, -1)]
    along = [device(0, 0, k) for k in range(1, 8)]
    across = [device(0, k, 0) for k in range(1, 8)]
    through = [device(k, 0, 0) for k in range(1, 4)]
    layer = [device(a, b, 0) for a in range(4) for b in range(8) if a or b]
    near1 = [
        (a, b, c) for a in (0, 1, -1) for b in (0, 1, -1) for c in (0, 1, -1) if a or b or c
    ]
    near2 = [
        (a, b, c) for a in range(4) for b in (0, 1, -1) for c in (0, 1, -1) if a or b or c
    ]
    peers = up + down

    own_rows = pl.ds(TOP, 32)
    loads = [
        pltpu.make_async_copy(viscosity, base.at[0, pl.ds(1, 8), own_rows], in_sem.at[0]),
        pltpu.make_async_copy(pressure, base.at[1, pl.ds(1, 8), own_rows], in_sem.at[1]),
        pltpu.make_async_copy(forcing, load, in_sem.at[2]),
        pltpu.make_async_copy(forward, fwd.at[:, pl.ds(1, 8), own_rows], in_sem.at[3]),
    ]
    for copy in loads:
        copy.start()

    def clear(ref, *at):
        ref[at] = jnp.zeros(ref[at].shape, F32)

    every, low_rows, high_rows = slice(None), slice(8, 16), slice(32, 40)
    for plane in (0, 9):
        clear(buf0, every, every, plane, slice(8, 40))
        clear(base, every, plane, slice(8, 40))
        clear(fwd, every, plane, slice(8, 40))
        clear(hbuf, every, plane, slice(8, 40))
        clear(mbuf, every, plane, slice(8, 40))
    clear(coef1, every, slice(0, 12), low_rows)
    clear(coef1, every, slice(0, 12), slice(32, 48))
    for planes in (slice(0, 4), slice(8, 12)):
        clear(coef1, every, planes, slice(16, 32))
        clear(right1, every, planes, slice(16, 32))
        clear(left1, every, planes, slice(16, 32))
    for ref in (right1, left1):
        clear(ref, every, every, low_rows)
        clear(ref, every, every, high_rows)
    clear(deep1, every, every, every, slice(0, 8))
    clear(deep1, every, every, every, slice(40, 48))
    clear(deep2, every, every, every, slice(0, 8))
    clear(deep2, every, every, every, slice(32, 40))
    for plane in (1, 10):
        clear(coef2, every, plane)
        clear(deep2, every, every, plane)
    clear(coef2, every, every, slice(32, 40))
    for plane in (0, 1, 10, 11):
        clear(sol2, every, plane, slice(8, 32))
    for side in (0, 2):
        clear(zgot1, every, side)

    barrier = pltpu.get_barrier_semaphore()
    for target in peers:
        pl.semaphore_signal(barrier, inc=1, device_id=target, device_id_type=MESH)

    def remote(src, dst, ssem, rsem, target):
        return pltpu.make_async_remote_copy(
            src_ref=src, dst_ref=dst, send_sem=ssem, recv_sem=rsem,
            device_id=target, device_id_type=MESH,
        )

    lane8 = lanes_of((8, 128))

    zero8 = jnp.zeros((8, 128), F32)

    def pack(accs, planes, x, lows=True, highs=True):
        parts = [p[8 * g : 8 * g + 8] for p in planes for g in range(4)]
        n = len(parts)
        low = high = zero8
        for j, part in enumerate(parts):
            turned = pltpu.roll(part, j, 1) if j else part
            if lows:
                low = jnp.where(lane8 == j, turned, low)
            if highs:
                high = jnp.where(lane8 == (127 + j) % 128, turned, high)
        return (
            accs[0] + pltpu.roll(low, n * x, 1) if lows else accs[0],
            accs[1] + pltpu.roll(high, n * x, 1) if highs else accs[1],
        )

    def merged(before, after):
        before, after = pltpu.roll(before, 1, 1), pltpu.roll(after, 127, 1)
        even = jnp.bitwise_and(lane8, 1) == 0
        return jnp.where(even, before, after), jnp.where(even, after, before)

    def rims_of(halo, n, x):
        turn_back = lax.rem(128 - n * x, 128)
        halo = [pltpu.roll(h, turn_back, 1) for h in halo]
        return [pltpu.roll(halo[j % 2], 128 - j, 1) if j else halo[0] for j in range(n)]

    lane32, lane16 = lanes_of((32, 128)), lanes_of((16, 128))

    def shifted(v, rims):
        rim = jnp.concatenate(rims, 0) if isinstance(rims, list) else rims
        low = jnp.where(lane32 == 0, rim, pltpu.roll(v, 1, 1))
        high = jnp.where(lane32 == 127, rim, pltpu.roll(v, 127, 1))
        return low, high

    def guarded(copy, step):
        sends_it, gets_it = (rad < 3, rad > 0) if step == 1 else (rad > 0, rad < 3)

        def start():
            pl.when(sends_it)(copy.start)

        def wait():
            pl.when(sends_it)(copy.wait_send)
            pl.when(gets_it)(copy.wait_recv)

        return start, wait

    def plain(copy):
        return copy.start, copy.wait

    def sends(buf, zref, ssem, rsem):
        rows, planes = pl.ds(TOP, 32), pl.ds(1, 8)
        parts = [
            (buf.at[:, 8, rows], buf.at[:, 0, rows], up[0]),
            (buf.at[:, 1, rows], buf.at[:, 9, rows], down[0]),
            (buf.at[:, planes, pl.ds(TOP + 31, 1)], buf.at[:, planes, pl.ds(TOP - 1, 1)], up[1]),
            (buf.at[:, planes, pl.ds(TOP, 1)], buf.at[:, planes, pl.ds(TOP + 32, 1)], down[1]),
            (zref.at[1], zref.at[2], up[2]),
            (zref.at[0], zref.at[3], down[2]),
        ]
        copies = [
            remote(src, dst, ssem.at[i], rsem.at[i], target)
            for i, (src, dst, target) in enumerate(parts)
        ]
        return [guarded(copies[0], 1), guarded(copies[1], -1)] + [plain(copy) for copy in copies[2:]]

    turn = [0]

    def send_all(accs, buf, zref, ssem, rsem):
        zref[0], zref[1] = accs
        copies = sends(buf, zref, ssem, rsem)
        for start, _ in copies:
            start()

        def finish():
            for _, wait in copies:
                wait()
            return merged(zref[2], zref[3])

        return finish

    def exchange(accs, buf=None):
        p = turn[0] % 2
        turn[0] += 1
        return send_all(accs, buf0.at[p] if buf is None else buf, zbuf.at[p], send_sem.at[p], recv_sem.at[p])

    for copy in loads[:2]:
        copy.wait()

    def pack_base(x, accs):
        return pack(accs, [base[c, x + 1, own_rows, :] for c in range(2)], x)

    accs = lax.fori_loop(0, 8, pack_base, (zero8, zero8), unroll=2)
    pl.semaphore_wait(barrier, len(peers))
    finish = exchange(accs, base)
    loads[3].wait()

    def pack_fwd(x, accs):
        return pack(accs, [fwd[c, x + 1, own_rows, :] for c in range(3)], x, highs=False)

    fwd_z[0] = lax.fori_loop(0, 8, pack_fwd, (zero8, zero8), unroll=2)[0]
    fwd_parts = [
        (fwd.at[:, 1, own_rows], fwd.at[:, 9, own_rows], down[0]),
        (fwd.at[:, pl.ds(1, 8), pl.ds(TOP, 1)], fwd.at[:, pl.ds(1, 8), pl.ds(TOP + 32, 1)], down[1]),
        (fwd_z.at[0], fwd_z.at[1], down[2]),
    ]
    fwd_copies = [
        remote(src, dst, fsend.at[i], frecv.at[i], target)
        for i, (src, dst, target) in enumerate(fwd_parts)
    ]
    fwd_copies = [guarded(fwd_copies[0], -1)] + [plain(copy) for copy in fwd_copies[1:]]
    for begin, _ in fwd_copies:
        begin()

    grid_row, grid_lane = rows_of((128, 128)), lanes_of((128, 128))
    pair = (grid_row // 2 == grid_lane).astype(F32)
    own_pair = jnp.where(grid_row < 64, pair, 0.0)
    pick = [(grid_row == 2 * grid_lane + s).astype(F32) for s in range(2)]
    spread0 = (grid_row == grid_lane // 2).astype(F32)
    spread1 = (grid_row == jnp.where(grid_lane < 96, 0, 64) + grid_lane // 2).astype(F32)

    def times(a, b):
        return jnp.dot(a, b, precision=HI, preferred_element_type=F32)

    def edge(x, side, nx):
        at_edge = (rad == 0) & (x == 0) if side == 0 else (rad == 3) & (x == nx - 1)
        return jnp.where(at_edge, 0.0, 1.0).astype(F32)

    def edge_rows(side, ny):
        row = rows_of((ny, 128))
        at_edge = (lat == 0) & (row == 0) if side == 0 else (lat == 7) & (row == ny - 1)
        return jnp.where(at_edge, 0.0, 1.0).astype(F32)

    loads[2].wait()
    halo = finish()

    def setup_plane(x, accs):
        v = base[0, x + 1, own_rows, :]
        rims = rims_of(halo, 8, x)
        low_z, high_z = shifted(v, rims[:4])
        lower_x, upper_x, lower_y, upper_y = edge(x, 0, 8), edge(x, 1, 8), edge_rows(0, 32), edge_rows(1, 32)
        six = [
            0.5 * (v + lower_x * base[0, x, own_rows, :]),
            0.5 * (v + upper_x * base[0, x + 2, own_rows, :]),
            0.5 * (v + lower_y * base[0, x + 1, pl.ds(TOP - 1, 32), :]),
            0.5 * (v + upper_y * base[0, x + 1, pl.ds(TOP + 1, 32), :]),
            0.5 * (v + low_z),
            0.5 * (v + high_z),
        ]
        at = block(x, 32)
        for k in range(6):
            faces0[k, at, :] = six[k]
        masks = (lower_x, upper_x, lower_y, upper_y)
        for k in range(6):
            links0[k, at, :] = six[k] * masks[k] if k < 4 else six[k]
        diag = six[0] + six[1] + six[2] + six[3] + six[4] + six[5]
        inv = 1.0 / diag
        diag0[at, :] = diag
        inv0[at, :] = inv
        p = base[1, x + 1, own_rows, :]
        _, high_p = shifted(p, rims[4:])
        grads = [
            base[1, x + 2, own_rows, :] * upper_x - p,
            base[1, x + 1, pl.ds(TOP + 1, 32), :] * upper_y - p,
            high_p - p,
        ]
        updates = []
        for c in range(3):
            right = load[c, x] - grads[c]
            res0[c, at, :] = right
            update = inv * right * FIRST
            sol0[c, at, :] = update
            buf0[1, c, x + 1, own_rows, :] = update
            updates.append(update)
        return pack(accs, updates, x)

    start = lax.fori_loop(0, 8, setup_plane, (zero8, zero8))

    def coarsen(level, fine, coarse):
        nx, ny, _ = LEVELS[level]
        half_x, half_y = nx // 2, ny // 2
        n = half_x * half_y

        def one(x, carry):
            for k in range(6):
                way, side = k // 2, k % 2
                if way == 0:
                    plane = fine[k, block(2 * x + side, ny), :]
                else:
                    plane = fine[k, block(2 * x, ny), :] + fine[k, block(2 * x + 1, ny), :]
                tmp[k, pl.ds(0, ny), :] = plane
            for k in range(6):
                way, side = k // 2, k % 2
                if way == 1:
                    both = tmp[k, pl.ds(side, half_y, 2), :]
                else:
                    both = tmp[k, pl.ds(0, half_y, 2), :] + tmp[k, pl.ds(1, half_y, 2), :]
                flat[k, block(x, half_y), :] = both
            return carry

        lax.fori_loop(0, half_x, one, 0)
        sums = times(flat[0:4, :n, :].reshape(4 * n, 128), pair).reshape(4, n, 128)
        for k in range(4):
            coarse[k] = sums[k]
        for k in range(4, 6):
            coarse[k] = times(flat[k, :n, :], pick[k - 4])

    def coefficients(level, faces, x):
        nx, ny, _ = LEVELS[level]
        six = [faces[k, pl.ds(x * ny, ny), :] for k in range(6)]
        total = six[0] + six[1] + six[2] + six[3] + six[4] + six[5]
        return [total, six[0] * edge(x, 0, nx), six[2] * edge_rows(0, ny), six[4]]

    def invert(coef, inv, planes):
        def one(x, carry):
            d = coef[0, x]
            inv[x] = jnp.where(d > 0.0, 1.0 / jnp.where(d > 0.0, d, 1.0), 0.0)
            return carry

        lax.fori_loop(0, planes, one, 0)

    side_lanes = (lane8 < 68) | (lane8 >= 124)

    def exchange1(use, ref, depth_up, depth_down):
        n = ref.shape[0]
        zlow = zhigh = zero8
        for x in range(4):
            for a in range(n):
                for g in range(2):
                    at = 4 * ((x * n + a) * 2 + g)
                    part = ref[a, 4 + x, pl.ds(16 + 8 * g, 8), :]
                    turned = pltpu.roll(part, at, 1) if at else part
                    zlow = jnp.where((lane8 >= at) & (lane8 < at + 4), turned, zlow)
                    top = (60 + at) % 128
                    zhigh = jnp.where((lane8 >= top) & (lane8 < top + 4), turned, zhigh)
        zsend1[use, 0] = zlow
        zsend1[use, 1] = zhigh
        copies = []
        for i, (a, b, c) in enumerate(near1):
            if c:
                src = zsend1.at[use, (c + 1) // 2]
                dst = zgot1.at[use, 1 - a, 1 - b, (1 - c) // 2]
            else:
                from_x, to_x, from_y, to_y = pl.ds(4, 4), pl.ds(4, 4), OWN1, OWN1
                if a == 1:
                    from_x, to_x = pl.ds(8 - depth_up, depth_up), pl.ds(4 - depth_up, depth_up)
                if a == -1:
                    from_x, to_x = pl.ds(4, depth_down), pl.ds(8, depth_down)
                if b == 1:
                    from_y, to_y = pl.ds(28, 4), pl.ds(12, 4)
                if b == -1:
                    from_y, to_y = pl.ds(16, 4), pl.ds(32, 4)
                src, dst = ref.at[:, from_x, from_y], ref.at[:, to_x, to_y]
            copy = remote(src, dst, dsend1.at[use, i], drecv1.at[use, i], device(a, b, c))
            copies.append((a, copy))

        def each(way, do):
            group = [copy for a, copy in copies if a == way]
            for copy in group:
                do(copy)

        for way, there in ((1, rad < 3), (-1, rad > 0)):
            pl.when(there)(lambda way=way: each(way, lambda copy: copy.start()))
        each(0, lambda copy: copy.start())

        def finish(low_plane, high_plane):
            for way, sends_it, gets_it in ((1, rad < 3, rad > 0), (-1, rad > 0, rad < 3)):
                pl.when(sends_it)(lambda way=way: each(way, lambda copy: copy.wait_send()))
                pl.when(gets_it)(lambda way=way: each(way, lambda copy: copy.wait_recv()))
            each(0, lambda copy: copy.wait())

            def one(plane, carry):
                dx, x = lax.div(plane, 4), lax.rem(plane, 4)
                back = lax.rem(192 - 8 * n * x, 128)
                for dy, groups in ((0, (1,)), (1, (2, 3)), (2, (4,))):
                    above = pltpu.roll(zgot1[use, dx, dy, 1], back, 1)
                    below = pltpu.roll(zgot1[use, dx, dy, 0], back, 1)
                    both = jnp.where((lane8 >= 64) & (lane8 < 96), above, below)
                    for a in range(n):
                        for group in groups:
                            g = (1, group - 2, 0)[dy]
                            at = (128 - 4 * (2 * a + g)) % 128
                            side = pltpu.roll(both, at, 1) if at else both
                            rows = pl.ds(8 * group, 8)
                            own = ref[a, plane, rows, :]
                            side = jnp.where(side_lanes, side, 0.0)
                            ref[a, plane, rows, :] = jnp.where(lane8 < 64, own, side)
                return carry

            lax.fori_loop(low_plane, high_plane, one, 0)

        return finish

    def spread_coef1():
        def go(copies):
            for start, _ in copies:
                start()

        def done(copies):
            for _, wait in copies:
                wait()

        def copy(i, src, dst, target):
            return remote(src, dst, csend1.at[i], crecv1.at[i], target)

        ref, planes = coef1, pl.ds(0, 12)
        in_x = [
            guarded(copy(0, ref.at[:, pl.ds(5, 3), OWN1], ref.at[:, pl.ds(1, 3), OWN1], up[0]), 1),
            guarded(copy(1, ref.at[:, pl.ds(4, 4), OWN1], ref.at[:, pl.ds(8, 4), OWN1], down[0]), -1),
        ]
        in_y = [
            plain(copy(2, ref.at[:, planes, pl.ds(28, 4)], ref.at[:, planes, pl.ds(12, 4)], up[1])),
            plain(copy(3, ref.at[:, planes, pl.ds(16, 4)], ref.at[:, planes, pl.ds(32, 4)], down[1])),
        ]
        in_z = [
            plain(copy(4, cz.at[1], cz.at[2], up[2])),
            plain(copy(5, cz.at[0], cz.at[3], down[2])),
        ]
        parts = [(s, a, g) for s in range(2) for a in range(4) for g in range(4)]

        def pack_pair(t, carry):
            zlow = zhigh = zero8
            for j, (s, a, g) in enumerate(parts):
                part = ref[a, 2 * t + s, pl.ds(8 + 8 * g, 8), :]
                turned = pltpu.roll(part, 4 * j, 1) if j else part
                zlow = jnp.where((lane8 >= 4 * j) & (lane8 < 4 * j + 4), turned, zlow)
                top = (60 + 4 * j) % 128
                zhigh = jnp.where((lane8 >= top) & (lane8 < top + 4), turned, zhigh)
            cz[0, t] = zlow
            cz[1, t] = zhigh
            return carry

        def unpack_pair(t, carry):
            below, above = cz[2, t], cz[3, t]
            for m in range(4):
                turn_by = (192 - 32 * m) % 128
                high = pltpu.roll(above, turn_by, 1) if turn_by else above
                low = pltpu.roll(below, turn_by, 1) if turn_by else below
                both = jnp.where((lane8 >= 64) & (lane8 < 96), high, low)
                for j in range(8):
                    s, a, g = parts[8 * m + j]
                    side = pltpu.roll(both, 128 - 4 * j, 1) if j else both
                    rows = pl.ds(8 + 8 * g, 8)
                    own = ref[a, 2 * t + s, rows, :]
                    side = jnp.where(side_lanes, side, 0.0)
                    ref[a, 2 * t + s, rows, :] = jnp.where(lane8 < 64, own, side)
            return carry

        def first():
            go(in_x)

        def second():
            done(in_x)
            go(in_y)

        def third():
            done(in_y)
            lax.fori_loop(0, 6, pack_pair, 0)
            go(in_z)

        def last():
            done(in_z)
            lax.fori_loop(0, 6, unpack_pair, 0)

        return first, second, third, last

    def spread_coef2(tiles):
        ref = dgot2.at[0]
        for i, t in enumerate(tiles):
            ref[rad, 1, 1, i] = t

        def copy(i, src, dst, target):
            return remote(src, dst, csend2.at[i], crecv2.at[i], target)

        steps = [
            [copy(i, ref.at[rad, 1, 1], ref.at[rad, 1, 1], target) for i, target in enumerate(through)],
            [
                copy(3, ref.at[:, 1, 1], ref.at[:, 0, 1], up[1]),
                copy(4, ref.at[:, 1, 1], ref.at[:, 2, 1], down[1]),
            ],
            [
                copy(5, ref.at[:, :, 1], ref.at[:, :, 0], up[2]),
                copy(6, ref.at[:, :, 1], ref.at[:, :, 2], down[2]),
            ],
        ]

        def go(i):
            if i:
                for c in steps[i - 1]:
                    c.wait()
            if i < 3:
                for c in steps[i]:
                    c.start()

        return go

    def exchange2(use, tiles):
        n = len(tiles)
        for i, t in enumerate(tiles):
            dgot2[use, rad, 1, 1, i] = t
        copies = []
        for i, (a, b, c) in enumerate(near2):
            src = dgot2.at[use, rad, 1, 1, pl.ds(0, n)]
            dst = dgot2.at[use, rad, 1 - b, 1 - c, pl.ds(0, n)]
            copies.append(remote(src, dst, dsend2.at[i], drecv2.at[i], device(a, b, c)))
        for copy in copies:
            copy.start()

        def finish():
            for copy in copies:
                copy.wait()

        return finish

    def packed2(parts):
        tiles = []
        for i in range(0, len(parts), 4):
            out = zero8
            for j, part in enumerate(parts[i : i + 4]):
                part = pltpu.roll(part, 32 * j, 1) if j else part
                out = jnp.where((lane8 >= 32 * j) & (lane8 < 32 * j + 32), part, out)
            tiles.append(out)
        return tiles

    def turned2(use, source, dy, dz, tile_at, lanes):
        t = dgot2[use, source, dy, dz, tile_at]
        return pltpu.roll(t, lanes % 128, 1) if lanes % 128 else t

    def joined2(use, source, dy, part):
        i, at = part // 4, 32 * (part % 4)
        own = turned2(use, source, dy, 1, i, -at)
        after = turned2(use, source, dy, 2, i, 32 - at)
        before = turned2(use, source, dy, 0, i, 96 - at)
        out = jnp.where(lane8 < 32, own, jnp.where(lane8 < 64, after, before))
        return jnp.where((lane8 < 64) | (lane8 >= 96), out, 0.0)

    def unpack2(use, ref):
        n = ref.shape[0]

        def one(source, carry):
            for a in range(n):
                for x in range(2):
                    for dy in range(3):
                        ref[a, 2 + 2 * source + x, pl.ds(8 + 8 * dy, 8), :] = joined2(use, source, dy, 2 * a + x)
            return carry

        lax.fori_loop(0, 4, one, 0)

    coefs, invs = (None, coef1, coef2), (None, inv1, inv2)
    deeps, sols = (None, deep1, deep2), (None, sol1, sol2)

    def begin_deep(level, res, planes, keep):
        rows = pl.ds(8, DEEP_ROWS[level] - 16)

        def one(x, carry):
            for c in range(3):
                update = FIRST * invs[level][x, rows, :] * res[c, x, rows, :]
                deeps[level][0, c, x, rows, :] = update
                sols[level][c, x, rows, :] = update
            return carry

        lax.fori_loop(planes[0], planes[1], one, 0, unroll=2)

    def sweep_deep(level, p, res, out, planes, step, initial=False, rows=None):
        coef, inv, deep, sol = coefs[level], invs[level], deeps[level], sols[level]
        first, count = (8, DEEP_ROWS[level] - 16) if rows is None else rows
        here, under, over = pl.ds(first, count), pl.ds(first - 1, count), pl.ds(first + 1, count)

        def one(x, carry):
            diag, lower_x, upper_x = coef[0, x, here, :], coef[1, x, here, :], coef[1, x + 1, here, :]
            lower_y, upper_y, lower_z = coef[2, x, here, :], coef[2, x, over, :], coef[3, x, here, :]
            upper_z = pltpu.roll(lower_z, 127, 1)
            for c in range(3):
                v = deep[p, c, x, here, :]
                total = diag * v - lower_x * deep[p, c, x - 1, here, :] - upper_x * deep[p, c, x + 1, here, :]
                total = total - lower_y * deep[p, c, x, under, :] - upper_y * deep[p, c, x, over, :]
                total = total - lower_z * pltpu.roll(v, 1, 1) - upper_z * pltpu.roll(v, 127, 1)
                r = res[c, x, here, :] - total
                out[c, x, here, :] = r
                if step is None:
                    continue
                if initial:
                    update = FIRST * inv[x, here, :] * r
                    sol[c, x, here, :] = sol[c, x, here, :] + v + update
                else:
                    update = step[0] * v + step[1] * inv[x, here, :] * r
                    sol[c, x, here, :] = sol[c, x, here, :] + update
                deep[1 - p, c, x, here, :] = update
            return carry

        lax.fori_loop(planes[0], planes[1], one, 0, unroll=2)

    def sweep(p, halo, step, initial=False, emit=None):
        def plane(x, accs):
            at = block(x, 32)
            diag, inv = diag0[at, :], inv0[at, :]
            ls = [links0[k, at, :] for k in range(6)]
            rims = rims_of(halo, 12, x) if halo is not None else None
            packs = []
            for c in range(3):
                v = buf0[p, c, x + 1, own_rows, :]
                low_z, high_z = shifted(v, rims[4 * c : 4 * c + 4] if rims else rim0[c, x])
                total = diag * v - ls[0] * buf0[p, c, x, own_rows, :]
                total = total - ls[1] * buf0[p, c, x + 2, own_rows, :]
                total = total - ls[2] * buf0[p, c, x + 1, pl.ds(TOP - 1, 32), :]
                total = total - ls[3] * buf0[p, c, x + 1, pl.ds(TOP + 1, 32), :]
                total = total - ls[4] * low_z - ls[5] * high_z
                r = res0[c, at, :] - total
                if step is None:
                    res0[c, at, :] = r
                    continue
                if initial:
                    update = FIRST * inv * r
                    after = sol0[c, at, :] + v + update
                else:
                    update = step[0] * v + step[1] * inv * r
                    after = sol0[c, at, :] + update
                if emit is None:
                    sol0[c, at, :] = after
                    res0[c, at, :] = r
                    buf0[1 - p, c, x + 1, own_rows, :] = update
                    packs.append(update)
                else:
                    packs.append(after)
            if step is None:
                return accs
            low, high = pack(accs, packs, x)
            if emit is not None:
                emit(packs, x)
            return low, high

        return lax.fori_loop(0, 8, plane, (zero8, zero8), unroll=2)

    def restrict(source, rows, level, matrix):
        nx, ny, _ = LEVELS[level]
        half_x, half_y = nx // 2, ny // 2
        n = half_x * half_y

        def one(x, carry):
            for c in range(3):
                tmp[c, pl.ds(0, ny), :] = source(c, 2 * x) + source(c, 2 * x + 1)
            for c in range(3):
                flat[c, block(x, half_y), :] = tmp[c, pl.ds(0, half_y, 2), :] + tmp[c, pl.ds(1, half_y, 2), :]
            return carry

        lax.fori_loop(0, half_x, one, 0)
        return times(flat[0:3, :n, :].reshape(3 * n, 128), matrix)

    def gather(use):
        first = [
            remote(tile.at[use, 0], got1.at[use, lon], send1.at[use, i], recv1.at[use, i], target)
            for i, target in enumerate(along)
        ]
        second = [
            remote(tile.at[use, 1], got2.at[use, block(lat, 8)], send2.at[use, i], recv2.at[use, i], target)
            for i, target in enumerate(across)
        ]

        def begin(value):
            tile[use, 0] = value
            got1[use, lon] = value
            for copy in first:
                copy.start()

        def middle():
            for copy in first:
                copy.wait()
            total = got1[use, 0]
            for k in range(1, 8):
                total = total + got1[use, k]
            tile[use, 1] = total
            got2[use, block(lat, 8), :] = total
            for copy in second:
                copy.start()

        def end():
            for copy in second:
                copy.wait()

        return begin, middle, end

    lane1 = lanes_of((1, 128))
    runs = jnp.bitwise_and(owner[0, 0:1, :], 31)
    runs = jnp.concatenate([runs, jnp.full((1, 96), -1, jnp.int32)], 1)

    def member_of(columns):
        return (grid_row == jnp.broadcast_to(columns, (128, 128))).astype(F32)

    own_member = member_of(runs)

    def to_runs(rows):
        return lax.dot_general(
            rows, own_member, (((1,), (1,)), ((), ())), precision=HI, preferred_element_type=F32
        )

    def stacked(rows, count=8):
        out = jnp.zeros((count, 128), F32)
        at = rows_of((count, 128))
        for i, row in enumerate(rows):
            out = jnp.where(at == i, jnp.broadcast_to(row, (count, 128)), out)
        return out

    def rowsum(plane):
        return jnp.sum(plane, axis=0, keepdims=True)

    def run_sides():
        f = faces2
        wide = jnp.broadcast_to(runs, (8, 128))
        first_cell = (lane1 == 0) | (runs != pltpu.roll(wide, 1, 1)[0:1])
        last_cell = (lane1 == 31) | (runs != pltpu.roll(wide, 127, 1)[0:1])
        sides = [
            rowsum(f[0, 0:8, :]),
            rowsum(f[1, 8:16, :]),
            f[2, 0:1, :] + f[2, 8:9, :],
            f[3, 7:8, :] + f[3, 15:16, :],
            jnp.where(first_cell, rowsum(f[4, 0:8, :] + f[4, 8:16, :]), 0.0),
            jnp.where(last_cell, rowsum(f[5, 0:8, :] + f[5, 8:16, :]), 0.0),
        ]
        whole = sides[0] + sides[1] + sides[2] + sides[3] + sides[4] + sides[5]
        return to_runs(stacked([sides[0], sides[2], sides[4], whole]))

    def coarse_solve(meanwhile):
        begin, middle, end = gather(0)
        rows = []
        for block_x in range(4):
            for c in range(3):
                both = right2[c, 2 + 2 * block_x, OWN2, :] + right2[c, 3 + 2 * block_x, OWN2, :]
                rows.append(rowsum(both))
        sums = to_runs(stacked(rows, 16))
        row8 = rows_of((8, 128))
        value = zero8
        for block_x in range(4):
            part = jnp.where(row8 < 3, 0.0, pltpu.roll(dgot2[0, block_x, 1, 1, 2], 2, 0))
            for c in range(3):
                row = jnp.broadcast_to(sums[3 * block_x + c : 3 * block_x + c + 1], (8, 128))
                part = jnp.where(row8 == c, row, part)
            value = value + (pltpu.roll(part, 32 * block_x, 1) if block_x else part)
        begin(value)
        meanwhile[0]()
        middle()
        meanwhile[1]()
        end()

        def all_of(i):
            return got2[0, pl.ds(i, 8, 8), :]

        wrap = jnp.bitwise_and(lane8, 31)

        def lower_z(v):
            return jnp.where(wrap == 0, pltpu.roll(v, 97, 1), pltpu.roll(v, 1, 1))

        def upper_z(v):
            return jnp.where(wrap == 31, pltpu.roll(v, 31, 1), pltpu.roll(v, 127, 1))

        link_x = jnp.where(lane8 < 32, 0.0, all_of(3))
        link_y = jnp.where(row8 == 0, 0.0, all_of(4))
        link_z = all_of(5)
        link_xu, link_yu, link_zu = pltpu.roll(link_x, 96, 1), pltpu.roll(link_y, 7, 0), upper_z(link_z)
        diagonal = all_of(6)
        inverse = 1.0 / diagonal

        def operate(v):
            out = diagonal * v - link_x * pltpu.roll(v, 32, 1) - link_xu * pltpu.roll(v, 96, 1)
            out = out - link_y * pltpu.roll(v, 1, 0) - link_yu * pltpu.roll(v, 7, 0)
            return out - link_z * lower_z(v) - link_zu * upper_z(v)

        rs = [all_of(c) for c in range(3)]
        ds = [inverse * r * COARSE_FIRST for r in rs]
        es = list(ds)
        for a, b in COARSE_STEPS:
            rs = [r - operate(d) for r, d in zip(rs, ds)]
            ds = [a * d + b * inverse * r for r, d in zip(rs, ds)]
            es = [e + d for e, d in zip(es, ds)]
        for c in range(3):
            erows[c] = es[c]
        lats = [lax.rem(lat + 7, 8), lat, lax.rem(lat + 1, 8)]
        rows = [erows[c, pl.ds(at, 1), :] for c in range(3) for at in lats]
        rows = stacked(rows, 16)
        rows = [rows if k == 0 else pltpu.roll(rows, 128 - 32 * k, 1) for k in range(4)]
        spans = times(jnp.concatenate(rows, 0), region_member())
        for block_x in range(4):
            for c in range(3):
                for dy in range(3):
                    i = 16 * block_x + 3 * c + dy
                    row = jnp.broadcast_to(spans[i : i + 1], (8, 128))
                    for x in range(2):
                        deep2[1, c, 2 + 2 * block_x + x, pl.ds(8 + 8 * dy, 8), :] = row

    def region_member():
        own, before, after = (turned2(0, rad, 1, k, 2, t)[0:1] for k, t in ((1, 0), (0, 96), (2, 32)))
        columns = jnp.where(lane1 < 32, own, jnp.where(lane1 < 64, after, before))
        columns = jnp.where((lane1 < 64) | (lane1 >= 96), columns, -1.0).astype(jnp.int32)
        return member_of(columns)

    pending = {}

    def while_first():
        coarsen(0, faces0, faces1)
        for x in range(4):
            for k, value in enumerate(coefficients(1, faces1, x)):
                coef1[k, 4 + x, OWN1, :] = value
        pending["coef1"] = spread_coef1()
        pending["coef1"][0]()

    def while_second():
        pending["coef1"][1]()
        coarsen(1, faces1, faces2)
        values = [coefficients(2, faces2, x) for x in range(2)]
        last = jnp.where(rows_of((8, 128)) == 0, runs.astype(F32), pltpu.roll(run_sides(), 1, 0))
        parts = packed2([values[x][k] for k in range(4) for x in range(2)])
        pending["coef2"] = spread_coef2(parts + [last])
        pending["coef2"](0)

    def weigh_all():
        def weigh(x, accs):
            v, inv = base[0, x + 1, own_rows, :], inv0[block(x, 32), :]
            parts = [2.0 * inv * (v - faces0[2 * c + 1, block(x, 32), :]) for c in range(3)]
            for c in range(3):
                hbuf[c, x + 1, own_rows, :] = parts[c]
            return pack(accs, parts, x)

        accs = lax.fori_loop(0, 8, weigh, (zero8, zero8), unroll=2)
        pending["h"] = send_all(accs, hbuf, hz, hsend, hrecv)

    def applied_to(buf, halo, x):
        at = block(x, 32)
        rims = rims_of(halo, 12, x)
        out = []
        for c in range(3):
            v = buf[c, x + 1, own_rows, :]
            low_z, high_z = shifted(v, rims[4 * c : 4 * c + 4])
            total = diag0[at, :] * v - links0[0, at, :] * buf[c, x, own_rows, :]
            total = total - links0[1, at, :] * buf[c, x + 2, own_rows, :]
            total = total - links0[2, at, :] * buf[c, x + 1, pl.ds(TOP - 1, 32), :]
            total = total - links0[3, at, :] * buf[c, x + 1, pl.ds(TOP + 1, 32), :]
            out.append(total - links0[4, at, :] * low_z - links0[5, at, :] * high_z)
        return out

    def apply_to_h():
        halo = pending["h"]()

        def one(x, accs):
            at = block(x, 32)
            v, inv = base[0, x + 1, own_rows, :], inv0[at, :]
            parts = []
            for c, g in enumerate(applied_to(hbuf, halo, x)):
                u = (1.0 + STEPS[1][0]) * 2.0 * (v - faces0[2 * c + 1, at, :]) - STEPS[1][1] * g
                applied[c, at, :] = u
                m = STEPS[0][1] * inv * u + STEPS[1][1] * hbuf[c, x + 1, own_rows, :]
                mbuf[c, x + 1, own_rows, :] = m
                parts.append(m)
            return pack(accs, parts, x)

        accs = lax.fori_loop(0, 8, one, (zero8, zero8))
        pending["m"] = send_all(accs, mbuf, mz, msend, mrecv)

    def apply_to_m():
        halo = pending["m"]()

        def one(x, carry):
            at = block(x, 32)
            for c, g in enumerate(applied_to(mbuf, halo, x)):
                applied[c, at, :] = STEPS[0][0] * applied[c, at, :] - g
            return carry

        lax.fori_loop(0, 8, one, 0)

    def while_third():
        pending["coef1"][2]()
        pending["coef2"](1)

    accs = start
    for step, meanwhile in ((STEPS[0], while_first), (STEPS[1], while_second), (None, while_third)):
        p = turn[0] % 2
        finish = exchange(accs)
        meanwhile()
        accs = sweep(p, finish(), step)

    sums = restrict(lambda c, x: res0[c, block(x, 32), :], 32, 0, pair)
    for c in range(3):
        for x in range(4):
            right1[c, 4 + x, OWN1, :] = sums[64 * c + 16 * x : 64 * c + 16 * x + 16]
    finish = exchange1(0, right1, 3, 3)
    pending["coef1"][3]()
    invert(coef1, inv1, 12)
    pending["coef2"](2)
    weigh_all()
    finish(1, 11)
    begin_deep(1, right1, (1, 11), None)
    sweep_deep(1, 0, right1, right1, (2, 10), STEPS[0])
    sweep_deep(1, 1, right1, right1, (3, 9), STEPS[1])
    sweep_deep(1, 0, right1, left1, (4, 8), None, rows=(16, 16))

    sums = restrict(lambda c, x: left1[c, 4 + x, OWN1, :], 16, 1, own_pair)
    finish2 = exchange2(1, packed2([sums[16 * c + 8 * x : 16 * c + 8 * x + 8] for c in range(3) for x in range(2)]))
    finish1 = exchange1(1, left1, 3, 3)
    pending["coef2"](3)
    unpack2(0, coef2)
    invert(coef2, inv2, 12)
    apply_to_h()
    finish2()
    unpack2(1, right2)
    all2 = (2, 10)
    begin_deep(2, right2, all2, None)
    sweep_deep(2, 0, right2, right2, all2, STEPS[0])
    sweep_deep(2, 1, right2, right2, all2, STEPS[1])
    sweep_deep(2, 0, right2, right2, all2, None)
    coarse_solve((lambda: finish1(1, 11), apply_to_m))
    sweep_deep(2, 1, right2, right2, all2, STEPS[0], initial=True)
    sweep_deep(2, 0, right2, right2, all2, STEPS[0])
    sweep_deep(2, 1, right2, right2, all2, STEPS[1])

    def gather_rows(k, carry):
        for c in range(3):
            flat[c, block(k, 16), :] = sol2[c, 2 * rad + k, pl.ds(12, 16), :]
        return carry

    lax.fori_loop(0, 6, gather_rows, 0)
    for c in range(3):
        flat[c, 0:96, :] = times(flat[c, 0:96, :], spread1)

    def to_level1(k, carry):
        for c in range(3):
            value = flat[c, block(k, 16), :]
            for s in range(2):
                for t in range(2):
                    deep1[1, c, 2 * k + s, pl.ds(8 + t, 16, 2), :] = value
        return carry

    lax.fori_loop(0, 6, to_level1, 0)
    sweep_deep(1, 1, left1, left1, (1, 11), STEPS[0], initial=True)
    sweep_deep(1, 0, left1, left1, (2, 10), STEPS[0])
    sweep_deep(1, 1, left1, left1, (3, 9), STEPS[1])

    p = turn[0] % 2
    turn[0] += 1
    for c in range(3):
        flat[c] = times(sol1[c, 3:9, 12:36, :].reshape(144, 128), spread0)

    for k in range(6):
        for c in range(3):
            value = flat[c, 24 * k : 24 * k + 24, :]
            tmp[c, pl.ds(0, 24, 2), :] = value
            tmp[c, pl.ds(1, 24, 2), :] = value
            if 1 <= k <= 4:
                coarse = sol1[c, 3 + k, OWN1, :]
                rim = jnp.where(lane16 == 0, pltpu.roll(coarse, 1, 1), pltpu.roll(coarse, 63, 1))
                tmp[3 + c, pl.ds(0, 16, 2), :] = rim
                tmp[3 + c, pl.ds(1, 16, 2), :] = rim
        for c in range(3):
            for at in (2 * k - 1, 2 * k):
                if 0 <= at <= 9:
                    buf0[p, c, at] = tmp[c, pl.ds(0, 48), :]
                if 1 <= at <= 8:
                    rim0[c, at - 1] = tmp[3 + c, pl.ds(0, 32), :]

    accs = sweep(p, None, STEPS[0], initial=True)
    p = turn[0] % 2
    finish = exchange(accs)

    def add_up(x, total):
        at = block(x, 32)
        v = base[0, x + 1, own_rows, :]
        part = base[1, x + 1, own_rows, :]
        for c in range(3):
            part = part - 2.0 * (v - faces0[2 * c + 1, at, :]) * sol0[c, at, :]
            part = part - mbuf[c, x + 1, own_rows, :] * res0[c, at, :]
            part = part - applied[c, at, :] * buf0[p, c, x + 1, own_rows, :]
        return total + (part[0:8] + part[8:16] + part[16:24] + part[24:32])

    partial = lax.fori_loop(0, 8, add_up, zero8, unroll=2)
    sums1 = [
        remote(summed.at[0], layers.at[rad, lat], sum_send1.at[i], sum_recv1.at[i], target)
        for i, target in enumerate(layer)
    ]
    sums2 = [
        remote(summed.at[1], rings.at[lon], sum_send2.at[i], sum_recv2.at[i], target)
        for i, target in enumerate(along)
    ]
    summed[0] = partial
    layers[rad, lat] = partial
    for copy in sums1:
        copy.start()
    accs = sweep(p, finish(), STEPS[0])
    p = turn[0] % 2
    finish = exchange(accs)
    for copy in sums1:
        copy.wait()
    total = zero8
    for a in range(4):
        for b in range(8):
            total = total + layers[a, b]
    summed[1] = total
    rings[lon] = total
    for copy in sums2:
        copy.start()
    final = 1 - p

    def emit(afters, x):
        for c, after in enumerate(afters):
            adjoint[c, x] = after
            buf0[final, c, x + 1, own_rows, :] = after

    accs = sweep(p, finish(), STEPS[1], emit=emit)

    finish = exchange(accs)
    for _, wait in fwd_copies:
        wait()
    halo = finish()
    fwd_halo = merged(zero8, fwd_z[1])

    def outputs(x, carry):
        v = base[0, x + 1, own_rows, :]
        keep_x, keep_y = edge(x, 1, 8), edge_rows(1, 32)
        ga, gf = [], []
        us = []
        rims, fwd_rims = rims_of(halo, 12, x), rims_of(fwd_halo, 12, x)
        for c in range(3):
            u = buf0[final, c, x + 1, own_rows, :]
            low_z, high_z = shifted(u, rims[4 * c : 4 * c + 4])
            ga.append([
                buf0[final, c, x + 2, own_rows, :] * keep_x - u,
                buf0[final, c, x + 1, pl.ds(TOP + 1, 32), :] * keep_y - u,
                high_z - u,
            ])
            us.append((u, low_z))
            w = fwd[c, x + 1, own_rows, :]
            _, high_w = shifted(w, fwd_rims[4 * c : 4 * c + 4])
            gf.append([
                fwd[c, x + 2, own_rows, :] * keep_x - w,
                fwd[c, x + 1, pl.ds(TOP + 1, 32), :] * keep_y - w,
                high_w - w,
            ])
        divergence = (
            us[0][0] - edge(x, 0, 8) * buf0[final, 0, x, own_rows, :]
            + (us[1][0] - edge_rows(0, 32) * buf0[final, 1, x + 1, pl.ds(TOP - 1, 32), :])
            + (us[2][0] - us[2][1])
        )
        pnext[x] = base[1, x + 1, own_rows, :] - v * divergence
        summed = gf[0][0] * ga[0][0] + gf[1][1] * ga[1][1] + gf[2][2] * ga[2][2]
        for d, e in ((0, 1), (0, 2), (1, 2)):
            summed = summed + 0.5 * (gf[e][d] + gf[d][e]) * (ga[e][d] + ga[d][e])
        gradient[x] = 2.0 * v * summed
        return carry

    lax.fori_loop(0, 8, outputs, 0, unroll=2)
    for copy in sums2:
        copy.wait()
    total = rings[0]
    for k in range(1, 8):
        total = total + rings[k]
    mean = jnp.sum(total) / CELLS

    def shift(x, carry):
        pnext[x] = pnext[x] - mean
        return carry

    lax.fori_loop(0, 8, shift, 0)


def per_device(forcing, pressure, viscosity, forward, owner):
    vmem, anywhere = pl.BlockSpec(memory_space=pltpu.VMEM), pl.BlockSpec(memory_space=pl.ANY)
    f32 = lambda *shape: pltpu.VMEM(shape, F32)
    dma = lambda *shape: pltpu.SemaphoreType.DMA(shape)
    return pl.pallas_call(
        kernel,
        out_shape=(
            jax.ShapeDtypeStruct((3, 8, 32, 128), F32),
            jax.ShapeDtypeStruct((8, 32, 128), F32),
            jax.ShapeDtypeStruct((8, 32, 128), F32),
        ),
        in_specs=[anywhere] * 4 + [vmem],
        out_specs=(vmem, vmem, vmem),
        scratch_shapes=[
            f32(3, 8, 32, 128), f32(2, 10, 48, 128), f32(3, 10, 48, 128), f32(1, 8, 128), f32(2, 8, 128),
            f32(2, 3, 10, 48, 128), f32(2, 4, 8, 128), f32(6, 256, 128), f32(6, 64, 128), f32(6, 16, 128),
            f32(6, 256, 128), f32(256, 128), f32(256, 128), f32(3, 256, 128), f32(3, 256, 128), f32(3, 8, 32, 128),
            f32(3, 10, 48, 128), f32(4, 8, 128), f32(3, 256, 128), f32(3, 10, 48, 128), f32(4, 8, 128),
            f32(4, 13, 48, 128), f32(4, 12, 40, 128), f32(12, 48, 128), f32(12, 40, 128),
            f32(3, 12, 48, 128), f32(3, 12, 48, 128), f32(3, 12, 40, 128),
            f32(2, 3, 12, 48, 128), f32(2, 3, 12, 40, 128), f32(3, 12, 48, 128), f32(3, 12, 40, 128),
            f32(2, 2, 8, 128), f32(2, 3, 3, 2, 8, 128), f32(4, 6, 8, 128), f32(2, 4, 3, 3, 3, 8, 128),
            f32(6, 48, 128), f32(6, 144, 128), f32(3, 8, 128), f32(1, 2, 8, 128),
            f32(1, 8, 8, 128), f32(1, 64, 128), f32(2, 8, 128), f32(4, 8, 8, 128), f32(8, 8, 128),
            dma(4), dma(2, 6), dma(2, 6), dma(3), dma(3), dma(1, 7), dma(1, 7), dma(1, 7), dma(1, 7), dma(31), dma(31), dma(7), dma(7),
            dma(2, 26), dma(2, 26), dma(35), dma(35), dma(6), dma(6), dma(6), dma(6), dma(6), dma(6), dma(7), dma(7),
        ],
        compiler_params=pltpu.CompilerParams(
            collective_id=0, has_side_effects=True, vmem_limit_bytes=60 * 1024 * 1024
        ),
    )(forcing, pressure, viscosity, forward, owner)


def solution(mesh):
    placed = (
        P(None, "rad", "lat", "lon"),
        P("rad", "lat", "lon"),
        P("rad", "lat", "lon"),
        P(None, "rad", "lat", "lon"),
        P("rad", "lat", "lon"),
    )
    return jax.shard_map(
        per_device,
        mesh=mesh,
        in_specs=placed,
        out_specs=(P(None, "rad", "lat", "lon"), P("rad", "lat", "lon"), P("rad", "lat", "lon")),
        check_vma=False,
    )
```

```python
import jax
import jax.numpy as jnp
from jax import lax
from jax.experimental import pallas as pl
from jax.experimental.pallas import tpu as pltpu
from jax.sharding import PartitionSpec as P

AXES = ("rad", "lat", "lon")
SIZES = (4, 8, 8)
MESH = pl.DeviceIdType.MESH
F32 = jnp.float32
HI = lax.Precision.HIGHEST
CDEG = 8
CELLS = 32 * 256 * 1024
LEVELS = ((8, 32, 128), (4, 16, 64), (2, 8, 32))
TOP = 8
DEEP_ROWS = {1: 48, 2: 40}
OWN1, OWN2 = pl.ds(16, 16), pl.ds(16, 8)


def cheb_constants(low, high, degree):
    middle, spread = 0.5 * (high + low), 0.5 * (high - low)
    factor = middle / spread
    old = 1.0 / factor
    steps = []
    for _ in range(degree - 1):
        new = 1.0 / (2.0 * factor - old)
        steps.append((new * old, 2.0 * new / spread))
        old = new
    return 1.0 / middle, steps


FIRST, STEPS = cheb_constants(0.5, 2.0, 3)
COARSE_FIRST, COARSE_STEPS = cheb_constants(0.1, 2.0, CDEG)


def lanes_of(shape):
    return lax.broadcasted_iota(jnp.int32, shape, len(shape) - 1)


def rows_of(shape):
    return lax.broadcasted_iota(jnp.int32, shape, len(shape) - 2)


def block(x, rows):
    return pl.ds(pl.multiple_of(x * rows, 8), rows)


def kernel(
    forcing, pressure, viscosity, forward, owner,
    adjoint, pnext, gradient,
    load, base, fwd, base_z, fwd_z,
    buf0, zbuf, faces0, faces1, faces2, links0, diag0, inv0, res0, sol0, rim0, hbuf, hz, applied, mbuf, mz,
    wide0, rim_link, halo_x, halo_y,
    coef1, coef2, inv1, inv2, right1, left1, right2, deep1, deep2, sol1, sol2,
    zsend1, zgot1, cz, dgot2,
    tmp, flat, erows, tile, got1, got2, summed, sum_x, sum_y, sum_z,
    in_sem, send_sem, recv_sem, fsend, frecv, send1, recv1, send2, recv2, sum_send, sum_recv,
    dsend1, drecv1, dsend2, drecv2, hsend, hrecv, msend, mrecv, csend1, crecv1, csend2, crecv2,
):
    me = tuple(lax.axis_index(a) for a in AXES)
    rad, lat, lon = me

    def device(*steps):
        return tuple(
            lax.rem(m + (s % n), n) if s % n else m for m, s, n in zip(me, steps, SIZES)
        )

    up = [device(1, 0, 0), device(0, 1, 0), device(0, 0, 1)]
    down = [device(-1, 0, 0), device(0, -1, 0), device(0, 0, -1)]
    along = [device(0, 0, k) for k in (4, 3, 5, 2, 6, 1, 7)]
    across = [device(0, k, 0) for k in (4, 3, 5, 2, 6, 1, 7)]
    through = [device(k, 0, 0) for k in range(1, 4)]
    near1 = [
        (a, b, c) for c in (1, -1, 0) for b in (1, -1, 0) for a in (1, -1, 0) if a or b or c
    ]
    near2 = [
        (a, b, c) for c in (1, -1, 0) for a in (2, 1, 3, 0) for b in (1, -1, 0) if a or b or c
    ]
    peers = up + down

    own_rows = pl.ds(TOP, 32)
    loads = [
        pltpu.make_async_copy(viscosity, base.at[0, pl.ds(1, 8), own_rows], in_sem.at[0]),
        pltpu.make_async_copy(pressure, base.at[1, pl.ds(1, 8), own_rows], in_sem.at[1]),
        pltpu.make_async_copy(forcing, load, in_sem.at[2]),
        pltpu.make_async_copy(forward, fwd.at[:, pl.ds(1, 8), own_rows], in_sem.at[3]),
    ]
    for copy in loads:
        copy.start()

    def clear(ref, *at):
        ref[at] = jnp.zeros(ref[at].shape, F32)

    every, low_rows, high_rows = slice(None), slice(8, 16), slice(32, 40)
    for plane in (0, 9):
        clear(base, every, plane, slice(8, 40))
        clear(fwd, every, plane, slice(8, 40))

    barrier = pltpu.get_barrier_semaphore()
    for target in peers:
        pl.semaphore_signal(barrier, inc=1, device_id=target, device_id_type=MESH)

    for plane in (0, 9):
        clear(buf0, every, every, plane, slice(8, 40))
        clear(halo_x, every, plane // 9)
        clear(halo_y, every, plane // 9)
        clear(hbuf, every, plane, slice(8, 40))
        clear(mbuf, every, plane, slice(8, 40))
    clear(buf0, every, every, slice(1, 9), slice(0, 8))
    clear(buf0, every, every, slice(1, 9), slice(40, 48))
    clear(coef1, every, slice(0, 12), low_rows)
    clear(coef1, every, slice(0, 12), slice(32, 48))
    for planes in (slice(0, 4), slice(8, 12)):
        clear(coef1, every, planes, slice(16, 32))
        clear(right1, every, planes, slice(16, 32))
        clear(left1, every, planes, slice(16, 32))
    for ref in (right1, left1):
        clear(ref, every, every, low_rows)
        clear(ref, every, every, high_rows)
    clear(deep1, every, every, every, slice(0, 8))
    clear(deep1, every, every, every, slice(40, 48))
    clear(deep2, every, every, every, slice(0, 8))
    clear(deep2, every, every, every, slice(32, 40))
    for plane in (1, 10):
        clear(coef2, every, plane)
        clear(deep2, every, every, plane)
    clear(coef2, every, every, slice(32, 40))
    for plane in (0, 1, 10, 11):
        clear(sol2, every, plane, slice(8, 32))
    for side in (0, 2):
        clear(zgot1, every, side)

    def remote(src, dst, ssem, rsem, target):
        return pltpu.make_async_remote_copy(
            src_ref=src, dst_ref=dst, send_sem=ssem, recv_sem=rsem,
            device_id=target, device_id_type=MESH,
        )

    lane8 = lanes_of((8, 128))

    zero8 = jnp.zeros((8, 128), F32)

    def pack(accs, planes, x, lows=True, highs=True):
        parts = [p[8 * g : 8 * g + 8] for p in planes for g in range(4)]
        n = len(parts)
        low = high = zero8
        for j, part in enumerate(parts):
            turned = pltpu.roll(part, j, 1) if j else part
            if lows:
                low = jnp.where(lane8 == j, turned, low)
            if highs:
                high = jnp.where(lane8 == (127 + j) % 128, turned, high)
        return (
            accs[0] + pltpu.roll(low, n * x, 1) if lows else accs[0],
            accs[1] + pltpu.roll(high, n * x, 1) if highs else accs[1],
        )

    def merged(before, after):
        before, after = pltpu.roll(before, 1, 1), pltpu.roll(after, 127, 1)
        even = jnp.bitwise_and(lane8, 1) == 0
        return jnp.where(even, before, after), jnp.where(even, after, before)

    def rims_of(halo, n, x):
        turn_back = lax.rem(128 - n * x, 128)
        halo = [pltpu.roll(h, turn_back, 1) for h in halo]
        return [pltpu.roll(halo[j % 2], 128 - j, 1) if j else halo[0] for j in range(n)]

    lane32, lane16 = lanes_of((32, 128)), lanes_of((16, 128))

    def shifted(v, rims):
        rim = jnp.concatenate(rims, 0) if isinstance(rims, list) else rims
        low = jnp.where(lane32 == 0, rim, pltpu.roll(v, 1, 1))
        high = jnp.where(lane32 == 127, rim, pltpu.roll(v, 127, 1))
        return low, high

    def guarded(copy, step):
        sends_it, gets_it = (rad < 3, rad > 0) if step == 1 else (rad > 0, rad < 3)

        def start():
            pl.when(sends_it)(copy.start)

        def wait():
            pl.when(sends_it)(copy.wait_send)
            pl.when(gets_it)(copy.wait_recv)

        return start, wait

    def plain(copy):
        return copy.start, copy.wait

    def sends(buf, zref, ssem, rsem, beside=None):
        rows, planes = pl.ds(TOP, 32), pl.ds(1, 8)
        if beside is None:
            to = [buf.at[:, 0, rows], buf.at[:, 9, rows], buf.at[:, planes, pl.ds(TOP - 1, 1)], buf.at[:, planes, pl.ds(TOP + 32, 1)]]
        else:
            in_x, in_y = beside
            to = [in_x.at[0], in_x.at[1], in_y.at[0, :, :, pl.ds(0, 1)], in_y.at[1, :, :, pl.ds(7, 1)]]
        parts = [
            (buf.at[:, 8, rows], to[0], up[0]),
            (buf.at[:, 1, rows], to[1], down[0]),
            (buf.at[:, planes, pl.ds(TOP + 31, 1)], to[2], up[1]),
            (buf.at[:, planes, pl.ds(TOP, 1)], to[3], down[1]),
            (zref.at[1], zref.at[2], up[2]),
            (zref.at[0], zref.at[3], down[2]),
        ]
        copies = [
            remote(src, dst, ssem.at[i], rsem.at[i], target)
            for i, (src, dst, target) in enumerate(parts)
        ]
        return [plain(copy) for copy in copies[4:]] + [guarded(copies[0], 1), guarded(copies[1], -1)] + [plain(copy) for copy in copies[2:4]]

    turn = [0]

    def send_all(accs, buf, zref, ssem, rsem, beside=None):
        zref[0], zref[1] = accs
        copies = sends(buf, zref, ssem, rsem, beside)
        for start, _ in copies:
            start()

        def finish():
            for _, wait in copies:
                wait()
            return merged(zref[2], zref[3])

        return finish

    def exchange(accs, buf=None):
        p = turn[0] % 2
        turn[0] += 1
        sems = (zbuf.at[p], send_sem.at[p], recv_sem.at[p])
        return send_all(accs, buf0.at[p], *sems, (halo_x.at[p], halo_y.at[p])) if buf is None else send_all(accs, buf, *sems)

    for copy in loads[:2]:
        copy.wait()

    def pack_base(x, accs):
        return pack(accs, [base[c, x + 1, own_rows, :] for c in range(2)], x)

    accs = lax.fori_loop(0, 8, pack_base, (zero8, zero8), unroll=2)
    pl.semaphore_wait(barrier, len(peers))
    finish = exchange(accs, base)
    loads[3].wait()

    def pack_fwd(x, accs):
        return pack(accs, [fwd[c, x + 1, own_rows, :] for c in range(3)], x, highs=False)

    fwd_z[0] = lax.fori_loop(0, 8, pack_fwd, (zero8, zero8), unroll=2)[0]
    fwd_parts = [
        (fwd.at[:, 1, own_rows], fwd.at[:, 9, own_rows], down[0]),
        (fwd.at[:, pl.ds(1, 8), pl.ds(TOP, 1)], fwd.at[:, pl.ds(1, 8), pl.ds(TOP + 32, 1)], down[1]),
        (fwd_z.at[0], fwd_z.at[1], down[2]),
    ]
    fwd_copies = [
        remote(src, dst, fsend.at[i], frecv.at[i], target)
        for i, (src, dst, target) in enumerate(fwd_parts)
    ]
    fwd_copies = [guarded(fwd_copies[0], -1)] + [plain(copy) for copy in fwd_copies[1:]]
    for begin, _ in fwd_copies:
        begin()

    grid_row, grid_lane = rows_of((128, 128)), lanes_of((128, 128))
    pair = (grid_row // 2 == grid_lane).astype(F32)
    own_pair = jnp.where(grid_row < 64, pair, 0.0)
    pick = [(grid_row == 2 * grid_lane + s).astype(F32) for s in range(2)]
    spread0 = (grid_row == grid_lane // 2).astype(F32)
    spread1 = (grid_row == jnp.where(grid_lane < 96, 0, 64) + grid_lane // 2).astype(F32)

    def times(a, b):
        return jnp.dot(a, b, precision=HI, preferred_element_type=F32)

    def edge(x, side, nx):
        at_edge = (rad == 0) & (x == 0) if side == 0 else (rad == 3) & (x == nx - 1)
        return jnp.where(at_edge, 0.0, 1.0).astype(F32)

    def edge_rows(side, ny):
        row = rows_of((ny, 128))
        at_edge = (lat == 0) & (row == 0) if side == 0 else (lat == 7) & (row == ny - 1)
        return jnp.where(at_edge, 0.0, 1.0).astype(F32)

    loads[2].wait()
    halo = finish()

    def setup_plane(x, accs):
        v = base[0, x + 1, own_rows, :]
        rims = rims_of(halo, 8, x)
        low_z, high_z = shifted(v, rims[:4])
        lower_x, upper_x, lower_y, upper_y = edge(x, 0, 8), edge(x, 1, 8), edge_rows(0, 32), edge_rows(1, 32)
        six = [
            0.5 * (v + lower_x * base[0, x, own_rows, :]),
            0.5 * (v + upper_x * base[0, x + 2, own_rows, :]),
            0.5 * (v + lower_y * base[0, x + 1, pl.ds(TOP - 1, 32), :]),
            0.5 * (v + upper_y * base[0, x + 1, pl.ds(TOP + 1, 32), :]),
            0.5 * (v + low_z),
            0.5 * (v + high_z),
        ]
        at = block(x, 32)
        for k in range(6):
            faces0[k, at, :] = six[k]
        masks = (lower_x, upper_x, lower_y, upper_y)
        for k in range(6):
            links0[k, at, :] = six[k] * masks[k] if k < 4 else jnp.where(lane32 == (0, 127)[k - 4], 0.0, six[k])
        rim_link[at, :] = jnp.where(lane32 == 0, six[4], jnp.where(lane32 == 127, six[5], 0.0))
        diag = six[0] + six[1] + six[2] + six[3] + six[4] + six[5]
        inv = 1.0 / diag
        diag0[at, :] = diag
        inv0[at, :] = inv
        p = base[1, x + 1, own_rows, :]
        _, high_p = shifted(p, rims[4:])
        grads = [
            base[1, x + 2, own_rows, :] * upper_x - p,
            base[1, x + 1, pl.ds(TOP + 1, 32), :] * upper_y - p,
            high_p - p,
        ]
        updates = []
        for c in range(3):
            right = load[c, x] - grads[c]
            res0[c, at, :] = right
            update = inv * right * FIRST
            buf0[1, c, x + 1, own_rows, :] = update
            updates.append(update)
        return pack(accs, updates, x)

    start = lax.fori_loop(0, 8, setup_plane, (zero8, zero8))

    def coarsen(level, fine, coarse):
        nx, ny, _ = LEVELS[level]
        half_x, half_y = nx // 2, ny // 2
        n = half_x * half_y

        def one(x, carry):
            for k in range(6):
                way, side = k // 2, k % 2
                if way == 0:
                    plane = fine[k, block(2 * x + side, ny), :]
                else:
                    plane = fine[k, block(2 * x, ny), :] + fine[k, block(2 * x + 1, ny), :]
                tmp[k, pl.ds(0, ny), :] = plane
            for k in range(6):
                way, side = k // 2, k % 2
                if way == 1:
                    both = tmp[k, pl.ds(side, half_y, 2), :]
                else:
                    both = tmp[k, pl.ds(0, half_y, 2), :] + tmp[k, pl.ds(1, half_y, 2), :]
                flat[k, block(x, half_y), :] = both
            return carry

        lax.fori_loop(0, half_x, one, 0)
        sums = times(flat[0:4, :n, :].reshape(4 * n, 128), pair).reshape(4, n, 128)
        for k in range(4):
            coarse[k] = sums[k]
        for k in range(4, 6):
            coarse[k] = times(flat[k, :n, :], pick[k - 4])

    def coefficients(level, faces, x):
        nx, ny, _ = LEVELS[level]
        six = [faces[k, pl.ds(x * ny, ny), :] for k in range(6)]
        total = six[0] + six[1] + six[2] + six[3] + six[4] + six[5]
        return [total, six[0] * edge(x, 0, nx), six[2] * edge_rows(0, ny), six[4]]

    def invert(coef, inv, planes):
        def one(x, carry):
            d = coef[0, x]
            inv[x] = jnp.where(d > 0.0, 1.0 / jnp.where(d > 0.0, d, 1.0), 0.0)
            return carry

        lax.fori_loop(0, planes, one, 0)

    side_lanes = (lane8 < 68) | (lane8 >= 124)

    def exchange1(use, ref, depth_up, depth_down):
        n = ref.shape[0]
        zlow = zhigh = zero8
        for x in range(4):
            for a in range(n):
                for g in range(2):
                    at = 4 * ((x * n + a) * 2 + g)
                    part = ref[a, 4 + x, pl.ds(16 + 8 * g, 8), :]
                    turned = pltpu.roll(part, at, 1) if at else part
                    zlow = jnp.where((lane8 >= at) & (lane8 < at + 4), turned, zlow)
                    top = (60 + at) % 128
                    zhigh = jnp.where((lane8 >= top) & (lane8 < top + 4), turned, zhigh)
        zsend1[use, 0] = zlow
        zsend1[use, 1] = zhigh
        copies = []
        for i, (a, b, c) in enumerate(near1):
            if c:
                src = zsend1.at[use, (c + 1) // 2]
                dst = zgot1.at[use, 1 - a, 1 - b, (1 - c) // 2]
            else:
                from_x, to_x, from_y, to_y = pl.ds(4, 4), pl.ds(4, 4), OWN1, OWN1
                if a == 1:
                    from_x, to_x = pl.ds(8 - depth_up, depth_up), pl.ds(4 - depth_up, depth_up)
                if a == -1:
                    from_x, to_x = pl.ds(4, depth_down), pl.ds(8, depth_down)
                if b == 1:
                    from_y, to_y = pl.ds(28, 4), pl.ds(12, 4)
                if b == -1:
                    from_y, to_y = pl.ds(16, 4), pl.ds(32, 4)
                src, dst = ref.at[:, from_x, from_y], ref.at[:, to_x, to_y]
            copy = remote(src, dst, dsend1.at[use, i], drecv1.at[use, i], device(a, b, c))
            copies.append((a, copy))

        def each(way, do):
            group = [copy for a, copy in copies if a == way]
            for copy in group:
                do(copy)

        for way, there in ((1, rad < 3), (-1, rad > 0)):
            pl.when(there)(lambda way=way: each(way, lambda copy: copy.start()))
        each(0, lambda copy: copy.start())

        def finish(low_plane, high_plane):
            for way, sends_it, gets_it in ((1, rad < 3, rad > 0), (-1, rad > 0, rad < 3)):
                pl.when(sends_it)(lambda way=way: each(way, lambda copy: copy.wait_send()))
                pl.when(gets_it)(lambda way=way: each(way, lambda copy: copy.wait_recv()))
            each(0, lambda copy: copy.wait())

            def one(plane, carry):
                dx, x = lax.div(plane, 4), lax.rem(plane, 4)
                back = lax.rem(192 - 8 * n * x, 128)
                for dy, groups in ((0, (1,)), (1, (2, 3)), (2, (4,))):
                    above = pltpu.roll(zgot1[use, dx, dy, 1], back, 1)
                    below = pltpu.roll(zgot1[use, dx, dy, 0], back, 1)
                    both = jnp.where((lane8 >= 64) & (lane8 < 96), above, below)
                    for a in range(n):
                        for group in groups:
                            g = (1, group - 2, 0)[dy]
                            at = (128 - 4 * (2 * a + g)) % 128
                            side = pltpu.roll(both, at, 1) if at else both
                            rows = pl.ds(8 * group, 8)
                            own = ref[a, plane, rows, :]
                            side = jnp.where(side_lanes, side, 0.0)
                            ref[a, plane, rows, :] = jnp.where(lane8 < 64, own, side)
                return carry

            lax.fori_loop(low_plane, high_plane, one, 0, unroll=2)

        return finish

    def layers1(use, ref, depth_up, depth_down):
        n = ref.shape[0]

        def go(copies):
            for start, _ in copies:
                start()

        def done(copies):
            for _, wait in copies:
                wait()

        def copy(i, src, dst, target):
            return remote(src, dst, csend1.at[use, i], crecv1.at[use, i], target)

        planes, zs = pl.ds(0, 12), cz.at[use]
        up_x, down_x = (pl.ds(8 - depth_up, depth_up), pl.ds(4 - depth_up, depth_up)), (pl.ds(4, depth_down), pl.ds(8, depth_down))
        in_x = [
            guarded(copy(0, ref.at[:, up_x[0], OWN1], ref.at[:, up_x[1], OWN1], up[0]), 1),
            guarded(copy(1, ref.at[:, down_x[0], OWN1], ref.at[:, down_x[1], OWN1], down[0]), -1),
        ]
        in_y = [
            plain(copy(2, ref.at[:, planes, pl.ds(28, 4)], ref.at[:, planes, pl.ds(12, 4)], up[1])),
            plain(copy(3, ref.at[:, planes, pl.ds(16, 4)], ref.at[:, planes, pl.ds(32, 4)], down[1])),
        ]
        in_z = [
            plain(copy(4, zs.at[1], zs.at[2], up[2])),
            plain(copy(5, zs.at[0], zs.at[3], down[2])),
        ]
        parts = [(s, a, g) for s in range(2) for a in range(n) for g in range(4)]

        def pack_pair(t, carry):
            zlow = zhigh = zero8
            for j, (s, a, g) in enumerate(parts):
                part = ref[a, 2 * t + s, pl.ds(8 + 8 * g, 8), :]
                turned = pltpu.roll(part, 4 * j, 1) if j else part
                zlow = jnp.where((lane8 >= 4 * j) & (lane8 < 4 * j + 4), turned, zlow)
                top = (60 + 4 * j) % 128
                zhigh = jnp.where((lane8 >= top) & (lane8 < top + 4), turned, zhigh)
            zs[0, t] = zlow
            zs[1, t] = zhigh
            return carry

        def unpack_pair(t, carry):
            below, above = zs[2, t], zs[3, t]
            for m in range(n):
                turn_by = (192 - 32 * m) % 128
                high = pltpu.roll(above, turn_by, 1) if turn_by else above
                low = pltpu.roll(below, turn_by, 1) if turn_by else below
                both = jnp.where((lane8 >= 64) & (lane8 < 96), high, low)
                for j in range(8):
                    s, a, g = parts[8 * m + j]
                    side = pltpu.roll(both, 128 - 4 * j, 1) if j else both
                    rows = pl.ds(8 + 8 * g, 8)
                    own = ref[a, 2 * t + s, rows, :]
                    side = jnp.where(side_lanes, side, 0.0)
                    ref[a, 2 * t + s, rows, :] = jnp.where(lane8 < 64, own, side)
            return carry

        def first():
            go(in_x)

        def second():
            done(in_x)
            go(in_y)

        def third():
            done(in_y)
            lax.fori_loop(0, 6, pack_pair, 0)
            go(in_z)

        def last():
            done(in_z)
            lax.fori_loop(0, 6, unpack_pair, 0)

        return first, second, third, last

    def spread_coef2(tiles):
        ref = dgot2.at[0]
        for i, t in enumerate(tiles):
            ref[rad, 1, 1, i] = t

        def copy(i, src, dst, target):
            return remote(src, dst, csend2.at[i], crecv2.at[i], target)

        steps = [
            [copy(i, ref.at[rad, 1, 1], ref.at[rad, 1, 1], target) for i, target in enumerate(through)],
            [
                copy(3, ref.at[:, 1, 1], ref.at[:, 0, 1], up[1]),
                copy(4, ref.at[:, 1, 1], ref.at[:, 2, 1], down[1]),
            ],
            [
                copy(5, ref.at[:, :, 1], ref.at[:, :, 0], up[2]),
                copy(6, ref.at[:, :, 1], ref.at[:, :, 2], down[2]),
            ],
        ]

        def go(i):
            if i:
                for c in steps[i - 1]:
                    c.wait()
            if i < 3:
                for c in steps[i]:
                    c.start()

        return go

    def exchange2(use, tiles):
        n = len(tiles)
        for i, t in enumerate(tiles):
            dgot2[use, rad, 1, 1, i] = t
        copies = []
        for i, (a, b, c) in enumerate(near2):
            src = dgot2.at[use, rad, 1, 1, pl.ds(0, n)]
            dst = dgot2.at[use, rad, 1 - b, 1 - c, pl.ds(0, n)]
            copies.append(remote(src, dst, dsend2.at[i], drecv2.at[i], device(a, b, c)))
        for copy in copies:
            copy.start()

        def finish():
            for copy in copies:
                copy.wait()

        return finish

    def packed2(parts):
        tiles = []
        for i in range(0, len(parts), 4):
            out = zero8
            for j, part in enumerate(parts[i : i + 4]):
                part = pltpu.roll(part, 32 * j, 1) if j else part
                out = jnp.where((lane8 >= 32 * j) & (lane8 < 32 * j + 32), part, out)
            tiles.append(out)
        return tiles

    def turned2(use, source, dy, dz, tile_at, lanes):
        t = dgot2[use, source, dy, dz, tile_at]
        return pltpu.roll(t, lanes % 128, 1) if lanes % 128 else t

    def joined2(use, source, dy, part):
        i, at = part // 4, 32 * (part % 4)
        own = turned2(use, source, dy, 1, i, -at)
        after = turned2(use, source, dy, 2, i, 32 - at)
        before = turned2(use, source, dy, 0, i, 96 - at)
        out = jnp.where(lane8 < 32, own, jnp.where(lane8 < 64, after, before))
        return jnp.where((lane8 < 64) | (lane8 >= 96), out, 0.0)

    def unpack2(use, ref):
        n = ref.shape[0]

        def one(source, carry):
            for a in range(n):
                for x in range(2):
                    for dy in range(3):
                        ref[a, 2 + 2 * source + x, pl.ds(8 + 8 * dy, 8), :] = joined2(use, source, dy, 2 * a + x)
            return carry

        lax.fori_loop(0, 4, one, 0)

    coefs, invs = (None, coef1, coef2), (None, inv1, inv2)
    deeps, sols = (None, deep1, deep2), (None, sol1, sol2)

    def begin_deep(level, res, planes, keep):
        rows = pl.ds(8, DEEP_ROWS[level] - 16)

        def one(x, carry):
            for c in range(3):
                update = FIRST * invs[level][x, rows, :] * res[c, x, rows, :]
                deeps[level][0, c, x, rows, :] = update
                sols[level][c, x, rows, :] = update
            return carry

        lax.fori_loop(planes[0], planes[1], one, 0, unroll=2)

    def sweep_deep(level, p, res, out, planes, step, initial=False, rows=None):
        coef, inv, deep, sol = coefs[level], invs[level], deeps[level], sols[level]
        first, count = (8, DEEP_ROWS[level] - 16) if rows is None else rows
        here, under, over = pl.ds(first, count), pl.ds(first - 1, count), pl.ds(first + 1, count)

        def one(x, carry):
            diag, lower_x, upper_x = coef[0, x, here, :], coef[1, x, here, :], coef[1, x + 1, here, :]
            lower_y, upper_y, lower_z = coef[2, x, here, :], coef[2, x, over, :], coef[3, x, here, :]
            upper_z = pltpu.roll(lower_z, 127, 1)
            for c in range(3):
                v = deep[p, c, x, here, :]
                total = diag * v - lower_x * deep[p, c, x - 1, here, :] - upper_x * deep[p, c, x + 1, here, :]
                total = total - lower_y * deep[p, c, x, under, :] - upper_y * deep[p, c, x, over, :]
                total = total - lower_z * pltpu.roll(v, 1, 1) - upper_z * pltpu.roll(v, 127, 1)
                r = res[c, x, here, :] - total
                out[c, x, here, :] = r
                if step is None:
                    continue
                if initial:
                    update = FIRST * inv[x, here, :] * r
                    sol[c, x, here, :] = sol[c, x, here, :] + v + update
                else:
                    update = step[0] * v + step[1] * inv[x, here, :] * r
                    sol[c, x, here, :] = sol[c, x, here, :] + update
                deep[1 - p, c, x, here, :] = update
            return carry

        lax.fori_loop(planes[0], planes[1], one, 0, unroll=2)

    def inside(p, first=False):
        def plane(x, carry):
            at = block(x, 32)
            diag = diag0[at, :]
            ls = [links0[k, at, :] for k in range(6)]
            for c in range(3):
                v = buf0[p, c, x + 1, own_rows, :]
                total = diag * v - ls[0] * buf0[p, c, x, own_rows, :]
                total = total - ls[1] * buf0[p, c, x + 2, own_rows, :]
                total = total - ls[2] * buf0[p, c, x + 1, pl.ds(TOP - 1, 32), :]
                total = total - ls[3] * buf0[p, c, x + 1, pl.ds(TOP + 1, 32), :]
                total = total - ls[4] * pltpu.roll(v, 1, 1) - ls[5] * pltpu.roll(v, 127, 1)
                res0[c, at, :] = res0[c, at, :] - total
                sol0[c, at, :] = v if first else sol0[c, at, :] + v
            return carry

        lax.fori_loop(0, 8, plane, 0, unroll=2)

    def rim_terms(p, halo, step, emit=None):
        for side, rows in ((0, pl.ds(0, 32)), (1, pl.ds(224, 32))):
            link = links0[side, rows, :]
            for c in range(3):
                res0[c, rows, :] = res0[c, rows, :] + link * halo_x[p, side, c]

        def plane(x, accs):
            at = block(x, 32)
            inv, rim = inv0[at, :], rim_link[at, :]
            low_y, high_y = links0[2, block(4 * x, 8), :], links0[3, block(4 * x + 3, 8), :]
            rims = rims_of(halo, 12, x)
            packs = []
            for c in range(3):
                r = res0[c, at, :] + rim * jnp.concatenate(rims[4 * c : 4 * c + 4], 0)
                top = r[0:8] + low_y * halo_y[p, 0, c, x]
                bottom = r[24:32] + high_y * halo_y[p, 1, c, x]
                r = jnp.concatenate([top, r[8:24], bottom], 0)
                if emit is None:
                    res0[c, at, :] = r
                if step is None:
                    continue
                update = step[0] * buf0[p, c, x + 1, own_rows, :] + step[1] * inv * r
                if emit is None:
                    buf0[1 - p, c, x + 1, own_rows, :] = update
                    packs.append(update)
                else:
                    packs.append(sol0[c, at, :] + update)
            if step is None:
                return accs
            if emit is not None:
                emit(packs, x)
            return pack(accs, packs, x)

        return lax.fori_loop(0, 8, plane, (zero8, zero8), unroll=2)

    def correct(p):
        def plane(x, accs):
            at = block(x, 32)
            diag, inv = diag0[at, :], inv0[at, :]
            ls = [links0[k, at, :] for k in range(6)]
            packs = []
            for c in range(3):
                v = wide0[c, x + 1, own_rows, :]
                total = diag * v - ls[0] * wide0[c, x, own_rows, :]
                total = total - ls[1] * wide0[c, x + 2, own_rows, :]
                total = total - ls[2] * wide0[c, x + 1, pl.ds(TOP - 1, 32), :]
                total = total - ls[3] * wide0[c, x + 1, pl.ds(TOP + 1, 32), :]
                total = total - ls[4] * pltpu.roll(v, 1, 1) - ls[5] * pltpu.roll(v, 127, 1)
                r = res0[c, at, :] - total + rim_link[at, :] * rim0[c, x]
                res0[c, at, :] = r
                sol0[c, at, :] = sol0[c, at, :] + v
                update = FIRST * inv * r
                buf0[p, c, x + 1, own_rows, :] = update
                packs.append(update)
            return pack(accs, packs, x)

        return lax.fori_loop(0, 8, plane, (zero8, zero8), unroll=2)

    def restrict(source, rows, level, matrix):
        nx, ny, _ = LEVELS[level]
        half_x, half_y = nx // 2, ny // 2
        n = half_x * half_y

        def one(x, carry):
            for c in range(3):
                tmp[c, pl.ds(0, ny), :] = source(c, 2 * x) + source(c, 2 * x + 1)
            for c in range(3):
                flat[c, block(x, half_y), :] = tmp[c, pl.ds(0, half_y, 2), :] + tmp[c, pl.ds(1, half_y, 2), :]
            return carry

        lax.fori_loop(0, half_x, one, 0)
        return times(flat[0:3, :n, :].reshape(3 * n, 128), matrix)

    def gather(use):
        first = [
            remote(tile.at[use, 0], got1.at[use, lon], send1.at[use, i], recv1.at[use, i], target)
            for i, target in enumerate(along)
        ]
        second = [
            remote(tile.at[use, 1], got2.at[use, block(lat, 8)], send2.at[use, i], recv2.at[use, i], target)
            for i, target in enumerate(across)
        ]

        def begin(value):
            tile[use, 0] = value
            got1[use, lon] = value
            for copy in first:
                copy.start()

        def middle():
            for copy in first:
                copy.wait()
            total = got1[use, 0]
            for k in range(1, 8):
                total = total + got1[use, k]
            tile[use, 1] = total
            got2[use, block(lat, 8), :] = total
            for copy in second:
                copy.start()

        def end():
            for copy in second:
                copy.wait()

        return begin, middle, end

    lane1 = lanes_of((1, 128))
    runs = jnp.bitwise_and(owner[0, 0:1, :], 31)
    runs = jnp.concatenate([runs, jnp.full((1, 96), -1, jnp.int32)], 1)

    def member_of(columns):
        return (grid_row == jnp.broadcast_to(columns, (128, 128))).astype(F32)

    own_member = member_of(runs)

    def to_runs(rows):
        return lax.dot_general(
            rows, own_member, (((1,), (1,)), ((), ())), precision=HI, preferred_element_type=F32
        )

    def stacked(rows, count=8):
        out = jnp.zeros((count, 128), F32)
        at = rows_of((count, 128))
        for i, row in enumerate(rows):
            out = jnp.where(at == i, jnp.broadcast_to(row, (count, 128)), out)
        return out

    def rowsum(plane):
        return jnp.sum(plane, axis=0, keepdims=True)

    def run_sides():
        f = faces2
        wide = jnp.broadcast_to(runs, (8, 128))
        first_cell = (lane1 == 0) | (runs != pltpu.roll(wide, 1, 1)[0:1])
        last_cell = (lane1 == 31) | (runs != pltpu.roll(wide, 127, 1)[0:1])
        sides = [
            rowsum(f[0, 0:8, :]),
            rowsum(f[1, 8:16, :]),
            f[2, 0:1, :] + f[2, 8:9, :],
            f[3, 7:8, :] + f[3, 15:16, :],
            jnp.where(first_cell, rowsum(f[4, 0:8, :] + f[4, 8:16, :]), 0.0),
            jnp.where(last_cell, rowsum(f[5, 0:8, :] + f[5, 8:16, :]), 0.0),
        ]
        whole = sides[0] + sides[1] + sides[2] + sides[3] + sides[4] + sides[5]
        return to_runs(stacked([sides[0], sides[2], sides[4], whole]))

    def coarse_solve(meanwhile):
        begin, middle, end = gather(0)
        rows = []
        for block_x in range(4):
            for c in range(3):
                both = right2[c, 2 + 2 * block_x, OWN2, :] + right2[c, 3 + 2 * block_x, OWN2, :]
                rows.append(rowsum(both))
        sums = to_runs(stacked(rows, 16))
        row8 = rows_of((8, 128))
        value = zero8
        for block_x in range(4):
            part = jnp.where(row8 < 3, 0.0, pltpu.roll(dgot2[0, block_x, 1, 1, 2], 2, 0))
            for c in range(3):
                row = jnp.broadcast_to(sums[3 * block_x + c : 3 * block_x + c + 1], (8, 128))
                part = jnp.where(row8 == c, row, part)
            value = value + (pltpu.roll(part, 32 * block_x, 1) if block_x else part)
        begin(value)
        meanwhile[0]()
        middle()
        meanwhile[1]()
        end()

        def all_of(i):
            return got2[0, pl.ds(i, 8, 8), :]

        wrap = jnp.bitwise_and(lane8, 31)

        def lower_z(v):
            return jnp.where(wrap == 0, pltpu.roll(v, 97, 1), pltpu.roll(v, 1, 1))

        def upper_z(v):
            return jnp.where(wrap == 31, pltpu.roll(v, 31, 1), pltpu.roll(v, 127, 1))

        link_x = jnp.where(lane8 < 32, 0.0, all_of(3))
        link_y = jnp.where(row8 == 0, 0.0, all_of(4))
        link_z = all_of(5)
        link_xu, link_yu, link_zu = pltpu.roll(link_x, 96, 1), pltpu.roll(link_y, 7, 0), upper_z(link_z)
        diagonal = all_of(6)
        inverse = 1.0 / diagonal

        def operate(v):
            out = diagonal * v - link_x * pltpu.roll(v, 32, 1) - link_xu * pltpu.roll(v, 96, 1)
            out = out - link_y * pltpu.roll(v, 1, 0) - link_yu * pltpu.roll(v, 7, 0)
            return out - link_z * lower_z(v) - link_zu * upper_z(v)

        rs = [all_of(c) for c in range(3)]
        ds = [inverse * r * COARSE_FIRST for r in rs]
        es = list(ds)
        for a, b in COARSE_STEPS:
            rs = [r - operate(d) for r, d in zip(rs, ds)]
            ds = [a * d + b * inverse * r for r, d in zip(rs, ds)]
            es = [e + d for e, d in zip(es, ds)]
        for c in range(3):
            erows[c] = es[c]
        lats = [lax.rem(lat + 7, 8), lat, lax.rem(lat + 1, 8)]
        rows = [erows[c, pl.ds(at, 1), :] for c in range(3) for at in lats]
        rows = stacked(rows, 16)
        rows = [rows if k == 0 else pltpu.roll(rows, 128 - 32 * k, 1) for k in range(4)]
        spans = times(jnp.concatenate(rows, 0), region_member())
        for block_x in range(4):
            for c in range(3):
                for dy in range(3):
                    i = 16 * block_x + 3 * c + dy
                    row = jnp.broadcast_to(spans[i : i + 1], (8, 128))
                    for x in range(2):
                        deep2[1, c, 2 + 2 * block_x + x, pl.ds(8 + 8 * dy, 8), :] = row

    def region_member():
        own, before, after = (turned2(0, rad, 1, k, 2, t)[0:1] for k, t in ((1, 0), (0, 96), (2, 32)))
        columns = jnp.where(lane1 < 32, own, jnp.where(lane1 < 64, after, before))
        columns = jnp.where((lane1 < 64) | (lane1 >= 96), columns, -1.0).astype(jnp.int32)
        return member_of(columns)

    pending = {}

    def while_first():
        coarsen(0, faces0, faces1)
        for x in range(4):
            for k, value in enumerate(coefficients(1, faces1, x)):
                coef1[k, 4 + x, OWN1, :] = value
        pending["coef1"] = layers1(0, coef1, 3, 4)
        pending["coef1"][0]()

    def while_second():
        pending["coef1"][1]()
        coarsen(1, faces1, faces2)
        values = [coefficients(2, faces2, x) for x in range(2)]
        last = jnp.where(rows_of((8, 128)) == 0, runs.astype(F32), pltpu.roll(run_sides(), 1, 0))
        parts = packed2([values[x][k] for k in range(4) for x in range(2)])
        pending["coef2"] = spread_coef2(parts + [last])
        pending["coef2"](0)

    def weigh_all():
        def weigh(x, accs):
            v, inv = base[0, x + 1, own_rows, :], inv0[block(x, 32), :]
            parts = [2.0 * inv * (v - faces0[2 * c + 1, block(x, 32), :]) for c in range(3)]
            for c in range(3):
                hbuf[c, x + 1, own_rows, :] = parts[c]
            return pack(accs, parts, x)

        accs = lax.fori_loop(0, 8, weigh, (zero8, zero8), unroll=2)
        pending["h"] = send_all(accs, hbuf, hz, hsend, hrecv)

    def applied_to(buf, halo, x):
        at = block(x, 32)
        rims = rims_of(halo, 12, x)
        out = []
        for c in range(3):
            v = buf[c, x + 1, own_rows, :]
            total = diag0[at, :] * v - links0[0, at, :] * buf[c, x, own_rows, :]
            total = total - links0[1, at, :] * buf[c, x + 2, own_rows, :]
            total = total - links0[2, at, :] * buf[c, x + 1, pl.ds(TOP - 1, 32), :]
            total = total - links0[3, at, :] * buf[c, x + 1, pl.ds(TOP + 1, 32), :]
            total = total - links0[4, at, :] * pltpu.roll(v, 1, 1) - links0[5, at, :] * pltpu.roll(v, 127, 1)
            out.append(total - rim_link[at, :] * jnp.concatenate(rims[4 * c : 4 * c + 4], 0))
        return out

    def apply_to_h():
        halo = pending["h"]()

        def one(x, accs):
            at = block(x, 32)
            v, inv = base[0, x + 1, own_rows, :], inv0[at, :]
            parts = []
            for c, g in enumerate(applied_to(hbuf, halo, x)):
                u = (1.0 + STEPS[1][0]) * 2.0 * (v - faces0[2 * c + 1, at, :]) - STEPS[1][1] * g
                applied[c, at, :] = u
                m = STEPS[0][1] * inv * u + STEPS[1][1] * hbuf[c, x + 1, own_rows, :]
                mbuf[c, x + 1, own_rows, :] = m
                parts.append(m)
            return pack(accs, parts, x)

        accs = lax.fori_loop(0, 8, one, (zero8, zero8), unroll=2)
        pending["m"] = send_all(accs, mbuf, mz, msend, mrecv)

    def apply_to_m():
        halo = pending["m"]()

        def one(x, carry):
            at = block(x, 32)
            for c, g in enumerate(applied_to(mbuf, halo, x)):
                applied[c, at, :] = STEPS[0][0] * applied[c, at, :] - g
            return carry

        lax.fori_loop(0, 8, one, 0, unroll=2)

    def while_third():
        pending["coef1"][2]()
        pending["coef2"](1)

    accs = start
    for step, meanwhile in ((STEPS[0], while_first), (STEPS[1], while_second), (None, while_third)):
        p = turn[0] % 2
        finish = exchange(accs)
        inside(p, meanwhile is while_first)
        meanwhile()
        accs = rim_terms(p, finish(), step)

    sums = restrict(lambda c, x: res0[c, block(x, 32), :], 32, 0, pair)
    for c in range(3):
        for x in range(4):
            right1[c, 4 + x, OWN1, :] = sums[64 * c + 16 * x : 64 * c + 16 * x + 16]
    finish = exchange1(0, right1, 3, 3)
    pending["coef1"][3]()
    invert(coef1, inv1, 12)
    pending["coef2"](2)
    weigh_all()
    finish(1, 11)
    begin_deep(1, right1, (1, 11), None)
    sweep_deep(1, 0, right1, right1, (2, 10), STEPS[0])
    sweep_deep(1, 1, right1, right1, (3, 9), STEPS[1])
    sweep_deep(1, 0, right1, left1, (4, 8), None, rows=(16, 16))

    sums = restrict(lambda c, x: left1[c, 4 + x, OWN1, :], 16, 1, own_pair)
    finish2 = exchange2(1, packed2([sums[16 * c + 8 * x : 16 * c + 8 * x + 8] for c in range(3) for x in range(2)]))
    rest = layers1(1, left1, 3, 3)
    rest[0]()
    pending["coef2"](3)
    unpack2(0, coef2)
    invert(coef2, inv2, 12)
    apply_to_h()
    rest[1]()
    finish2()
    unpack2(1, right2)
    all2 = (2, 10)
    begin_deep(2, right2, all2, None)
    sweep_deep(2, 0, right2, right2, all2, STEPS[0])
    sweep_deep(2, 1, right2, right2, all2, STEPS[1])
    sweep_deep(2, 0, right2, right2, all2, None)

    def while_along():
        rest[2]()
        apply_to_m()

    coarse_solve((while_along, rest[3]))
    sweep_deep(2, 1, right2, right2, all2, STEPS[0], initial=True)
    sweep_deep(2, 0, right2, right2, all2, STEPS[0])
    sweep_deep(2, 1, right2, right2, all2, STEPS[1])

    def gather_rows(k, carry):
        for c in range(3):
            flat[c, block(k, 16), :] = sol2[c, 2 * rad + k, pl.ds(12, 16), :]
        return carry

    lax.fori_loop(0, 6, gather_rows, 0)
    for c in range(3):
        flat[c, 0:96, :] = times(flat[c, 0:96, :], spread1)

    def to_level1(k, carry):
        for c in range(3):
            value = flat[c, block(k, 16), :]
            for s in range(2):
                for t in range(2):
                    deep1[1, c, 2 * k + s, pl.ds(8 + t, 16, 2), :] = value
        return carry

    lax.fori_loop(0, 6, to_level1, 0)
    sweep_deep(1, 1, left1, left1, (1, 11), STEPS[0], initial=True)
    sweep_deep(1, 0, left1, left1, (2, 10), STEPS[0])
    sweep_deep(1, 1, left1, left1, (3, 9), STEPS[1])

    for c in range(3):
        flat[c] = times(sol1[c, 3:9, 12:36, :].reshape(144, 128), spread0)

    for k in range(6):
        for c in range(3):
            value = flat[c, 24 * k : 24 * k + 24, :]
            tmp[c, pl.ds(0, 24, 2), :] = value
            tmp[c, pl.ds(1, 24, 2), :] = value
            if 1 <= k <= 4:
                coarse = sol1[c, 3 + k, OWN1, :]
                rim = jnp.where(lane16 == 0, pltpu.roll(coarse, 1, 1), pltpu.roll(coarse, 63, 1))
                tmp[3 + c, pl.ds(0, 16, 2), :] = rim
                tmp[3 + c, pl.ds(1, 16, 2), :] = rim
        for c in range(3):
            for at in (2 * k - 1, 2 * k):
                if 0 <= at <= 9:
                    wide0[c, at] = tmp[c, pl.ds(0, 48), :]
                if 1 <= at <= 8:
                    rim0[c, at - 1] = tmp[3 + c, pl.ds(0, 32), :]

    p = turn[0] % 2
    accs = correct(p)
    finish = exchange(accs)

    def add_up(x, total):
        at = block(x, 32)
        v = base[0, x + 1, own_rows, :]
        part = base[1, x + 1, own_rows, :]
        for c in range(3):
            update = buf0[p, c, x + 1, own_rows, :]
            part = part - 2.0 * (v - faces0[2 * c + 1, at, :]) * (sol0[c, at, :] + update)
            part = part - mbuf[c, x + 1, own_rows, :] * res0[c, at, :] - applied[c, at, :] * update
        return total + (part[0:8] + part[8:16] + part[16:24] + part[24:32])

    partial = lax.fori_loop(0, 8, add_up, zero8, unroll=2)
    rounds = []
    for i, (got, at, targets) in enumerate(((sum_x, rad, through), (sum_y, lat, across), (sum_z, lon, along))):
        copies = [
            remote(summed.at[i], got.at[at], sum_send.at[i, k], sum_recv.at[i, k], target)
            for k, target in enumerate(targets)
        ]
        rounds.append((got, at, copies))

    def send_sum(i, value):
        got, at, copies = rounds[i]
        summed[i] = value
        got[at] = value
        for copy in copies:
            copy.start()

    def get_sum(i):
        got, _, copies = rounds[i]
        for copy in copies:
            copy.wait()
        total = got[0]
        for k in range(1, len(copies) + 1):
            total = total + got[k]
        return total

    send_sum(0, partial)
    inside(p)
    accs = rim_terms(p, finish(), STEPS[0])
    p = turn[0] % 2
    finish = exchange(accs)
    inside(p)
    send_sum(1, get_sum(0))

    def emit(afters, x):
        for c, after in enumerate(afters):
            adjoint[c, x] = after
            wide0[c, x + 1, own_rows, :] = after

    accs = rim_terms(p, finish(), STEPS[1], emit=emit)

    finish = exchange(accs, wide0)
    send_sum(2, get_sum(1))
    for _, wait in fwd_copies:
        wait()
    halo = finish()
    fwd_halo = merged(zero8, fwd_z[1])

    def outputs(x, carry):
        v = base[0, x + 1, own_rows, :]
        keep_x, keep_y = edge(x, 1, 8), edge_rows(1, 32)
        ga, gf = [], []
        us = []
        rims, fwd_rims = rims_of(halo, 12, x), rims_of(fwd_halo, 12, x)
        for c in range(3):
            u = wide0[c, x + 1, own_rows, :]
            low_z, high_z = shifted(u, rims[4 * c : 4 * c + 4])
            ga.append([
                wide0[c, x + 2, own_rows, :] * keep_x - u,
                wide0[c, x + 1, pl.ds(TOP + 1, 32), :] * keep_y - u,
                high_z - u,
            ])
            us.append((u, low_z))
            w = fwd[c, x + 1, own_rows, :]
            _, high_w = shifted(w, fwd_rims[4 * c : 4 * c + 4])
            gf.append([
                fwd[c, x + 2, own_rows, :] * keep_x - w,
                fwd[c, x + 1, pl.ds(TOP + 1, 32), :] * keep_y - w,
                high_w - w,
            ])
        divergence = (
            us[0][0] - edge(x, 0, 8) * wide0[0, x, own_rows, :]
            + (us[1][0] - edge_rows(0, 32) * wide0[1, x + 1, pl.ds(TOP - 1, 32), :])
            + (us[2][0] - us[2][1])
        )
        pnext[x] = base[1, x + 1, own_rows, :] - v * divergence
        summed = gf[0][0] * ga[0][0] + gf[1][1] * ga[1][1] + gf[2][2] * ga[2][2]
        for d, e in ((0, 1), (0, 2), (1, 2)):
            summed = summed + 0.5 * (gf[e][d] + gf[d][e]) * (ga[e][d] + ga[d][e])
        gradient[x] = 2.0 * v * summed
        return carry

    lax.fori_loop(0, 8, outputs, 0, unroll=2)
    mean = jnp.sum(get_sum(2)) / CELLS

    def shift(x, carry):
        pnext[x] = pnext[x] - mean
        return carry

    lax.fori_loop(0, 8, shift, 0)


def per_device(forcing, pressure, viscosity, forward, owner):
    vmem, anywhere = pl.BlockSpec(memory_space=pltpu.VMEM), pl.BlockSpec(memory_space=pl.ANY)
    f32 = lambda *shape: pltpu.VMEM(shape, F32)
    dma = lambda *shape: pltpu.SemaphoreType.DMA(shape)
    return pl.pallas_call(
        kernel,
        out_shape=(
            jax.ShapeDtypeStruct((3, 8, 32, 128), F32),
            jax.ShapeDtypeStruct((8, 32, 128), F32),
            jax.ShapeDtypeStruct((8, 32, 128), F32),
        ),
        in_specs=[anywhere] * 4 + [vmem],
        out_specs=(vmem, vmem, vmem),
        scratch_shapes=[
            f32(3, 8, 32, 128), f32(2, 10, 48, 128), f32(3, 10, 48, 128), f32(1, 8, 128), f32(2, 8, 128),
            f32(2, 3, 10, 48, 128), f32(2, 4, 8, 128), f32(6, 256, 128), f32(6, 64, 128), f32(6, 16, 128),
            f32(6, 256, 128), f32(256, 128), f32(256, 128), f32(3, 256, 128), f32(3, 256, 128), f32(3, 8, 32, 128),
            f32(3, 10, 48, 128), f32(4, 8, 128), f32(3, 256, 128), f32(3, 10, 48, 128), f32(4, 8, 128),
            f32(3, 10, 48, 128), f32(256, 128), f32(2, 2, 3, 32, 128), f32(2, 2, 3, 8, 8, 128),
            f32(4, 13, 48, 128), f32(4, 12, 40, 128), f32(12, 48, 128), f32(12, 40, 128),
            f32(3, 12, 48, 128), f32(3, 12, 48, 128), f32(3, 12, 40, 128),
            f32(2, 3, 12, 48, 128), f32(2, 3, 12, 40, 128), f32(3, 12, 48, 128), f32(3, 12, 40, 128),
            f32(1, 2, 8, 128), f32(1, 3, 3, 2, 8, 128), f32(2, 4, 6, 8, 128), f32(2, 4, 3, 3, 3, 8, 128),
            f32(6, 48, 128), f32(6, 144, 128), f32(3, 8, 128), f32(1, 2, 8, 128),
            f32(1, 8, 8, 128), f32(1, 64, 128), f32(3, 8, 128), f32(4, 8, 128), f32(8, 8, 128), f32(8, 8, 128),
            dma(4), dma(2, 6), dma(2, 6), dma(3), dma(3), dma(1, 7), dma(1, 7), dma(1, 7), dma(1, 7), dma(3, 7), dma(3, 7),
            dma(1, 26), dma(1, 26), dma(35), dma(35), dma(6), dma(6), dma(6), dma(6), dma(2, 6), dma(2, 6), dma(7), dma(7),
        ],
        compiler_params=pltpu.CompilerParams(
            collective_id=0, has_side_effects=True, vmem_limit_bytes=60 * 1024 * 1024
        ),
    )(forcing, pressure, viscosity, forward, owner)


def solution(mesh):
    placed = (
        P(None, "rad", "lat", "lon"),
        P("rad", "lat", "lon"),
        P("rad", "lat", "lon"),
        P(None, "rad", "lat", "lon"),
        P("rad", "lat", "lon"),
    )
    return jax.shard_map(
        per_device,
        mesh=mesh,
        in_specs=placed,
        out_specs=(P(None, "rad", "lat", "lon"), P("rad", "lat", "lon"), P("rad", "lat", "lon")),
        check_vma=False,
    )
```

```python
import jax
import jax.numpy as jnp
from jax import lax
from jax.experimental import pallas as pl
from jax.experimental.pallas import tpu as pltpu
from jax.sharding import PartitionSpec as P

AXES = ("rad", "lat", "lon")
SIZES = (4, 8, 8)
MESH = pl.DeviceIdType.MESH
F32 = jnp.float32
HI = lax.Precision.HIGHEST
CDEG = 8
CELLS = 32 * 256 * 1024
LEVELS = ((8, 32, 128), (4, 16, 64), (2, 8, 32))
TOP = 8
DEEP_ROWS = {1: 48, 2: 40}
OWN1, OWN2 = pl.ds(16, 16), pl.ds(16, 8)


def cheb_constants(low, high, degree):
    middle, spread = 0.5 * (high + low), 0.5 * (high - low)
    factor = middle / spread
    old = 1.0 / factor
    steps = []
    for _ in range(degree - 1):
        new = 1.0 / (2.0 * factor - old)
        steps.append((new * old, 2.0 * new / spread))
        old = new
    return 1.0 / middle, steps


FIRST, STEPS = cheb_constants(0.5, 2.0, 3)
COARSE_FIRST, COARSE_STEPS = cheb_constants(0.1, 2.0, CDEG)


def lanes_of(shape):
    return lax.broadcasted_iota(jnp.int32, shape, len(shape) - 1)


def rows_of(shape):
    return lax.broadcasted_iota(jnp.int32, shape, len(shape) - 2)


def block(x, rows):
    return pl.ds(pl.multiple_of(x * rows, 8), rows)


def kernel(
    forcing, pressure, viscosity, forward, owner,
    adjoint, pnext, gradient,
    load, base, fwd, base_z, fwd_z,
    buf0, zbuf, faces0, faces1, faces2, links0, diag0, inv0, res0, sol0, rim0, hbuf, hz, applied, mbuf, mz,
    wide0, rim_link, halo_x, halo_y, strain,
    coef1, coef2, inv1, inv2, right1, mid1, left1, right2, deep1, deep2, sol1, sol2,
    zsend1, zgot1, cz, dgot2,
    tmp, flat, erows, tile, got1, got2, summed, sum_x, sum_y, sum_z,
    in_sem, send_sem, recv_sem, fsend, frecv, send1, recv1, send2, recv2, sum_send, sum_recv,
    dsend1, drecv1, dsend2, drecv2, hsend, hrecv, msend, mrecv, csend1, crecv1, csend2, crecv2,
):
    me = tuple(lax.axis_index(a) for a in AXES)
    rad, lat, lon = me

    def device(*steps):
        return tuple(
            lax.rem(m + (s % n), n) if s % n else m for m, s, n in zip(me, steps, SIZES)
        )

    up = [device(1, 0, 0), device(0, 1, 0), device(0, 0, 1)]
    down = [device(-1, 0, 0), device(0, -1, 0), device(0, 0, -1)]
    along = [device(0, 0, k) for k in (4, 3, 5, 2, 6, 1, 7)]
    across = [device(0, k, 0) for k in (4, 3, 5, 2, 6, 1, 7)]
    through = [device(k, 0, 0) for k in range(1, 4)]
    near1 = [
        (a, b, c) for c in (1, -1, 0) for b in (1, -1, 0) for a in (1, -1, 0) if a or b or c
    ]
    near2 = [
        (a, b, c) for c in (1, -1, 0) for a in (2, 1, 3, 0) for b in (1, -1, 0) if a or b or c
    ]
    peers = up + down

    own_rows = pl.ds(TOP, 32)
    loads = [
        pltpu.make_async_copy(viscosity, base.at[0, pl.ds(1, 8), own_rows], in_sem.at[0]),
        pltpu.make_async_copy(pressure, base.at[1, pl.ds(1, 8), own_rows], in_sem.at[1]),
        pltpu.make_async_copy(forcing, load, in_sem.at[2]),
        pltpu.make_async_copy(forward, fwd.at[:, pl.ds(1, 8), own_rows], in_sem.at[3]),
    ]
    for copy in loads:
        copy.start()

    def clear(ref, *at):
        ref[at] = jnp.zeros(ref[at].shape, F32)

    every, low_rows, high_rows = slice(None), slice(8, 16), slice(32, 40)
    for plane in (0, 9):
        clear(base, every, plane, slice(8, 40))
        clear(fwd, every, plane, slice(8, 40))

    barrier = pltpu.get_barrier_semaphore()
    for target in peers:
        pl.semaphore_signal(barrier, inc=1, device_id=target, device_id_type=MESH)

    for plane in (0, 9):
        clear(buf0, every, every, plane, slice(8, 40))
        clear(halo_x, every, plane // 9)
        clear(halo_y, every, plane // 9)
        clear(hbuf, every, plane, slice(8, 40))
        clear(mbuf, every, plane, slice(8, 40))
    clear(buf0, every, every, slice(1, 9), slice(0, 8))
    clear(buf0, every, every, slice(1, 9), slice(40, 48))
    clear(coef1, every, slice(0, 12), low_rows)
    clear(coef1, every, slice(0, 12), slice(32, 48))
    for planes in (slice(0, 4), slice(8, 12)):
        clear(coef1, every, planes, slice(16, 32))
        clear(right1, every, planes, slice(16, 32))
        clear(left1, every, planes, slice(16, 32))
    for ref in (right1, left1):
        clear(ref, every, every, low_rows)
        clear(ref, every, every, high_rows)
    clear(deep1, every, every, every, slice(0, 8))
    clear(deep1, every, every, every, slice(40, 48))
    clear(deep2, every, every, every, slice(0, 8))
    clear(deep2, every, every, every, slice(32, 40))
    for plane in (1, 10):
        clear(coef2, every, plane)
        clear(deep2, every, every, plane)
    clear(coef2, every, every, slice(32, 40))
    for plane in (0, 1, 10, 11):
        clear(sol2, every, plane, slice(8, 32))
    for side in (0, 2):
        clear(zgot1, every, side)

    def remote(src, dst, ssem, rsem, target):
        return pltpu.make_async_remote_copy(
            src_ref=src, dst_ref=dst, send_sem=ssem, recv_sem=rsem,
            device_id=target, device_id_type=MESH,
        )

    lane8 = lanes_of((8, 128))

    zero8 = jnp.zeros((8, 128), F32)

    def pack(accs, planes, x, lows=True, highs=True):
        parts = [p[8 * g : 8 * g + 8] for p in planes for g in range(4)]
        n = len(parts)
        low = high = zero8
        for j, part in enumerate(parts):
            turned = pltpu.roll(part, j, 1) if j else part
            if lows:
                low = jnp.where(lane8 == j, turned, low)
            if highs:
                high = jnp.where(lane8 == (127 + j) % 128, turned, high)
        return (
            accs[0] + pltpu.roll(low, n * x, 1) if lows else accs[0],
            accs[1] + pltpu.roll(high, n * x, 1) if highs else accs[1],
        )

    def merged(before, after):
        before, after = pltpu.roll(before, 1, 1), pltpu.roll(after, 127, 1)
        even = jnp.bitwise_and(lane8, 1) == 0
        return jnp.where(even, before, after), jnp.where(even, after, before)

    def rims_of(halo, n, x):
        turn_back = lax.rem(128 - n * x, 128)
        halo = [pltpu.roll(h, turn_back, 1) for h in halo]
        return [pltpu.roll(halo[j % 2], 128 - j, 1) if j else halo[0] for j in range(n)]

    lane32, lane16 = lanes_of((32, 128)), lanes_of((16, 128))

    def shifted(v, rims):
        rim = jnp.concatenate(rims, 0) if isinstance(rims, list) else rims
        low = jnp.where(lane32 == 0, rim, pltpu.roll(v, 1, 1))
        high = jnp.where(lane32 == 127, rim, pltpu.roll(v, 127, 1))
        return low, high

    def guarded(copy, step):
        sends_it, gets_it = (rad < 3, rad > 0) if step == 1 else (rad > 0, rad < 3)

        def start():
            pl.when(sends_it)(copy.start)

        def arrived():
            pl.when(gets_it)(copy.wait_recv)

        def left():
            pl.when(sends_it)(copy.wait_send)

        return start, arrived, left

    def plain(copy):
        return copy.start, copy.wait_recv, copy.wait_send

    unsettled = []

    def settle():
        for left in unsettled:
            left()
        unsettled.clear()

    def sends(buf, zref, ssem, rsem, beside=None):
        rows, planes = pl.ds(TOP, 32), pl.ds(1, 8)
        if beside is None:
            to = [buf.at[:, 0, rows], buf.at[:, 9, rows], buf.at[:, planes, pl.ds(TOP - 1, 1)], buf.at[:, planes, pl.ds(TOP + 32, 1)]]
        else:
            in_x, in_y = beside
            to = [in_x.at[0], in_x.at[1], in_y.at[0, :, :, pl.ds(0, 1)], in_y.at[1, :, :, pl.ds(7, 1)]]
        parts = [
            (buf.at[:, 8, rows], to[0], up[0]),
            (buf.at[:, 1, rows], to[1], down[0]),
            (buf.at[:, planes, pl.ds(TOP + 31, 1)], to[2], up[1]),
            (buf.at[:, planes, pl.ds(TOP, 1)], to[3], down[1]),
            (zref.at[1], zref.at[2], up[2]),
            (zref.at[0], zref.at[3], down[2]),
        ]
        copies = [
            remote(src, dst, ssem.at[i], rsem.at[i], target)
            for i, (src, dst, target) in enumerate(parts)
        ]
        return [plain(copy) for copy in copies[4:]] + [guarded(copies[0], 1), guarded(copies[1], -1)] + [plain(copy) for copy in copies[2:4]]

    turn = [0]

    def send_all(accs, buf, zref, ssem, rsem, beside=None):
        zref[0], zref[1] = accs
        copies = sends(buf, zref, ssem, rsem, beside)
        for start, _, _ in copies:
            start()
        settle()

        def finish():
            for _, arrived, left in copies:
                arrived()
                unsettled.append(left)
            return merged(zref[2], zref[3])

        return finish

    def exchange(accs, buf=None):
        p = turn[0] % 2
        turn[0] += 1
        sems = (zbuf.at[p], send_sem.at[p], recv_sem.at[p])
        return send_all(accs, buf0.at[p], *sems, (halo_x.at[p], halo_y.at[p])) if buf is None else send_all(accs, buf, *sems)

    for copy in loads[:2]:
        copy.wait()

    def pack_base(x, accs):
        return pack(accs, [base[c, x + 1, own_rows, :] for c in range(2)], x)

    accs = lax.fori_loop(0, 8, pack_base, (zero8, zero8), unroll=2)
    pl.semaphore_wait(barrier, len(peers))
    finish = exchange(accs, base)
    loads[3].wait()

    def pack_fwd(x, accs):
        return pack(accs, [fwd[c, x + 1, own_rows, :] for c in range(3)], x, highs=False)

    fwd_z[0] = lax.fori_loop(0, 8, pack_fwd, (zero8, zero8), unroll=2)[0]
    fwd_parts = [
        (fwd.at[:, 1, own_rows], fwd.at[:, 9, own_rows], down[0]),
        (fwd.at[:, pl.ds(1, 8), pl.ds(TOP, 1)], fwd.at[:, pl.ds(1, 8), pl.ds(TOP + 32, 1)], down[1]),
        (fwd_z.at[0], fwd_z.at[1], down[2]),
    ]
    fwd_copies = [
        remote(src, dst, fsend.at[i], frecv.at[i], target)
        for i, (src, dst, target) in enumerate(fwd_parts)
    ]
    fwd_copies = [guarded(fwd_copies[0], -1)] + [plain(copy) for copy in fwd_copies[1:]]
    for begin, _, _ in fwd_copies:
        begin()

    grid_row, grid_lane = rows_of((128, 128)), lanes_of((128, 128))
    pair = (grid_row // 2 == grid_lane).astype(F32)
    own_pair = jnp.where(grid_row < 64, pair, 0.0)
    pick = [(grid_row == 2 * grid_lane + s).astype(F32) for s in range(2)]
    spread0 = (grid_row == grid_lane // 2).astype(F32)
    spread1 = (grid_row == jnp.where(grid_lane < 96, 0, 64) + grid_lane // 2).astype(F32)

    def times(a, b):
        return jnp.dot(a, b, precision=HI, preferred_element_type=F32)

    def edge(x, side, nx):
        at_edge = (rad == 0) & (x == 0) if side == 0 else (rad == 3) & (x == nx - 1)
        return jnp.where(at_edge, 0.0, 1.0).astype(F32)

    def edge_rows(side, ny):
        row = rows_of((ny, 128))
        at_edge = (lat == 0) & (row == 0) if side == 0 else (lat == 7) & (row == ny - 1)
        return jnp.where(at_edge, 0.0, 1.0).astype(F32)

    loads[2].wait()
    halo = finish()

    def setup_plane(x, accs):
        v = base[0, x + 1, own_rows, :]
        rims = rims_of(halo, 8, x)
        low_z, high_z = shifted(v, rims[:4])
        lower_x, upper_x, lower_y, upper_y = edge(x, 0, 8), edge(x, 1, 8), edge_rows(0, 32), edge_rows(1, 32)
        six = [
            0.5 * (v + lower_x * base[0, x, own_rows, :]),
            0.5 * (v + upper_x * base[0, x + 2, own_rows, :]),
            0.5 * (v + lower_y * base[0, x + 1, pl.ds(TOP - 1, 32), :]),
            0.5 * (v + upper_y * base[0, x + 1, pl.ds(TOP + 1, 32), :]),
            0.5 * (v + low_z),
            0.5 * (v + high_z),
        ]
        at = block(x, 32)
        for k in range(6):
            faces0[k, at, :] = six[k]
        masks = (lower_x, upper_x, lower_y, upper_y)
        for k in range(6):
            links0[k, at, :] = six[k] * masks[k] if k < 4 else jnp.where(lane32 == (0, 127)[k - 4], 0.0, six[k])
        rim_link[at, :] = jnp.where(lane32 == 0, six[4], jnp.where(lane32 == 127, six[5], 0.0))
        diag = six[0] + six[1] + six[2] + six[3] + six[4] + six[5]
        inv = 1.0 / diag
        diag0[at, :] = diag
        inv0[at, :] = inv
        p = base[1, x + 1, own_rows, :]
        _, high_p = shifted(p, rims[4:])
        grads = [
            base[1, x + 2, own_rows, :] * upper_x - p,
            base[1, x + 1, pl.ds(TOP + 1, 32), :] * upper_y - p,
            high_p - p,
        ]
        updates = []
        for c in range(3):
            right = load[c, x] - grads[c]
            res0[c, at, :] = right
            update = inv * right * FIRST
            buf0[1, c, x + 1, own_rows, :] = update
            updates.append(update)
        return pack(accs, updates, x)

    start = lax.fori_loop(0, 8, setup_plane, (zero8, zero8))

    def coarsen(level, fine, coarse):
        nx, ny, _ = LEVELS[level]
        half_x, half_y = nx // 2, ny // 2
        n = half_x * half_y

        def one(x, carry):
            for k in range(6):
                way, side = k // 2, k % 2
                if way == 0:
                    plane = fine[k, block(2 * x + side, ny), :]
                else:
                    plane = fine[k, block(2 * x, ny), :] + fine[k, block(2 * x + 1, ny), :]
                tmp[k, pl.ds(0, ny), :] = plane
            for k in range(6):
                way, side = k // 2, k % 2
                if way == 1:
                    both = tmp[k, pl.ds(side, half_y, 2), :]
                else:
                    both = tmp[k, pl.ds(0, half_y, 2), :] + tmp[k, pl.ds(1, half_y, 2), :]
                flat[k, block(x, half_y), :] = both
            return carry

        lax.fori_loop(0, half_x, one, 0)
        sums = times(flat[0:4, :n, :].reshape(4 * n, 128), pair).reshape(4, n, 128)
        for k in range(4):
            coarse[k] = sums[k]
        for k in range(4, 6):
            coarse[k] = times(flat[k, :n, :], pick[k - 4])

    def coefficients(level, faces, x):
        nx, ny, _ = LEVELS[level]
        six = [faces[k, pl.ds(x * ny, ny), :] for k in range(6)]
        total = six[0] + six[1] + six[2] + six[3] + six[4] + six[5]
        return [total, six[0] * edge(x, 0, nx), six[2] * edge_rows(0, ny), six[4]]

    def invert(coef, inv, planes):
        def one(x, carry):
            d = coef[0, x]
            inv[x] = jnp.where(d > 0.0, 1.0 / jnp.where(d > 0.0, d, 1.0), 0.0)
            return carry

        lax.fori_loop(0, planes, one, 0)

    side_lanes = (lane8 < 68) | (lane8 >= 124)

    def exchange1(use, ref, depth_up, depth_down):
        n = ref.shape[0]
        zlow = zhigh = zero8
        for x in range(4):
            for a in range(n):
                for g in range(2):
                    at = 4 * ((x * n + a) * 2 + g)
                    part = ref[a, 4 + x, pl.ds(16 + 8 * g, 8), :]
                    turned = pltpu.roll(part, at, 1) if at else part
                    zlow = jnp.where((lane8 >= at) & (lane8 < at + 4), turned, zlow)
                    top = (60 + at) % 128
                    zhigh = jnp.where((lane8 >= top) & (lane8 < top + 4), turned, zhigh)
        zsend1[use, 0] = zlow
        zsend1[use, 1] = zhigh
        copies = []
        for i, (a, b, c) in enumerate(near1):
            if c:
                src = zsend1.at[use, (c + 1) // 2]
                dst = zgot1.at[use, 1 - a, 1 - b, (1 - c) // 2]
            else:
                from_x, to_x, from_y, to_y = pl.ds(4, 4), pl.ds(4, 4), OWN1, OWN1
                if a == 1:
                    from_x, to_x = pl.ds(8 - depth_up, depth_up), pl.ds(4 - depth_up, depth_up)
                if a == -1:
                    from_x, to_x = pl.ds(4, depth_down), pl.ds(8, depth_down)
                if b == 1:
                    from_y, to_y = pl.ds(28, 4), pl.ds(12, 4)
                if b == -1:
                    from_y, to_y = pl.ds(16, 4), pl.ds(32, 4)
                src, dst = ref.at[:, from_x, from_y], ref.at[:, to_x, to_y]
            copy = remote(src, dst, dsend1.at[use, i], drecv1.at[use, i], device(a, b, c))
            copies.append((a, copy))

        def each(way, do):
            group = [copy for a, copy in copies if a == way]
            for copy in group:
                do(copy)

        for way, there in ((1, rad < 3), (-1, rad > 0)):
            pl.when(there)(lambda way=way: each(way, lambda copy: copy.start()))
        each(0, lambda copy: copy.start())

        def finish(low_plane, high_plane):
            for way, gets_it in ((1, rad > 0), (-1, rad < 3)):
                pl.when(gets_it)(lambda way=way: each(way, lambda copy: copy.wait_recv()))
            each(0, lambda copy: copy.wait_recv())

            for way, sends_it in ((1, rad < 3), (-1, rad > 0)):
                pl.when(sends_it)(lambda way=way: each(way, lambda copy: copy.wait_send()))
            each(0, lambda copy: copy.wait_send())

            def one(plane, carry):
                dx, x = lax.div(plane, 4), lax.rem(plane, 4)
                back = lax.rem(192 - 8 * n * x, 128)
                for dy, groups in ((0, (1,)), (1, (2, 3)), (2, (4,))):
                    above = pltpu.roll(zgot1[use, dx, dy, 1], back, 1)
                    below = pltpu.roll(zgot1[use, dx, dy, 0], back, 1)
                    both = jnp.where((lane8 >= 64) & (lane8 < 96), above, below)
                    for a in range(n):
                        for group in groups:
                            g = (1, group - 2, 0)[dy]
                            at = (128 - 4 * (2 * a + g)) % 128
                            side = pltpu.roll(both, at, 1) if at else both
                            rows = pl.ds(8 * group, 8)
                            own = ref[a, plane, rows, :]
                            side = jnp.where(side_lanes, side, 0.0)
                            ref[a, plane, rows, :] = jnp.where(lane8 < 64, own, side)
                return carry

            lax.fori_loop(low_plane, high_plane, one, 0, unroll=2)

        return finish

    def layers1(use, ref, depth_up, depth_down):
        n = ref.shape[0]

        def go(copies):
            for start, _, _ in copies:
                start()

        def done(copies):
            for _, arrived, left in copies:
                arrived()
                left()

        def copy(i, src, dst, target):
            return remote(src, dst, csend1.at[use, i], crecv1.at[use, i], target)

        planes, zs = pl.ds(0, 12), cz.at[use]
        up_x, down_x = (pl.ds(8 - depth_up, depth_up), pl.ds(4 - depth_up, depth_up)), (pl.ds(4, depth_down), pl.ds(8, depth_down))
        in_x = [
            guarded(copy(0, ref.at[:, up_x[0], OWN1], ref.at[:, up_x[1], OWN1], up[0]), 1),
            guarded(copy(1, ref.at[:, down_x[0], OWN1], ref.at[:, down_x[1], OWN1], down[0]), -1),
        ]
        in_y = [
            plain(copy(2, ref.at[:, planes, pl.ds(28, 4)], ref.at[:, planes, pl.ds(12, 4)], up[1])),
            plain(copy(3, ref.at[:, planes, pl.ds(16, 4)], ref.at[:, planes, pl.ds(32, 4)], down[1])),
        ]
        in_z = [
            plain(copy(4, zs.at[1], zs.at[2], up[2])),
            plain(copy(5, zs.at[0], zs.at[3], down[2])),
        ]
        parts = [(s, a, g) for s in range(2) for a in range(n) for g in range(4)]

        def pack_pair(t, carry):
            zlow = zhigh = zero8
            for j, (s, a, g) in enumerate(parts):
                part = ref[a, 2 * t + s, pl.ds(8 + 8 * g, 8), :]
                turned = pltpu.roll(part, 4 * j, 1) if j else part
                zlow = jnp.where((lane8 >= 4 * j) & (lane8 < 4 * j + 4), turned, zlow)
                top = (60 + 4 * j) % 128
                zhigh = jnp.where((lane8 >= top) & (lane8 < top + 4), turned, zhigh)
            zs[0, t] = zlow
            zs[1, t] = zhigh
            return carry

        def unpack_pair(t, carry):
            below, above = zs[2, t], zs[3, t]
            for m in range(n):
                turn_by = (192 - 32 * m) % 128
                high = pltpu.roll(above, turn_by, 1) if turn_by else above
                low = pltpu.roll(below, turn_by, 1) if turn_by else below
                both = jnp.where((lane8 >= 64) & (lane8 < 96), high, low)
                for j in range(8):
                    s, a, g = parts[8 * m + j]
                    side = pltpu.roll(both, 128 - 4 * j, 1) if j else both
                    rows = pl.ds(8 + 8 * g, 8)
                    own = ref[a, 2 * t + s, rows, :]
                    side = jnp.where(side_lanes, side, 0.0)
                    ref[a, 2 * t + s, rows, :] = jnp.where(lane8 < 64, own, side)
            return carry

        def first():
            go(in_x)

        def second():
            done(in_x)
            go(in_y)

        def third():
            done(in_y)
            lax.fori_loop(0, 6, pack_pair, 0)
            go(in_z)

        def last():
            done(in_z)
            lax.fori_loop(0, 6, unpack_pair, 0)

        return first, second, third, last

    def spread_coef2(tiles):
        ref = dgot2.at[0]
        for i, t in enumerate(tiles):
            ref[rad, 1, 1, i] = t

        def copy(i, src, dst, target):
            return remote(src, dst, csend2.at[i], crecv2.at[i], target)

        steps = [
            [copy(i, ref.at[rad, 1, 1], ref.at[rad, 1, 1], target) for i, target in enumerate(through)],
            [
                copy(3, ref.at[:, 1, 1], ref.at[:, 0, 1], up[1]),
                copy(4, ref.at[:, 1, 1], ref.at[:, 2, 1], down[1]),
            ],
            [
                copy(5, ref.at[:, :, 1], ref.at[:, :, 0], up[2]),
                copy(6, ref.at[:, :, 1], ref.at[:, :, 2], down[2]),
            ],
        ]

        def go(i):
            if i:
                for c in steps[i - 1]:
                    c.wait()
            if i < 3:
                for c in steps[i]:
                    c.start()

        return go

    def exchange2(use, tiles):
        n = len(tiles)
        for i, t in enumerate(tiles):
            dgot2[use, rad, 1, 1, i] = t
        copies = []
        for i, (a, b, c) in enumerate(near2):
            src = dgot2.at[use, rad, 1, 1, pl.ds(0, n)]
            dst = dgot2.at[use, rad, 1 - b, 1 - c, pl.ds(0, n)]
            copies.append(remote(src, dst, dsend2.at[i], drecv2.at[i], device(a, b, c)))
        for copy in copies:
            copy.start()

        def finish():
            for copy in copies:
                copy.wait_recv()
                unsettled.append(copy.wait_send)

        return finish

    def packed2(parts):
        tiles = []
        for i in range(0, len(parts), 4):
            out = zero8
            for j, part in enumerate(parts[i : i + 4]):
                part = pltpu.roll(part, 32 * j, 1) if j else part
                out = jnp.where((lane8 >= 32 * j) & (lane8 < 32 * j + 32), part, out)
            tiles.append(out)
        return tiles

    def turned2(use, source, dy, dz, tile_at, lanes):
        t = dgot2[use, source, dy, dz, tile_at]
        return pltpu.roll(t, lanes % 128, 1) if lanes % 128 else t

    def joined2(use, source, dy, part):
        i, at = part // 4, 32 * (part % 4)
        own = turned2(use, source, dy, 1, i, -at)
        after = turned2(use, source, dy, 2, i, 32 - at)
        before = turned2(use, source, dy, 0, i, 96 - at)
        out = jnp.where(lane8 < 32, own, jnp.where(lane8 < 64, after, before))
        return jnp.where((lane8 < 64) | (lane8 >= 96), out, 0.0)

    def unpack2(use, ref):
        n = ref.shape[0]

        def one(source, carry):
            for a in range(n):
                for x in range(2):
                    for dy in range(3):
                        ref[a, 2 + 2 * source + x, pl.ds(8 + 8 * dy, 8), :] = joined2(use, source, dy, 2 * a + x)
            return carry

        lax.fori_loop(0, 4, one, 0)

    coefs, invs = (None, coef1, coef2), (None, inv1, inv2)
    deeps, sols = (None, deep1, deep2), (None, sol1, sol2)

    def begin_deep(level, res, planes, keep):
        rows = pl.ds(8, DEEP_ROWS[level] - 16)

        def one(x, carry):
            for c in range(3):
                update = FIRST * invs[level][x, rows, :] * res[c, x, rows, :]
                deeps[level][0, c, x, rows, :] = update
                sols[level][c, x, rows, :] = update
            return carry

        lax.fori_loop(planes[0], planes[1], one, 0, unroll=2)

    def sweep_deep(level, p, res, out, planes, step, initial=False, rows=None):
        coef, inv, deep, sol = coefs[level], invs[level], deeps[level], sols[level]
        first, count = (8, DEEP_ROWS[level] - 16) if rows is None else rows
        here, under, over = pl.ds(first, count), pl.ds(first - 1, count), pl.ds(first + 1, count)

        def one(x, carry):
            diag, lower_x, upper_x = coef[0, x, here, :], coef[1, x, here, :], coef[1, x + 1, here, :]
            lower_y, upper_y, lower_z = coef[2, x, here, :], coef[2, x, over, :], coef[3, x, here, :]
            upper_z = pltpu.roll(lower_z, 127, 1)
            for c in range(3):
                v = deep[p, c, x, here, :]
                total = diag * v - lower_x * deep[p, c, x - 1, here, :] - upper_x * deep[p, c, x + 1, here, :]
                total = total - lower_y * deep[p, c, x, under, :] - upper_y * deep[p, c, x, over, :]
                total = total - lower_z * pltpu.roll(v, 1, 1) - upper_z * pltpu.roll(v, 127, 1)
                r = res[c, x, here, :] - total
                out[c, x, here, :] = r
                if step is None:
                    continue
                if initial:
                    update = FIRST * inv[x, here, :] * r
                    sol[c, x, here, :] = sol[c, x, here, :] + v + update
                else:
                    update = step[0] * v + step[1] * inv[x, here, :] * r
                    sol[c, x, here, :] = sol[c, x, here, :] + update
                deep[1 - p, c, x, here, :] = update
            return carry

        lax.fori_loop(planes[0], planes[1], one, 0, unroll=4 if (planes[1] - planes[0]) % 4 == 0 else 2)

    def inside(p, first=False):
        def plane(x, carry):
            at = block(x, 32)
            diag = diag0[at, :]
            ls = [links0[k, at, :] for k in range(6)]
            for c in range(3):
                v = buf0[p, c, x + 1, own_rows, :]
                total = diag * v - ls[0] * buf0[p, c, x, own_rows, :]
                total = total - ls[1] * buf0[p, c, x + 2, own_rows, :]
                total = total - ls[2] * buf0[p, c, x + 1, pl.ds(TOP - 1, 32), :]
                total = total - ls[3] * buf0[p, c, x + 1, pl.ds(TOP + 1, 32), :]
                total = total - ls[4] * pltpu.roll(v, 1, 1) - ls[5] * pltpu.roll(v, 127, 1)
                res0[c, at, :] = res0[c, at, :] - total
                sol0[c, at, :] = v if first else sol0[c, at, :] + v
            return carry

        lax.fori_loop(0, 8, plane, 0, unroll=4)

    def rim_terms(p, halo, step, emit=None):
        for side, rows in ((0, pl.ds(0, 32)), (1, pl.ds(224, 32))):
            link = links0[side, rows, :]
            for c in range(3):
                res0[c, rows, :] = res0[c, rows, :] + link * halo_x[p, side, c]

        def plane(x, accs):
            at = block(x, 32)
            inv, rim = inv0[at, :], rim_link[at, :]
            low_y, high_y = links0[2, block(4 * x, 8), :], links0[3, block(4 * x + 3, 8), :]
            rims = rims_of(halo, 12, x)
            packs = []
            for c in range(3):
                r = res0[c, at, :] + rim * jnp.concatenate(rims[4 * c : 4 * c + 4], 0)
                top = r[0:8] + low_y * halo_y[p, 0, c, x]
                bottom = r[24:32] + high_y * halo_y[p, 1, c, x]
                r = jnp.concatenate([top, r[8:24], bottom], 0)
                if emit is None:
                    res0[c, at, :] = r
                if step is None:
                    continue
                update = step[0] * buf0[p, c, x + 1, own_rows, :] + step[1] * inv * r
                if emit is None:
                    buf0[1 - p, c, x + 1, own_rows, :] = update
                    packs.append(update)
                else:
                    packs.append(sol0[c, at, :] + update)
            if step is None:
                return accs
            if emit is not None:
                emit(packs, x)
            return pack(accs, packs, x)

        return lax.fori_loop(0, 8, plane, (zero8, zero8), unroll=4)

    def correct(p):
        def plane(x, accs):
            at = block(x, 32)
            diag, inv = diag0[at, :], inv0[at, :]
            ls = [links0[k, at, :] for k in range(6)]
            packs = []
            for c in range(3):
                v = wide0[c, x + 1, own_rows, :]
                total = diag * v - ls[0] * wide0[c, x, own_rows, :]
                total = total - ls[1] * wide0[c, x + 2, own_rows, :]
                total = total - ls[2] * wide0[c, x + 1, pl.ds(TOP - 1, 32), :]
                total = total - ls[3] * wide0[c, x + 1, pl.ds(TOP + 1, 32), :]
                total = total - ls[4] * pltpu.roll(v, 1, 1) - ls[5] * pltpu.roll(v, 127, 1)
                r = res0[c, at, :] - total + rim_link[at, :] * rim0[c, x]
                res0[c, at, :] = r
                sol0[c, at, :] = sol0[c, at, :] + v
                update = FIRST * inv * r
                buf0[p, c, x + 1, own_rows, :] = update
                packs.append(update)
            return pack(accs, packs, x)

        return lax.fori_loop(0, 8, plane, (zero8, zero8), unroll=2)

    def restrict(source, rows, level, matrix):
        nx, ny, _ = LEVELS[level]
        half_x, half_y = nx // 2, ny // 2
        n = half_x * half_y

        def one(x, carry):
            for c in range(3):
                tmp[c, pl.ds(0, ny), :] = source(c, 2 * x) + source(c, 2 * x + 1)
            for c in range(3):
                flat[c, block(x, half_y), :] = tmp[c, pl.ds(0, half_y, 2), :] + tmp[c, pl.ds(1, half_y, 2), :]
            return carry

        lax.fori_loop(0, half_x, one, 0)
        return times(flat[0:3, :n, :].reshape(3 * n, 128), matrix)

    def gather(use):
        first = [
            remote(tile.at[use, 0], got1.at[use, lon], send1.at[use, i], recv1.at[use, i], target)
            for i, target in enumerate(along)
        ]
        second = [
            remote(tile.at[use, 1], got2.at[use, block(lat, 8)], send2.at[use, i], recv2.at[use, i], target)
            for i, target in enumerate(across)
        ]

        def begin(value):
            tile[use, 0] = value
            got1[use, lon] = value
            for copy in first:
                copy.start()

        def middle():
            for copy in first:
                copy.wait_recv()
                unsettled.append(copy.wait_send)
            total = got1[use, 0]
            for k in range(1, 8):
                total = total + got1[use, k]
            tile[use, 1] = total
            got2[use, block(lat, 8), :] = total
            for copy in second:
                copy.start()

        def end():
            for copy in second:
                copy.wait_recv()
                unsettled.append(copy.wait_send)

        return begin, middle, end

    lane1 = lanes_of((1, 128))
    runs = jnp.bitwise_and(owner[0, 0:1, :], 31)
    runs = jnp.concatenate([runs, jnp.full((1, 96), -1, jnp.int32)], 1)

    def member_of(columns):
        return (grid_row == jnp.broadcast_to(columns, (128, 128))).astype(F32)

    own_member = member_of(runs)

    def to_runs(rows):
        return lax.dot_general(
            rows, own_member, (((1,), (1,)), ((), ())), precision=HI, preferred_element_type=F32
        )

    def stacked(rows, count=8):
        out = jnp.zeros((count, 128), F32)
        at = rows_of((count, 128))
        for i, row in enumerate(rows):
            out = jnp.where(at == i, jnp.broadcast_to(row, (count, 128)), out)
        return out

    def rowsum(plane):
        return jnp.sum(plane, axis=0, keepdims=True)

    def run_sides():
        f = faces2
        wide = jnp.broadcast_to(runs, (8, 128))
        first_cell = (lane1 == 0) | (runs != pltpu.roll(wide, 1, 1)[0:1])
        last_cell = (lane1 == 31) | (runs != pltpu.roll(wide, 127, 1)[0:1])
        sides = [
            rowsum(f[0, 0:8, :]),
            rowsum(f[1, 8:16, :]),
            f[2, 0:1, :] + f[2, 8:9, :],
            f[3, 7:8, :] + f[3, 15:16, :],
            jnp.where(first_cell, rowsum(f[4, 0:8, :] + f[4, 8:16, :]), 0.0),
            jnp.where(last_cell, rowsum(f[5, 0:8, :] + f[5, 8:16, :]), 0.0),
        ]
        whole = sides[0] + sides[1] + sides[2] + sides[3] + sides[4] + sides[5]
        return to_runs(stacked([sides[0], sides[2], sides[4], whole]))

    def coarse_solve(meanwhile):
        begin, middle, end = gather(0)
        rows = []
        for block_x in range(4):
            for c in range(3):
                both = right2[c, 2 + 2 * block_x, OWN2, :] + right2[c, 3 + 2 * block_x, OWN2, :]
                rows.append(rowsum(both))
        sums = to_runs(stacked(rows, 16))
        row8 = rows_of((8, 128))
        value = zero8
        for block_x in range(4):
            part = jnp.where(row8 < 3, 0.0, pltpu.roll(dgot2[0, block_x, 1, 1, 2], 2, 0))
            for c in range(3):
                row = jnp.broadcast_to(sums[3 * block_x + c : 3 * block_x + c + 1], (8, 128))
                part = jnp.where(row8 == c, row, part)
            value = value + (pltpu.roll(part, 32 * block_x, 1) if block_x else part)
        begin(value)
        meanwhile[0]()
        middle()
        meanwhile[1]()
        end()

        def all_of(i):
            return got2[0, pl.ds(i, 8, 8), :]

        wrap = jnp.bitwise_and(lane8, 31)

        def lower_z(v):
            return jnp.where(wrap == 0, pltpu.roll(v, 97, 1), pltpu.roll(v, 1, 1))

        def upper_z(v):
            return jnp.where(wrap == 31, pltpu.roll(v, 31, 1), pltpu.roll(v, 127, 1))

        link_x = jnp.where(lane8 < 32, 0.0, all_of(3))
        link_y = jnp.where(row8 == 0, 0.0, all_of(4))
        link_z = all_of(5)
        link_xu, link_yu, link_zu = pltpu.roll(link_x, 96, 1), pltpu.roll(link_y, 7, 0), upper_z(link_z)
        diagonal = all_of(6)
        inverse = 1.0 / diagonal

        def operate(v):
            out = diagonal * v - link_x * pltpu.roll(v, 32, 1) - link_xu * pltpu.roll(v, 96, 1)
            out = out - link_y * pltpu.roll(v, 1, 0) - link_yu * pltpu.roll(v, 7, 0)
            return out - link_z * lower_z(v) - link_zu * upper_z(v)

        rs = [all_of(c) for c in range(3)]
        ds = [inverse * r * COARSE_FIRST for r in rs]
        es = list(ds)
        for a, b in COARSE_STEPS:
            rs = [r - operate(d) for r, d in zip(rs, ds)]
            ds = [a * d + b * inverse * r for r, d in zip(rs, ds)]
            es = [e + d for e, d in zip(es, ds)]
        for c in range(3):
            erows[c] = es[c]
        lats = [lax.rem(lat + 7, 8), lat, lax.rem(lat + 1, 8)]
        rows = [erows[c, pl.ds(at, 1), :] for c in range(3) for at in lats]
        rows = stacked(rows, 16)
        rows = [rows if k == 0 else pltpu.roll(rows, 128 - 32 * k, 1) for k in range(4)]
        spans = times(jnp.concatenate(rows, 0), region_member())
        for block_x in range(4):
            for c in range(3):
                for dy in range(3):
                    i = 16 * block_x + 3 * c + dy
                    row = jnp.broadcast_to(spans[i : i + 1], (8, 128))
                    for x in range(2):
                        deep2[1, c, 2 + 2 * block_x + x, pl.ds(8 + 8 * dy, 8), :] = row

    def region_member():
        own, before, after = (turned2(0, rad, 1, k, 2, t)[0:1] for k, t in ((1, 0), (0, 96), (2, 32)))
        columns = jnp.where(lane1 < 32, own, jnp.where(lane1 < 64, after, before))
        columns = jnp.where((lane1 < 64) | (lane1 >= 96), columns, -1.0).astype(jnp.int32)
        return member_of(columns)

    pending = {}

    def while_first():
        coarsen(0, faces0, faces1)
        for x in range(4):
            for k, value in enumerate(coefficients(1, faces1, x)):
                coef1[k, 4 + x, OWN1, :] = value
        pending["coef1"] = layers1(0, coef1, 3, 4)
        pending["coef1"][0]()

    def while_second():
        pending["coef1"][1]()
        coarsen(1, faces1, faces2)
        values = [coefficients(2, faces2, x) for x in range(2)]
        last = jnp.where(rows_of((8, 128)) == 0, runs.astype(F32), pltpu.roll(run_sides(), 1, 0))
        parts = packed2([values[x][k] for k in range(4) for x in range(2)])
        pending["coef2"] = spread_coef2(parts + [last])
        pending["coef2"](0)

    def weigh_all():
        def weigh(x, accs):
            v, inv = base[0, x + 1, own_rows, :], inv0[block(x, 32), :]
            parts = [2.0 * inv * (v - faces0[2 * c + 1, block(x, 32), :]) for c in range(3)]
            for c in range(3):
                hbuf[c, x + 1, own_rows, :] = parts[c]
            return pack(accs, parts, x)

        accs = lax.fori_loop(0, 8, weigh, (zero8, zero8), unroll=2)
        pending["h"] = send_all(accs, hbuf, hz, hsend, hrecv)

    def applied_to(buf, halo, x):
        at = block(x, 32)
        rims = rims_of(halo, 12, x)
        out = []
        for c in range(3):
            v = buf[c, x + 1, own_rows, :]
            total = diag0[at, :] * v - links0[0, at, :] * buf[c, x, own_rows, :]
            total = total - links0[1, at, :] * buf[c, x + 2, own_rows, :]
            total = total - links0[2, at, :] * buf[c, x + 1, pl.ds(TOP - 1, 32), :]
            total = total - links0[3, at, :] * buf[c, x + 1, pl.ds(TOP + 1, 32), :]
            total = total - links0[4, at, :] * pltpu.roll(v, 1, 1) - links0[5, at, :] * pltpu.roll(v, 127, 1)
            out.append(total - rim_link[at, :] * jnp.concatenate(rims[4 * c : 4 * c + 4], 0))
        return out

    def apply_to_h():
        halo = pending["h"]()

        def one(x, accs):
            at = block(x, 32)
            v, inv = base[0, x + 1, own_rows, :], inv0[at, :]
            parts = []
            for c, g in enumerate(applied_to(hbuf, halo, x)):
                u = (1.0 + STEPS[1][0]) * 2.0 * (v - faces0[2 * c + 1, at, :]) - STEPS[1][1] * g
                applied[c, at, :] = u
                m = STEPS[0][1] * inv * u + STEPS[1][1] * hbuf[c, x + 1, own_rows, :]
                mbuf[c, x + 1, own_rows, :] = m
                parts.append(m)
            return pack(accs, parts, x)

        accs = lax.fori_loop(0, 8, one, (zero8, zero8), unroll=2)
        pending["m"] = send_all(accs, mbuf, mz, msend, mrecv)

    def apply_to_m():
        halo = pending["m"]()

        def one(x, carry):
            at = block(x, 32)
            for c, g in enumerate(applied_to(mbuf, halo, x)):
                applied[c, at, :] = STEPS[0][0] * applied[c, at, :] - g
            return carry

        lax.fori_loop(0, 8, one, 0, unroll=2)

    def while_third():
        pending["coef1"][2]()
        pending["coef2"](1)

    accs = start
    for step, meanwhile in ((STEPS[0], while_first), (STEPS[1], while_second), (None, while_third)):
        p = turn[0] % 2
        finish = exchange(accs)
        inside(p, meanwhile is while_first)
        meanwhile()
        accs = rim_terms(p, finish(), step)

    sums = restrict(lambda c, x: res0[c, block(x, 32), :], 32, 0, pair)
    for c in range(3):
        for x in range(4):
            right1[c, 4 + x, OWN1, :] = sums[64 * c + 16 * x : 64 * c + 16 * x + 16]
    finish = exchange1(0, right1, 3, 3)
    pending["coef1"][3]()
    invert(coef1, inv1, 12)
    pending["coef2"](2)
    weigh_all()
    finish(1, 11)
    begin_deep(1, right1, (1, 11), None)
    sweep_deep(1, 0, right1, mid1, (2, 10), STEPS[0])
    sweep_deep(1, 1, mid1, mid1, (3, 9), STEPS[1])
    sweep_deep(1, 0, mid1, left1, (4, 8), None, rows=(16, 16))

    sums = restrict(lambda c, x: left1[c, 4 + x, OWN1, :], 16, 1, own_pair)
    finish2 = exchange2(1, packed2([sums[16 * c + 8 * x : 16 * c + 8 * x + 8] for c in range(3) for x in range(2)]))
    rest = layers1(1, left1, 3, 3)
    rest[0]()
    settle()
    pending["coef2"](3)
    unpack2(0, coef2)
    invert(coef2, inv2, 12)
    apply_to_h()
    rest[1]()
    finish2()
    unpack2(1, right2)
    all2 = (2, 10)
    begin_deep(2, right2, all2, None)
    sweep_deep(2, 0, right2, right2, all2, STEPS[0])
    sweep_deep(2, 1, right2, right2, all2, STEPS[1])
    sweep_deep(2, 0, right2, right2, all2, None)

    def forward_strain():
        for _, arrived, left in fwd_copies:
            arrived()
            left()
        fwd_halo = merged(zero8, fwd_z[1])

        def one(x, carry):
            at = block(x, 32)
            v = base[0, x + 1, own_rows, :]
            keep_x, keep_y = edge(x, 1, 8), edge_rows(1, 32)
            rims = rims_of(fwd_halo, 12, x)
            gf = []
            for c in range(3):
                w = fwd[c, x + 1, own_rows, :]
                _, high_w = shifted(w, rims[4 * c : 4 * c + 4])
                gf.append([
                    fwd[c, x + 2, own_rows, :] * keep_x - w,
                    fwd[c, x + 1, pl.ds(TOP + 1, 32), :] * keep_y - w,
                    high_w - w,
                ])
            for c in range(3):
                strain[c, at, :] = 2.0 * v * gf[c][c]
            for i, (d, e) in enumerate(((0, 1), (0, 2), (1, 2))):
                strain[3 + i, at, :] = v * (gf[e][d] + gf[d][e])
            return carry

        lax.fori_loop(0, 8, one, 0)

    def while_along():
        rest[2]()
        settle()
        apply_to_m()
        forward_strain()

    coarse_solve((while_along, rest[3]))
    sweep_deep(2, 1, right2, right2, all2, STEPS[0], initial=True)
    sweep_deep(2, 0, right2, right2, all2, STEPS[0])
    sweep_deep(2, 1, right2, right2, all2, STEPS[1])

    def gather_rows(k, carry):
        for c in range(3):
            flat[c, block(k, 16), :] = sol2[c, 2 * rad + k, pl.ds(12, 16), :]
        return carry

    lax.fori_loop(0, 6, gather_rows, 0)
    for c in range(3):
        flat[c, 0:96, :] = times(flat[c, 0:96, :], spread1)

    def to_level1(k, carry):
        for c in range(3):
            value = flat[c, block(k, 16), :]
            for s in range(2):
                for t in range(2):
                    deep1[1, c, 2 * k + s, pl.ds(8 + t, 16, 2), :] = value
        return carry

    lax.fori_loop(0, 6, to_level1, 0)
    sweep_deep(1, 1, left1, left1, (1, 11), STEPS[0], initial=True)
    sweep_deep(1, 0, left1, left1, (2, 10), STEPS[0])
    sweep_deep(1, 1, left1, left1, (3, 9), STEPS[1])

    for c in range(3):
        flat[c] = times(sol1[c, 3:9, 12:36, :].reshape(144, 128), spread0)

    for k in range(6):
        for c in range(3):
            value = flat[c, 24 * k : 24 * k + 24, :]
            tmp[c, pl.ds(0, 24, 2), :] = value
            tmp[c, pl.ds(1, 24, 2), :] = value
            if 1 <= k <= 4:
                coarse = sol1[c, 3 + k, OWN1, :]
                rim = jnp.where(lane16 == 0, pltpu.roll(coarse, 1, 1), pltpu.roll(coarse, 63, 1))
                tmp[3 + c, pl.ds(0, 16, 2), :] = rim
                tmp[3 + c, pl.ds(1, 16, 2), :] = rim
        for c in range(3):
            for at in (2 * k - 1, 2 * k):
                if 0 <= at <= 9:
                    wide0[c, at] = tmp[c, pl.ds(0, 48), :]
                if 1 <= at <= 8:
                    rim0[c, at - 1] = tmp[3 + c, pl.ds(0, 32), :]

    p = turn[0] % 2
    accs = correct(p)
    finish = exchange(accs)

    def add_up(x, total):
        at = block(x, 32)
        v = base[0, x + 1, own_rows, :]
        part = base[1, x + 1, own_rows, :]
        for c in range(3):
            update = buf0[p, c, x + 1, own_rows, :]
            part = part - 2.0 * (v - faces0[2 * c + 1, at, :]) * (sol0[c, at, :] + update)
            part = part - mbuf[c, x + 1, own_rows, :] * res0[c, at, :] - applied[c, at, :] * update
        return total + (part[0:8] + part[8:16] + part[16:24] + part[24:32])

    partial = lax.fori_loop(0, 8, add_up, zero8, unroll=2)
    rounds = []
    for i, (got, at, targets) in enumerate(((sum_z, lon, along), (sum_y, lat, across), (sum_x, rad, through))):
        copies = [
            remote(summed.at[i], got.at[at], sum_send.at[i, k], sum_recv.at[i, k], target)
            for k, target in enumerate(targets)
        ]
        rounds.append((got, at, copies))

    def send_sum(i, value):
        got, at, copies = rounds[i]
        summed[i] = value
        got[at] = value
        for copy in copies:
            copy.start()

    def get_sum(i):
        got, _, copies = rounds[i]
        for copy in copies:
            copy.wait_recv()
            unsettled.append(copy.wait_send)
        total = got[0]
        for k in range(1, len(copies) + 1):
            total = total + got[k]
        return total

    send_sum(0, partial)
    inside(p)
    accs = rim_terms(p, finish(), STEPS[0])
    p = turn[0] % 2
    finish = exchange(accs)
    inside(p)
    send_sum(1, get_sum(0))

    def emit(afters, x):
        for c, after in enumerate(afters):
            adjoint[c, x] = after
            wide0[c, x + 1, own_rows, :] = after

    accs = rim_terms(p, finish(), STEPS[1], emit=emit)

    finish = exchange(accs, wide0)
    send_sum(2, get_sum(1))
    halo = finish()

    def outputs(x, carry):
        v = base[0, x + 1, own_rows, :]
        keep_x, keep_y = edge(x, 1, 8), edge_rows(1, 32)
        ga, us = [], []
        rims = rims_of(halo, 12, x)
        for c in range(3):
            u = wide0[c, x + 1, own_rows, :]
            low_z, high_z = shifted(u, rims[4 * c : 4 * c + 4])
            ga.append([
                wide0[c, x + 2, own_rows, :] * keep_x - u,
                wide0[c, x + 1, pl.ds(TOP + 1, 32), :] * keep_y - u,
                high_z - u,
            ])
            us.append((u, low_z))
        divergence = (
            us[0][0] - edge(x, 0, 8) * wide0[0, x, own_rows, :]
            + (us[1][0] - edge_rows(0, 32) * wide0[1, x + 1, pl.ds(TOP - 1, 32), :])
            + (us[2][0] - us[2][1])
        )
        pnext[x] = base[1, x + 1, own_rows, :] - v * divergence
        at = block(x, 32)
        total = strain[0, at, :] * ga[0][0] + strain[1, at, :] * ga[1][1] + strain[2, at, :] * ga[2][2]
        for i, (d, e) in enumerate(((0, 1), (0, 2), (1, 2))):
            total = total + strain[3 + i, at, :] * (ga[e][d] + ga[d][e])
        gradient[x] = total
        return carry

    lax.fori_loop(0, 8, outputs, 0, unroll=2)
    mean = jnp.sum(get_sum(2)) / CELLS
    settle()

    def shift(x, carry):
        pnext[x] = pnext[x] - mean
        return carry

    lax.fori_loop(0, 8, shift, 0)


def per_device(forcing, pressure, viscosity, forward, owner):
    vmem, anywhere = pl.BlockSpec(memory_space=pltpu.VMEM), pl.BlockSpec(memory_space=pl.ANY)
    f32 = lambda *shape: pltpu.VMEM(shape, F32)
    dma = lambda *shape: pltpu.SemaphoreType.DMA(shape)
    return pl.pallas_call(
        kernel,
        out_shape=(
            jax.ShapeDtypeStruct((3, 8, 32, 128), F32),
            jax.ShapeDtypeStruct((8, 32, 128), F32),
            jax.ShapeDtypeStruct((8, 32, 128), F32),
        ),
        in_specs=[anywhere] * 4 + [vmem],
        out_specs=(vmem, vmem, vmem),
        scratch_shapes=[
            f32(3, 8, 32, 128), f32(2, 10, 48, 128), f32(3, 10, 48, 128), f32(1, 8, 128), f32(2, 8, 128),
            f32(2, 3, 10, 48, 128), f32(2, 4, 8, 128), f32(6, 256, 128), f32(6, 64, 128), f32(6, 16, 128),
            f32(6, 256, 128), f32(256, 128), f32(256, 128), f32(3, 256, 128), f32(3, 256, 128), f32(3, 8, 32, 128),
            f32(3, 10, 48, 128), f32(4, 8, 128), f32(3, 256, 128), f32(3, 10, 48, 128), f32(4, 8, 128),
            f32(3, 10, 48, 128), f32(256, 128), f32(2, 2, 3, 32, 128), f32(2, 2, 3, 8, 8, 128), f32(6, 256, 128),
            f32(4, 13, 48, 128), f32(4, 12, 40, 128), f32(12, 48, 128), f32(12, 40, 128),
            f32(3, 12, 48, 128), f32(3, 12, 48, 128), f32(3, 12, 48, 128), f32(3, 12, 40, 128),
            f32(2, 3, 12, 48, 128), f32(2, 3, 12, 40, 128), f32(3, 12, 48, 128), f32(3, 12, 40, 128),
            f32(1, 2, 8, 128), f32(1, 3, 3, 2, 8, 128), f32(2, 4, 6, 8, 128), f32(2, 4, 3, 3, 3, 8, 128),
            f32(6, 48, 128), f32(6, 144, 128), f32(3, 8, 128), f32(1, 2, 8, 128),
            f32(1, 8, 8, 128), f32(1, 64, 128), f32(3, 8, 128), f32(4, 8, 128), f32(8, 8, 128), f32(8, 8, 128),
            dma(4), dma(2, 6), dma(2, 6), dma(3), dma(3), dma(1, 7), dma(1, 7), dma(1, 7), dma(1, 7), dma(3, 7), dma(3, 7),
            dma(1, 26), dma(1, 26), dma(35), dma(35), dma(6), dma(6), dma(6), dma(6), dma(2, 6), dma(2, 6), dma(7), dma(7),
        ],
        compiler_params=pltpu.CompilerParams(
            collective_id=0, has_side_effects=True, vmem_limit_bytes=60 * 1024 * 1024
        ),
    )(forcing, pressure, viscosity, forward, owner)


def solution(mesh):
    placed = (
        P(None, "rad", "lat", "lon"),
        P("rad", "lat", "lon"),
        P("rad", "lat", "lon"),
        P(None, "rad", "lat", "lon"),
        P("rad", "lat", "lon"),
    )
    return jax.shard_map(
        per_device,
        mesh=mesh,
        in_specs=placed,
        out_specs=(P(None, "rad", "lat", "lon"), P("rad", "lat", "lon"), P("rad", "lat", "lon")),
        check_vma=False,
    )
```

```python
import jax
import jax.numpy as jnp
from jax import lax
from jax.experimental import pallas as pl
from jax.experimental.pallas import tpu as pltpu
from jax.sharding import PartitionSpec as P

AXES = ("rad", "lat", "lon")
SIZES = (4, 8, 8)
MESH = pl.DeviceIdType.MESH
F32 = jnp.float32
HI = lax.Precision.HIGHEST
CDEG = 8
CELLS = 32 * 256 * 1024
LEVELS = ((8, 32, 128), (4, 16, 64), (2, 8, 32))
TOP = 8
DEEP_ROWS = {1: 48, 2: 40}
OWN1, OWN2 = pl.ds(16, 16), pl.ds(16, 8)


def cheb_constants(low, high, degree):
    middle, spread = 0.5 * (high + low), 0.5 * (high - low)
    factor = middle / spread
    old = 1.0 / factor
    steps = []
    for _ in range(degree - 1):
        new = 1.0 / (2.0 * factor - old)
        steps.append((new * old, 2.0 * new / spread))
        old = new
    return 1.0 / middle, steps


FIRST, STEPS = cheb_constants(0.5, 2.0, 3)
COARSE_FIRST, COARSE_STEPS = cheb_constants(0.1, 2.0, CDEG)


def lanes_of(shape):
    return lax.broadcasted_iota(jnp.int32, shape, len(shape) - 1)


def rows_of(shape):
    return lax.broadcasted_iota(jnp.int32, shape, len(shape) - 2)


def block(x, rows):
    return pl.ds(pl.multiple_of(x * rows, 8), rows)


def kernel(
    forcing, pressure, viscosity, forward, owner,
    adjoint, pnext, gradient,
    load, base, fwd, base_z, fwd_z,
    buf0, zbuf, faces0, faces1, faces2, links0, diag0, inv0, res0, sol0, rim0, hbuf, hz, applied, mbuf, mz,
    wide0, rim_link, halo_x, halo_y, strain,
    coef1, coef2, inv1, inv2, right1, mid1, left1, right2, deep1, deep2, sol1, sol2,
    zsend1, zgot1, cz, dgot2,
    tmp, flat, erows, tile, got1, got2, summed, sum_x, sum_y, sum_z,
    in_sem, send_sem, recv_sem, fsend, frecv, send1, recv1, send2, recv2, sum_send, sum_recv,
    dsend1, drecv1, dsend2, drecv2, hsend, hrecv, msend, mrecv, csend1, crecv1, csend2, crecv2,
):
    me = tuple(lax.axis_index(a) for a in AXES)
    rad, lat, lon = me

    def device(*steps):
        return tuple(
            lax.rem(m + (s % n), n) if s % n else m for m, s, n in zip(me, steps, SIZES)
        )

    up = [device(1, 0, 0), device(0, 1, 0), device(0, 0, 1)]
    down = [device(-1, 0, 0), device(0, -1, 0), device(0, 0, -1)]
    along = [device(0, 0, k) for k in (4, 3, 5, 2, 6, 1, 7)]
    across = [device(0, k, 0) for k in (4, 3, 5, 2, 6, 1, 7)]
    through = [device(k, 0, 0) for k in range(1, 4)]
    near1 = [
        (a, b, c) for c in (1, -1, 0) for b in (1, -1, 0) for a in (1, -1, 0) if a or b or c
    ]
    near2 = [
        (a, b, c) for c in (1, -1, 0) for a in (2, 1, 3, 0) for b in (1, -1, 0) if a or b or c
    ]
    peers = up + down

    own_rows = pl.ds(TOP, 32)
    loads = [
        pltpu.make_async_copy(viscosity, base.at[0, pl.ds(1, 8), own_rows], in_sem.at[0]),
        pltpu.make_async_copy(pressure, base.at[1, pl.ds(1, 8), own_rows], in_sem.at[1]),
        pltpu.make_async_copy(forcing, load, in_sem.at[2]),
        pltpu.make_async_copy(forward, fwd.at[:, pl.ds(1, 8), own_rows], in_sem.at[3]),
    ]
    for copy in loads:
        copy.start()

    def clear(ref, *at):
        ref[at] = jnp.zeros(ref[at].shape, F32)

    every, low_rows, high_rows = slice(None), slice(8, 16), slice(32, 40)
    for plane in (0, 9):
        clear(base, every, plane, slice(8, 40))
        clear(fwd, every, plane, slice(8, 40))

    barrier = pltpu.get_barrier_semaphore()
    for target in peers:
        pl.semaphore_signal(barrier, inc=1, device_id=target, device_id_type=MESH)

    for plane in (0, 9):
        clear(buf0, every, every, plane, slice(8, 40))
        clear(halo_x, every, plane // 9)
        clear(halo_y, every, plane // 9)
        clear(hbuf, every, plane, slice(8, 40))
        clear(mbuf, every, plane, slice(8, 40))
    clear(buf0, every, every, slice(1, 9), slice(0, 8))
    clear(buf0, every, every, slice(1, 9), slice(40, 48))
    clear(coef1, every, slice(0, 12), low_rows)
    clear(coef1, every, slice(0, 12), slice(32, 48))
    for planes in (slice(0, 4), slice(8, 12)):
        clear(coef1, every, planes, slice(16, 32))
        clear(right1, every, planes, slice(16, 32))
        clear(left1, every, planes, slice(16, 32))
    for ref in (right1, left1):
        clear(ref, every, every, low_rows)
        clear(ref, every, every, high_rows)
    clear(deep1, every, every, every, slice(0, 8))
    clear(deep1, every, every, every, slice(40, 48))
    clear(deep2, every, every, every, slice(0, 8))
    clear(deep2, every, every, every, slice(32, 40))
    for plane in (1, 10):
        clear(coef2, every, plane)
        clear(deep2, every, every, plane)
    clear(coef2, every, every, slice(32, 40))
    for plane in (0, 1, 10, 11):
        clear(sol2, every, plane, slice(8, 32))
    for side in (0, 2):
        clear(zgot1, every, side)

    def remote(src, dst, ssem, rsem, target):
        return pltpu.make_async_remote_copy(
            src_ref=src, dst_ref=dst, send_sem=ssem, recv_sem=rsem,
            device_id=target, device_id_type=MESH,
        )

    lane8 = lanes_of((8, 128))

    zero8 = jnp.zeros((8, 128), F32)

    def pack(accs, planes, x, lows=True, highs=True):
        parts = [p[8 * g : 8 * g + 8] for p in planes for g in range(4)]
        n = len(parts)
        low = high = zero8
        for j, part in enumerate(parts):
            turned = pltpu.roll(part, j, 1) if j else part
            if lows:
                low = jnp.where(lane8 == j, turned, low)
            if highs:
                high = jnp.where(lane8 == (127 + j) % 128, turned, high)
        return (
            accs[0] + pltpu.roll(low, n * x, 1) if lows else accs[0],
            accs[1] + pltpu.roll(high, n * x, 1) if highs else accs[1],
        )

    def merged(before, after):
        before, after = pltpu.roll(before, 1, 1), pltpu.roll(after, 127, 1)
        even = jnp.bitwise_and(lane8, 1) == 0
        return jnp.where(even, before, after), jnp.where(even, after, before)

    def rims_of(halo, n, x):
        turn_back = lax.rem(128 - n * x, 128)
        halo = [pltpu.roll(h, turn_back, 1) for h in halo]
        return [pltpu.roll(halo[j % 2], 128 - j, 1) if j else halo[0] for j in range(n)]

    lane32, lane16 = lanes_of((32, 128)), lanes_of((16, 128))

    def shifted(v, rims):
        rim = jnp.concatenate(rims, 0) if isinstance(rims, list) else rims
        low = jnp.where(lane32 == 0, rim, pltpu.roll(v, 1, 1))
        high = jnp.where(lane32 == 127, rim, pltpu.roll(v, 127, 1))
        return low, high

    def guarded(copy, step):
        sends_it, gets_it = (rad < 3, rad > 0) if step == 1 else (rad > 0, rad < 3)

        def start():
            pl.when(sends_it)(copy.start)

        def arrived():
            pl.when(gets_it)(copy.wait_recv)

        def left():
            pl.when(sends_it)(copy.wait_send)

        return start, arrived, left

    def plain(copy):
        return copy.start, copy.wait_recv, copy.wait_send

    unsettled = []

    def settle():
        for left in unsettled:
            left()
        unsettled.clear()

    def sends(buf, zref, ssem, rsem, beside=None):
        rows, planes = pl.ds(TOP, 32), pl.ds(1, 8)
        if beside is None:
            to = [buf.at[:, 0, rows], buf.at[:, 9, rows], buf.at[:, planes, pl.ds(TOP - 1, 1)], buf.at[:, planes, pl.ds(TOP + 32, 1)]]
        else:
            in_x, in_y = beside
            to = [in_x.at[0], in_x.at[1], in_y.at[0, :, :, pl.ds(0, 1)], in_y.at[1, :, :, pl.ds(7, 1)]]
        parts = [
            (buf.at[:, 8, rows], to[0], up[0]),
            (buf.at[:, 1, rows], to[1], down[0]),
            (buf.at[:, planes, pl.ds(TOP + 31, 1)], to[2], up[1]),
            (buf.at[:, planes, pl.ds(TOP, 1)], to[3], down[1]),
            (zref.at[1], zref.at[2], up[2]),
            (zref.at[0], zref.at[3], down[2]),
        ]
        copies = [
            remote(src, dst, ssem.at[i], rsem.at[i], target)
            for i, (src, dst, target) in enumerate(parts)
        ]
        return [plain(copy) for copy in copies[4:]] + [guarded(copies[0], 1), guarded(copies[1], -1)] + [plain(copy) for copy in copies[2:4]]

    turn = [0]

    def send_all(accs, buf, zref, ssem, rsem, beside=None):
        zref[0], zref[1] = accs
        copies = sends(buf, zref, ssem, rsem, beside)
        for start, _, _ in copies:
            start()
        settle()

        def finish():
            for _, arrived, left in copies:
                arrived()
                unsettled.append(left)
            return merged(zref[2], zref[3])

        return finish

    def exchange(accs, buf=None):
        p = turn[0] % 2
        turn[0] += 1
        sems = (zbuf.at[p], send_sem.at[p], recv_sem.at[p])
        return send_all(accs, buf0.at[p], *sems, (halo_x.at[p], halo_y.at[p])) if buf is None else send_all(accs, buf, *sems)

    for copy in loads[:2]:
        copy.wait()

    def pack_base(x, accs):
        return pack(accs, [base[c, x + 1, own_rows, :] for c in range(2)], x)

    accs = lax.fori_loop(0, 8, pack_base, (zero8, zero8), unroll=2)
    pl.semaphore_wait(barrier, len(peers))
    finish = exchange(accs, base)
    loads[3].wait()

    def pack_fwd(x, accs):
        return pack(accs, [fwd[c, x + 1, own_rows, :] for c in range(3)], x, highs=False)

    fwd_z[0] = lax.fori_loop(0, 8, pack_fwd, (zero8, zero8), unroll=2)[0]
    fwd_parts = [
        (fwd.at[:, 1, own_rows], fwd.at[:, 9, own_rows], down[0]),
        (fwd.at[:, pl.ds(1, 8), pl.ds(TOP, 1)], fwd.at[:, pl.ds(1, 8), pl.ds(TOP + 32, 1)], down[1]),
        (fwd_z.at[0], fwd_z.at[1], down[2]),
    ]
    fwd_copies = [
        remote(src, dst, fsend.at[i], frecv.at[i], target)
        for i, (src, dst, target) in enumerate(fwd_parts)
    ]
    fwd_copies = [guarded(fwd_copies[0], -1)] + [plain(copy) for copy in fwd_copies[1:]]
    for begin, _, _ in fwd_copies:
        begin()

    grid_row, grid_lane = rows_of((128, 128)), lanes_of((128, 128))
    pair = (grid_row // 2 == grid_lane).astype(F32)
    own_pair = jnp.where(grid_row < 64, pair, 0.0)
    pick = [(grid_row == 2 * grid_lane + s).astype(F32) for s in range(2)]
    spread0 = (grid_row == grid_lane // 2).astype(F32)
    spread1 = (grid_row == jnp.where(grid_lane < 96, 0, 64) + grid_lane // 2).astype(F32)

    def times(a, b):
        return jnp.dot(a, b, precision=HI, preferred_element_type=F32)

    def edge(x, side, nx):
        at_edge = (rad == 0) & (x == 0) if side == 0 else (rad == 3) & (x == nx - 1)
        return jnp.where(at_edge, 0.0, 1.0).astype(F32)

    def edge_rows(side, ny):
        row = rows_of((ny, 128))
        at_edge = (lat == 0) & (row == 0) if side == 0 else (lat == 7) & (row == ny - 1)
        return jnp.where(at_edge, 0.0, 1.0).astype(F32)

    loads[2].wait()
    halo = finish()

    def setup_plane(x, accs):
        v = base[0, x + 1, own_rows, :]
        rims = rims_of(halo, 8, x)
        low_z, high_z = shifted(v, rims[:4])
        lower_x, upper_x, lower_y, upper_y = edge(x, 0, 8), edge(x, 1, 8), edge_rows(0, 32), edge_rows(1, 32)
        six = [
            0.5 * (v + lower_x * base[0, x, own_rows, :]),
            0.5 * (v + upper_x * base[0, x + 2, own_rows, :]),
            0.5 * (v + lower_y * base[0, x + 1, pl.ds(TOP - 1, 32), :]),
            0.5 * (v + upper_y * base[0, x + 1, pl.ds(TOP + 1, 32), :]),
            0.5 * (v + low_z),
            0.5 * (v + high_z),
        ]
        at = block(x, 32)
        for k in range(6):
            faces0[k, at, :] = six[k]
        masks = (lower_x, upper_x, lower_y, upper_y)
        for k in range(6):
            links0[k, at, :] = six[k] * masks[k] if k < 4 else jnp.where(lane32 == (0, 127)[k - 4], 0.0, six[k])
        rim_link[at, :] = jnp.where(lane32 == 0, six[4], jnp.where(lane32 == 127, six[5], 0.0))
        diag = six[0] + six[1] + six[2] + six[3] + six[4] + six[5]
        inv = 1.0 / diag
        diag0[at, :] = diag
        inv0[at, :] = inv
        p = base[1, x + 1, own_rows, :]
        _, high_p = shifted(p, rims[4:])
        grads = [
            base[1, x + 2, own_rows, :] * upper_x - p,
            base[1, x + 1, pl.ds(TOP + 1, 32), :] * upper_y - p,
            high_p - p,
        ]
        updates = []
        for c in range(3):
            right = load[c, x] - grads[c]
            res0[c, at, :] = right
            update = inv * right * FIRST
            buf0[1, c, x + 1, own_rows, :] = update
            updates.append(update)
        return pack(accs, updates, x)

    start = lax.fori_loop(0, 8, setup_plane, (zero8, zero8))

    def coarsen(level, fine, coarse):
        nx, ny, _ = LEVELS[level]
        half_x, half_y = nx // 2, ny // 2
        n = half_x * half_y

        def one(x, carry):
            for k in range(6):
                way, side = k // 2, k % 2
                if way == 0:
                    plane = fine[k, block(2 * x + side, ny), :]
                else:
                    plane = fine[k, block(2 * x, ny), :] + fine[k, block(2 * x + 1, ny), :]
                tmp[k, pl.ds(0, ny), :] = plane
            for k in range(6):
                way, side = k // 2, k % 2
                if way == 1:
                    both = tmp[k, pl.ds(side, half_y, 2), :]
                else:
                    both = tmp[k, pl.ds(0, half_y, 2), :] + tmp[k, pl.ds(1, half_y, 2), :]
                flat[k, block(x, half_y), :] = both
            return carry

        lax.fori_loop(0, half_x, one, 0)
        sums = times(flat[0:4, :n, :].reshape(4 * n, 128), pair).reshape(4, n, 128)
        for k in range(4):
            coarse[k] = sums[k]
        for k in range(4, 6):
            coarse[k] = times(flat[k, :n, :], pick[k - 4])

    def coefficients(level, faces, x):
        nx, ny, _ = LEVELS[level]
        six = [faces[k, pl.ds(x * ny, ny), :] for k in range(6)]
        total = six[0] + six[1] + six[2] + six[3] + six[4] + six[5]
        return [total, six[0] * edge(x, 0, nx), six[2] * edge_rows(0, ny), six[4]]

    def invert(coef, inv, planes):
        def one(x, carry):
            d = coef[0, x]
            inv[x] = jnp.where(d > 0.0, 1.0 / jnp.where(d > 0.0, d, 1.0), 0.0)
            return carry

        lax.fori_loop(0, planes, one, 0)

    side_lanes = (lane8 < 68) | (lane8 >= 124)

    def exchange1(use, ref, depth_up, depth_down):
        n = ref.shape[0]
        zlow = zhigh = zero8
        for x in range(4):
            for a in range(n):
                for g in range(2):
                    at = 4 * ((x * n + a) * 2 + g)
                    part = ref[a, 4 + x, pl.ds(16 + 8 * g, 8), :]
                    turned = pltpu.roll(part, at, 1) if at else part
                    zlow = jnp.where((lane8 >= at) & (lane8 < at + 4), turned, zlow)
                    top = (60 + at) % 128
                    zhigh = jnp.where((lane8 >= top) & (lane8 < top + 4), turned, zhigh)
        zsend1[use, 0] = zlow
        zsend1[use, 1] = zhigh
        copies = []
        for i, (a, b, c) in enumerate(near1):
            if c:
                src = zsend1.at[use, (c + 1) // 2]
                dst = zgot1.at[use, 1 - a, 1 - b, (1 - c) // 2]
            else:
                from_x, to_x, from_y, to_y = pl.ds(4, 4), pl.ds(4, 4), OWN1, OWN1
                if a == 1:
                    from_x, to_x = pl.ds(8 - depth_up, depth_up), pl.ds(4 - depth_up, depth_up)
                if a == -1:
                    from_x, to_x = pl.ds(4, depth_down), pl.ds(8, depth_down)
                if b == 1:
                    from_y, to_y = pl.ds(28, 4), pl.ds(12, 4)
                if b == -1:
                    from_y, to_y = pl.ds(16, 4), pl.ds(32, 4)
                src, dst = ref.at[:, from_x, from_y], ref.at[:, to_x, to_y]
            copy = remote(src, dst, dsend1.at[use, i], drecv1.at[use, i], device(a, b, c))
            copies.append((a, copy))

        def each(way, do):
            group = [copy for a, copy in copies if a == way]
            for copy in group:
                do(copy)

        for way, there in ((1, rad < 3), (-1, rad > 0)):
            pl.when(there)(lambda way=way: each(way, lambda copy: copy.start()))
        each(0, lambda copy: copy.start())

        def finish(low_plane, high_plane):
            for way, gets_it in ((1, rad > 0), (-1, rad < 3)):
                pl.when(gets_it)(lambda way=way: each(way, lambda copy: copy.wait_recv()))
            each(0, lambda copy: copy.wait_recv())

            for way, sends_it in ((1, rad < 3), (-1, rad > 0)):
                pl.when(sends_it)(lambda way=way: each(way, lambda copy: copy.wait_send()))
            each(0, lambda copy: copy.wait_send())

            def one(plane, carry):
                dx, x = lax.div(plane, 4), lax.rem(plane, 4)
                back = lax.rem(192 - 8 * n * x, 128)
                for dy, groups in ((0, (1,)), (1, (2, 3)), (2, (4,))):
                    above = pltpu.roll(zgot1[use, dx, dy, 1], back, 1)
                    below = pltpu.roll(zgot1[use, dx, dy, 0], back, 1)
                    both = jnp.where((lane8 >= 64) & (lane8 < 96), above, below)
                    for a in range(n):
                        for group in groups:
                            g = (1, group - 2, 0)[dy]
                            at = (128 - 4 * (2 * a + g)) % 128
                            side = pltpu.roll(both, at, 1) if at else both
                            rows = pl.ds(8 * group, 8)
                            own = ref[a, plane, rows, :]
                            side = jnp.where(side_lanes, side, 0.0)
                            ref[a, plane, rows, :] = jnp.where(lane8 < 64, own, side)
                return carry

            lax.fori_loop(low_plane, high_plane, one, 0, unroll=2)

        return finish

    def layers1(use, ref, depth_up, depth_down):
        n = ref.shape[0]

        def go(copies):
            for start, _, _ in copies:
                start()

        def done(copies):
            for _, arrived, left in copies:
                arrived()
                left()

        def copy(i, src, dst, target):
            return remote(src, dst, csend1.at[use, i], crecv1.at[use, i], target)

        planes, zs = pl.ds(0, 12), cz.at[use]
        up_x, down_x = (pl.ds(8 - depth_up, depth_up), pl.ds(4 - depth_up, depth_up)), (pl.ds(4, depth_down), pl.ds(8, depth_down))
        in_x = [
            guarded(copy(0, ref.at[:, up_x[0], OWN1], ref.at[:, up_x[1], OWN1], up[0]), 1),
            guarded(copy(1, ref.at[:, down_x[0], OWN1], ref.at[:, down_x[1], OWN1], down[0]), -1),
        ]
        in_y = [
            plain(copy(2, ref.at[:, planes, pl.ds(28, 4)], ref.at[:, planes, pl.ds(12, 4)], up[1])),
            plain(copy(3, ref.at[:, planes, pl.ds(16, 4)], ref.at[:, planes, pl.ds(32, 4)], down[1])),
        ]
        in_z = [
            plain(copy(4, zs.at[1], zs.at[2], up[2])),
            plain(copy(5, zs.at[0], zs.at[3], down[2])),
        ]
        parts = [(s, a, g) for s in range(2) for a in range(n) for g in range(4)]

        def pack_pair(t, carry):
            zlow = zhigh = zero8
            for j, (s, a, g) in enumerate(parts):
                part = ref[a, 2 * t + s, pl.ds(8 + 8 * g, 8), :]
                turned = pltpu.roll(part, 4 * j, 1) if j else part
                zlow = jnp.where((lane8 >= 4 * j) & (lane8 < 4 * j + 4), turned, zlow)
                top = (60 + 4 * j) % 128
                zhigh = jnp.where((lane8 >= top) & (lane8 < top + 4), turned, zhigh)
            zs[0, t] = zlow
            zs[1, t] = zhigh
            return carry

        def unpack_pair(t, carry):
            below, above = zs[2, t], zs[3, t]
            for m in range(n):
                turn_by = (192 - 32 * m) % 128
                high = pltpu.roll(above, turn_by, 1) if turn_by else above
                low = pltpu.roll(below, turn_by, 1) if turn_by else below
                both = jnp.where((lane8 >= 64) & (lane8 < 96), high, low)
                for j in range(8):
                    s, a, g = parts[8 * m + j]
                    side = pltpu.roll(both, 128 - 4 * j, 1) if j else both
                    rows = pl.ds(8 + 8 * g, 8)
                    own = ref[a, 2 * t + s, rows, :]
                    side = jnp.where(side_lanes, side, 0.0)
                    ref[a, 2 * t + s, rows, :] = jnp.where(lane8 < 64, own, side)
            return carry

        def first():
            go(in_x)

        def second():
            done(in_x)
            go(in_y)

        def third():
            done(in_y)
            lax.fori_loop(0, 6, pack_pair, 0)
            go(in_z)

        def last():
            done(in_z)
            lax.fori_loop(0, 6, unpack_pair, 0)

        return first, second, third, last

    def spread_coef2(tiles):
        ref = dgot2.at[0]
        for i, t in enumerate(tiles):
            ref[rad, 1, 1, i] = t

        def copy(i, src, dst, target):
            return remote(src, dst, csend2.at[i], crecv2.at[i], target)

        steps = [
            [copy(i, ref.at[rad, 1, 1], ref.at[rad, 1, 1], target) for i, target in enumerate(through)],
            [
                copy(3, ref.at[:, 1, 1], ref.at[:, 0, 1], up[1]),
                copy(4, ref.at[:, 1, 1], ref.at[:, 2, 1], down[1]),
            ],
            [
                copy(5, ref.at[:, :, 1], ref.at[:, :, 0], up[2]),
                copy(6, ref.at[:, :, 1], ref.at[:, :, 2], down[2]),
            ],
        ]

        def go(i):
            if i:
                for c in steps[i - 1]:
                    c.wait()
            if i < 3:
                for c in steps[i]:
                    c.start()

        return go

    def exchange2(use, tiles):
        n = len(tiles)
        for i, t in enumerate(tiles):
            dgot2[use, rad, 1, 1, i] = t
        copies = []
        for i, (a, b, c) in enumerate(near2):
            src = dgot2.at[use, rad, 1, 1, pl.ds(0, n)]
            dst = dgot2.at[use, rad, 1 - b, 1 - c, pl.ds(0, n)]
            copies.append(remote(src, dst, dsend2.at[i], drecv2.at[i], device(a, b, c)))
        for copy in copies:
            copy.start()

        def finish():
            for copy in copies:
                copy.wait_recv()
                unsettled.append(copy.wait_send)

        return finish

    def packed2(parts):
        tiles = []
        for i in range(0, len(parts), 4):
            out = zero8
            for j, part in enumerate(parts[i : i + 4]):
                part = pltpu.roll(part, 32 * j, 1) if j else part
                out = jnp.where((lane8 >= 32 * j) & (lane8 < 32 * j + 32), part, out)
            tiles.append(out)
        return tiles

    def turned2(use, source, dy, dz, tile_at, lanes):
        t = dgot2[use, source, dy, dz, tile_at]
        return pltpu.roll(t, lanes % 128, 1) if lanes % 128 else t

    def joined2(use, source, dy, part):
        i, at = part // 4, 32 * (part % 4)
        own = turned2(use, source, dy, 1, i, -at)
        after = turned2(use, source, dy, 2, i, 32 - at)
        before = turned2(use, source, dy, 0, i, 96 - at)
        out = jnp.where(lane8 < 32, own, jnp.where(lane8 < 64, after, before))
        return jnp.where((lane8 < 64) | (lane8 >= 96), out, 0.0)

    def unpack2(use, ref):
        n = ref.shape[0]

        def one(source, carry):
            for a in range(n):
                for x in range(2):
                    for dy in range(3):
                        ref[a, 2 + 2 * source + x, pl.ds(8 + 8 * dy, 8), :] = joined2(use, source, dy, 2 * a + x)
            return carry

        lax.fori_loop(0, 4, one, 0)

    coefs, invs = (None, coef1, coef2), (None, inv1, inv2)
    deeps, sols = (None, deep1, deep2), (None, sol1, sol2)

    def begin_deep(level, res, planes, keep):
        rows = pl.ds(8, DEEP_ROWS[level] - 16)

        def one(x, carry):
            for c in range(3):
                update = FIRST * invs[level][x, rows, :] * res[c, x, rows, :]
                deeps[level][0, c, x, rows, :] = update
                sols[level][c, x, rows, :] = update
            return carry

        lax.fori_loop(planes[0], planes[1], one, 0, unroll=2)

    def sweep_deep(level, p, res, out, planes, step, initial=False, rows=None):
        coef, inv, deep, sol = coefs[level], invs[level], deeps[level], sols[level]
        first, count = (8, DEEP_ROWS[level] - 16) if rows is None else rows
        here, under, over = pl.ds(first, count), pl.ds(first - 1, count), pl.ds(first + 1, count)

        def one(x, carry):
            diag, lower_x, upper_x = coef[0, x, here, :], coef[1, x, here, :], coef[1, x + 1, here, :]
            lower_y, upper_y, lower_z = coef[2, x, here, :], coef[2, x, over, :], coef[3, x, here, :]
            upper_z = pltpu.roll(lower_z, 127, 1)
            for c in range(3):
                v = deep[p, c, x, here, :]
                total = diag * v - lower_x * deep[p, c, x - 1, here, :] - upper_x * deep[p, c, x + 1, here, :]
                total = total - lower_y * deep[p, c, x, under, :] - upper_y * deep[p, c, x, over, :]
                total = total - lower_z * pltpu.roll(v, 1, 1) - upper_z * pltpu.roll(v, 127, 1)
                r = res[c, x, here, :] - total
                out[c, x, here, :] = r
                if step is None:
                    continue
                if initial:
                    update = FIRST * inv[x, here, :] * r
                    sol[c, x, here, :] = sol[c, x, here, :] + v + update
                else:
                    update = step[0] * v + step[1] * inv[x, here, :] * r
                    sol[c, x, here, :] = sol[c, x, here, :] + update
                deep[1 - p, c, x, here, :] = update
            return carry

        lax.fori_loop(planes[0], planes[1], one, 0, unroll=4 if (planes[1] - planes[0]) % 4 == 0 else 2)

    def inside(p, first=False):
        def plane(x, carry):
            at = block(x, 32)
            diag = diag0[at, :]
            ls = [links0[k, at, :] for k in range(6)]
            for c in range(3):
                v = buf0[p, c, x + 1, own_rows, :]
                total = diag * v - ls[0] * buf0[p, c, x, own_rows, :]
                total = total - ls[1] * buf0[p, c, x + 2, own_rows, :]
                total = total - ls[2] * buf0[p, c, x + 1, pl.ds(TOP - 1, 32), :]
                total = total - ls[3] * buf0[p, c, x + 1, pl.ds(TOP + 1, 32), :]
                total = total - ls[4] * pltpu.roll(v, 1, 1) - ls[5] * pltpu.roll(v, 127, 1)
                res0[c, at, :] = res0[c, at, :] - total
                sol0[c, at, :] = v if first else sol0[c, at, :] + v
            return carry

        lax.fori_loop(0, 8, plane, 0, unroll=4)

    def rim_terms(p, halo, step, emit=None):
        for side, rows in ((0, pl.ds(0, 32)), (1, pl.ds(224, 32))):
            link = links0[side, rows, :]
            for c in range(3):
                res0[c, rows, :] = res0[c, rows, :] + link * halo_x[p, side, c]

        def plane(x, accs):
            at = block(x, 32)
            inv, rim = inv0[at, :], rim_link[at, :]
            low_y, high_y = links0[2, block(4 * x, 8), :], links0[3, block(4 * x + 3, 8), :]
            rims = rims_of(halo, 12, x)
            packs = []
            for c in range(3):
                r = res0[c, at, :] + rim * jnp.concatenate(rims[4 * c : 4 * c + 4], 0)
                top = r[0:8] + low_y * halo_y[p, 0, c, x]
                bottom = r[24:32] + high_y * halo_y[p, 1, c, x]
                r = jnp.concatenate([top, r[8:24], bottom], 0)
                if emit is None:
                    res0[c, at, :] = r
                if step is None:
                    continue
                update = step[0] * buf0[p, c, x + 1, own_rows, :] + step[1] * inv * r
                if emit is None:
                    buf0[1 - p, c, x + 1, own_rows, :] = update
                    packs.append(update)
                else:
                    packs.append(sol0[c, at, :] + update)
            if step is None:
                return accs
            if emit is not None:
                emit(packs, x)
            return pack(accs, packs, x)

        return lax.fori_loop(0, 8, plane, (zero8, zero8), unroll=4)

    def correct(p):
        def plane(x, accs):
            at = block(x, 32)
            diag, inv = diag0[at, :], inv0[at, :]
            ls = [links0[k, at, :] for k in range(6)]
            packs = []
            for c in range(3):
                v = wide0[c, x + 1, own_rows, :]
                total = diag * v - ls[0] * wide0[c, x, own_rows, :]
                total = total - ls[1] * wide0[c, x + 2, own_rows, :]
                total = total - ls[2] * wide0[c, x + 1, pl.ds(TOP - 1, 32), :]
                total = total - ls[3] * wide0[c, x + 1, pl.ds(TOP + 1, 32), :]
                total = total - ls[4] * pltpu.roll(v, 1, 1) - ls[5] * pltpu.roll(v, 127, 1)
                r = res0[c, at, :] - total + rim_link[at, :] * rim0[c, x]
                res0[c, at, :] = r
                sol0[c, at, :] = sol0[c, at, :] + v
                update = FIRST * inv * r
                buf0[p, c, x + 1, own_rows, :] = update
                packs.append(update)
            return pack(accs, packs, x)

        return lax.fori_loop(0, 8, plane, (zero8, zero8), unroll=4)

    def restrict(source, rows, level, matrix):
        nx, ny, _ = LEVELS[level]
        half_x, half_y = nx // 2, ny // 2
        n = half_x * half_y

        def one(x, carry):
            for c in range(3):
                tmp[c, pl.ds(0, ny), :] = source(c, 2 * x) + source(c, 2 * x + 1)
            for c in range(3):
                flat[c, block(x, half_y), :] = tmp[c, pl.ds(0, half_y, 2), :] + tmp[c, pl.ds(1, half_y, 2), :]
            return carry

        lax.fori_loop(0, half_x, one, 0)
        return times(flat[0:3, :n, :].reshape(3 * n, 128), matrix)

    def gather(use):
        first = [
            remote(tile.at[use, 0], got1.at[use, lon], send1.at[use, i], recv1.at[use, i], target)
            for i, target in enumerate(along)
        ]
        second = [
            remote(tile.at[use, 1], got2.at[use, block(lat, 8)], send2.at[use, i], recv2.at[use, i], target)
            for i, target in enumerate(across)
        ]

        def begin(value):
            tile[use, 0] = value
            got1[use, lon] = value
            for copy in first:
                copy.start()

        def middle():
            for copy in first:
                copy.wait_recv()
                unsettled.append(copy.wait_send)
            total = got1[use, 0]
            for k in range(1, 8):
                total = total + got1[use, k]
            tile[use, 1] = total
            got2[use, block(lat, 8), :] = total
            for copy in second:
                copy.start()

        def end():
            for copy in second:
                copy.wait_recv()
                unsettled.append(copy.wait_send)

        return begin, middle, end

    lane1 = lanes_of((1, 128))
    runs = jnp.bitwise_and(owner[0, 0:1, :], 31)
    runs = jnp.concatenate([runs, jnp.full((1, 96), -1, jnp.int32)], 1)

    def member_of(columns):
        return (grid_row == jnp.broadcast_to(columns, (128, 128))).astype(F32)

    own_member = member_of(runs)

    def to_runs(rows):
        return lax.dot_general(
            rows, own_member, (((1,), (1,)), ((), ())), precision=HI, preferred_element_type=F32
        )

    def stacked(rows, count=8):
        out = jnp.zeros((count, 128), F32)
        at = rows_of((count, 128))
        for i, row in enumerate(rows):
            out = jnp.where(at == i, jnp.broadcast_to(row, (count, 128)), out)
        return out

    def rowsum(plane):
        return jnp.sum(plane, axis=0, keepdims=True)

    def run_sides():
        f = faces2
        wide = jnp.broadcast_to(runs, (8, 128))
        first_cell = (lane1 == 0) | (runs != pltpu.roll(wide, 1, 1)[0:1])
        last_cell = (lane1 == 31) | (runs != pltpu.roll(wide, 127, 1)[0:1])
        sides = [
            rowsum(f[0, 0:8, :]),
            rowsum(f[1, 8:16, :]),
            f[2, 0:1, :] + f[2, 8:9, :],
            f[3, 7:8, :] + f[3, 15:16, :],
            jnp.where(first_cell, rowsum(f[4, 0:8, :] + f[4, 8:16, :]), 0.0),
            jnp.where(last_cell, rowsum(f[5, 0:8, :] + f[5, 8:16, :]), 0.0),
        ]
        whole = sides[0] + sides[1] + sides[2] + sides[3] + sides[4] + sides[5]
        return to_runs(stacked([sides[0], sides[2], sides[4], whole]))

    def coarse_solve(meanwhile):
        begin, middle, end = gather(0)
        rows = []
        for block_x in range(4):
            for c in range(3):
                both = right2[c, 2 + 2 * block_x, OWN2, :] + right2[c, 3 + 2 * block_x, OWN2, :]
                rows.append(rowsum(both))
        sums = to_runs(stacked(rows, 16))
        row8 = rows_of((8, 128))
        value = zero8
        for block_x in range(4):
            part = jnp.where(row8 < 3, 0.0, pltpu.roll(dgot2[0, block_x, 1, 1, 2], 2, 0))
            for c in range(3):
                row = jnp.broadcast_to(sums[3 * block_x + c : 3 * block_x + c + 1], (8, 128))
                part = jnp.where(row8 == c, row, part)
            value = value + (pltpu.roll(part, 32 * block_x, 1) if block_x else part)
        begin(value)
        meanwhile[0]()
        middle()
        meanwhile[1]()
        end()

        def all_of(i):
            return got2[0, pl.ds(i, 8, 8), :]

        wrap = jnp.bitwise_and(lane8, 31)

        def lower_z(v):
            return jnp.where(wrap == 0, pltpu.roll(v, 97, 1), pltpu.roll(v, 1, 1))

        def upper_z(v):
            return jnp.where(wrap == 31, pltpu.roll(v, 31, 1), pltpu.roll(v, 127, 1))

        link_x = jnp.where(lane8 < 32, 0.0, all_of(3))
        link_y = jnp.where(row8 == 0, 0.0, all_of(4))
        link_z = all_of(5)
        link_xu, link_yu, link_zu = pltpu.roll(link_x, 96, 1), pltpu.roll(link_y, 7, 0), upper_z(link_z)
        diagonal = all_of(6)
        inverse = 1.0 / diagonal

        def operate(v):
            out = diagonal * v - link_x * pltpu.roll(v, 32, 1) - link_xu * pltpu.roll(v, 96, 1)
            out = out - link_y * pltpu.roll(v, 1, 0) - link_yu * pltpu.roll(v, 7, 0)
            return out - link_z * lower_z(v) - link_zu * upper_z(v)

        rs = [all_of(c) for c in range(3)]
        ds = [inverse * r * COARSE_FIRST for r in rs]
        es = list(ds)
        for a, b in COARSE_STEPS:
            rs = [r - operate(d) for r, d in zip(rs, ds)]
            ds = [a * d + b * inverse * r for r, d in zip(rs, ds)]
            es = [e + d for e, d in zip(es, ds)]
        for c in range(3):
            erows[c] = es[c]
        lats = [lax.rem(lat + 7, 8), lat, lax.rem(lat + 1, 8)]
        rows = [erows[c, pl.ds(at, 1), :] for c in range(3) for at in lats]
        rows = stacked(rows, 16)
        rows = [rows if k == 0 else pltpu.roll(rows, 128 - 32 * k, 1) for k in range(4)]
        spans = times(jnp.concatenate(rows, 0), region_member())
        for block_x in range(4):
            for c in range(3):
                for dy in range(3):
                    i = 16 * block_x + 3 * c + dy
                    row = jnp.broadcast_to(spans[i : i + 1], (8, 128))
                    for x in range(2):
                        deep2[1, c, 2 + 2 * block_x + x, pl.ds(8 + 8 * dy, 8), :] = row

    def region_member():
        own, before, after = (turned2(0, rad, 1, k, 2, t)[0:1] for k, t in ((1, 0), (0, 96), (2, 32)))
        columns = jnp.where(lane1 < 32, own, jnp.where(lane1 < 64, after, before))
        columns = jnp.where((lane1 < 64) | (lane1 >= 96), columns, -1.0).astype(jnp.int32)
        return member_of(columns)

    pending = {}

    def while_first():
        coarsen(0, faces0, faces1)
        for x in range(4):
            for k, value in enumerate(coefficients(1, faces1, x)):
                coef1[k, 4 + x, OWN1, :] = value
        pending["coef1"] = layers1(0, coef1, 3, 4)
        pending["coef1"][0]()

    def while_second():
        pending["coef1"][1]()
        coarsen(1, faces1, faces2)
        values = [coefficients(2, faces2, x) for x in range(2)]
        last = jnp.where(rows_of((8, 128)) == 0, runs.astype(F32), pltpu.roll(run_sides(), 1, 0))
        parts = packed2([values[x][k] for k in range(4) for x in range(2)])
        pending["coef2"] = spread_coef2(parts + [last])
        pending["coef2"](0)

    def weigh_all():
        def weigh(x, accs):
            v, inv = base[0, x + 1, own_rows, :], inv0[block(x, 32), :]
            parts = [2.0 * inv * (v - faces0[2 * c + 1, block(x, 32), :]) for c in range(3)]
            for c in range(3):
                hbuf[c, x + 1, own_rows, :] = parts[c]
            return pack(accs, parts, x)

        accs = lax.fori_loop(0, 8, weigh, (zero8, zero8), unroll=2)
        pending["h"] = send_all(accs, hbuf, hz, hsend, hrecv)

    def applied_to(buf, halo, x):
        at = block(x, 32)
        rims = rims_of(halo, 12, x)
        out = []
        for c in range(3):
            v = buf[c, x + 1, own_rows, :]
            total = diag0[at, :] * v - links0[0, at, :] * buf[c, x, own_rows, :]
            total = total - links0[1, at, :] * buf[c, x + 2, own_rows, :]
            total = total - links0[2, at, :] * buf[c, x + 1, pl.ds(TOP - 1, 32), :]
            total = total - links0[3, at, :] * buf[c, x + 1, pl.ds(TOP + 1, 32), :]
            total = total - links0[4, at, :] * pltpu.roll(v, 1, 1) - links0[5, at, :] * pltpu.roll(v, 127, 1)
            out.append(total - rim_link[at, :] * jnp.concatenate(rims[4 * c : 4 * c + 4], 0))
        return out

    def apply_to_h():
        halo = pending["h"]()

        def one(x, accs):
            at = block(x, 32)
            v, inv = base[0, x + 1, own_rows, :], inv0[at, :]
            parts = []
            for c, g in enumerate(applied_to(hbuf, halo, x)):
                u = (1.0 + STEPS[1][0]) * 2.0 * (v - faces0[2 * c + 1, at, :]) - STEPS[1][1] * g
                applied[c, at, :] = u
                m = STEPS[0][1] * inv * u + STEPS[1][1] * hbuf[c, x + 1, own_rows, :]
                mbuf[c, x + 1, own_rows, :] = m
                parts.append(m)
            return pack(accs, parts, x)

        accs = lax.fori_loop(0, 8, one, (zero8, zero8), unroll=2)
        pending["m"] = send_all(accs, mbuf, mz, msend, mrecv)

    def apply_to_m():
        halo = pending["m"]()

        def one(x, carry):
            at = block(x, 32)
            for c, g in enumerate(applied_to(mbuf, halo, x)):
                applied[c, at, :] = STEPS[0][0] * applied[c, at, :] - g
            return carry

        lax.fori_loop(0, 8, one, 0, unroll=2)

    def while_third():
        pending["coef1"][2]()
        pending["coef2"](1)

    accs = start
    for step, meanwhile in ((STEPS[0], while_first), (STEPS[1], while_second), (None, while_third)):
        p = turn[0] % 2
        finish = exchange(accs)
        inside(p, meanwhile is while_first)
        meanwhile()
        accs = rim_terms(p, finish(), step)

    sums = restrict(lambda c, x: res0[c, block(x, 32), :], 32, 0, pair)
    for c in range(3):
        for x in range(4):
            right1[c, 4 + x, OWN1, :] = sums[64 * c + 16 * x : 64 * c + 16 * x + 16]
    finish = exchange1(0, right1, 3, 3)
    pending["coef1"][3]()
    invert(coef1, inv1, 12)
    pending["coef2"](2)
    weigh_all()
    finish(1, 11)
    begin_deep(1, right1, (1, 11), None)
    sweep_deep(1, 0, right1, mid1, (2, 10), STEPS[0])
    sweep_deep(1, 1, mid1, mid1, (3, 9), STEPS[1])
    sweep_deep(1, 0, mid1, left1, (4, 8), None, rows=(16, 16))

    sums = restrict(lambda c, x: left1[c, 4 + x, OWN1, :], 16, 1, own_pair)
    finish2 = exchange2(1, packed2([sums[16 * c + 8 * x : 16 * c + 8 * x + 8] for c in range(3) for x in range(2)]))
    rest = layers1(1, left1, 3, 3)
    rest[0]()
    settle()
    pending["coef2"](3)
    unpack2(0, coef2)
    invert(coef2, inv2, 12)
    apply_to_h()
    rest[1]()
    finish2()
    unpack2(1, right2)
    all2 = (2, 10)
    begin_deep(2, right2, all2, None)
    sweep_deep(2, 0, right2, right2, all2, STEPS[0])
    sweep_deep(2, 1, right2, right2, all2, STEPS[1])
    sweep_deep(2, 0, right2, right2, all2, None)

    def forward_strain():
        for _, arrived, left in fwd_copies:
            arrived()
            left()
        fwd_halo = merged(zero8, fwd_z[1])

        def one(x, carry):
            at = block(x, 32)
            v = base[0, x + 1, own_rows, :]
            keep_x, keep_y = edge(x, 1, 8), edge_rows(1, 32)
            rims = rims_of(fwd_halo, 12, x)
            gf = []
            for c in range(3):
                w = fwd[c, x + 1, own_rows, :]
                _, high_w = shifted(w, rims[4 * c : 4 * c + 4])
                gf.append([
                    fwd[c, x + 2, own_rows, :] * keep_x - w,
                    fwd[c, x + 1, pl.ds(TOP + 1, 32), :] * keep_y - w,
                    high_w - w,
                ])
            for c in range(3):
                strain[c, at, :] = 2.0 * v * gf[c][c]
            for i, (d, e) in enumerate(((0, 1), (0, 2), (1, 2))):
                strain[3 + i, at, :] = v * (gf[e][d] + gf[d][e])
            return carry

        lax.fori_loop(0, 8, one, 0)

    def while_along():
        rest[2]()
        settle()
        apply_to_m()
        forward_strain()

    coarse_solve((while_along, rest[3]))
    sweep_deep(2, 1, right2, right2, all2, STEPS[0], initial=True)
    sweep_deep(2, 0, right2, right2, all2, STEPS[0])
    sweep_deep(2, 1, right2, right2, all2, STEPS[1])

    def gather_rows(k, carry):
        for c in range(3):
            flat[c, block(k, 16), :] = sol2[c, 2 * rad + k, pl.ds(12, 16), :]
        return carry

    lax.fori_loop(0, 6, gather_rows, 0)
    for c in range(3):
        flat[c, 0:96, :] = times(flat[c, 0:96, :], spread1)

    def to_level1(k, carry):
        for c in range(3):
            value = flat[c, block(k, 16), :]
            for s in range(2):
                for t in range(2):
                    deep1[1, c, 2 * k + s, pl.ds(8 + t, 16, 2), :] = value
        return carry

    lax.fori_loop(0, 6, to_level1, 0)
    sweep_deep(1, 1, left1, left1, (1, 11), STEPS[0], initial=True)
    sweep_deep(1, 0, left1, left1, (2, 10), STEPS[0])
    sweep_deep(1, 1, left1, left1, (3, 9), STEPS[1])

    for c in range(3):
        flat[c] = times(sol1[c, 3:9, 12:36, :].reshape(144, 128), spread0)

    for k in range(6):
        for c in range(3):
            value = flat[c, 24 * k : 24 * k + 24, :]
            tmp[c, pl.ds(0, 24, 2), :] = value
            tmp[c, pl.ds(1, 24, 2), :] = value
            if 1 <= k <= 4:
                coarse = sol1[c, 3 + k, OWN1, :]
                rim = jnp.where(lane16 == 0, pltpu.roll(coarse, 1, 1), pltpu.roll(coarse, 63, 1))
                tmp[3 + c, pl.ds(0, 16, 2), :] = rim
                tmp[3 + c, pl.ds(1, 16, 2), :] = rim
        for c in range(3):
            for at in (2 * k - 1, 2 * k):
                if 0 <= at <= 9:
                    wide0[c, at] = tmp[c, pl.ds(0, 48), :]
                if 1 <= at <= 8:
                    rim0[c, at - 1] = tmp[3 + c, pl.ds(0, 32), :]

    p = turn[0] % 2
    accs = correct(p)
    finish = exchange(accs)

    def add_up(x, total):
        at = block(x, 32)
        v = base[0, x + 1, own_rows, :]
        part = base[1, x + 1, own_rows, :]
        for c in range(3):
            update = buf0[p, c, x + 1, own_rows, :]
            part = part - 2.0 * (v - faces0[2 * c + 1, at, :]) * (sol0[c, at, :] + update)
            part = part - mbuf[c, x + 1, own_rows, :] * res0[c, at, :] - applied[c, at, :] * update
        return total + (part[0:8] + part[8:16] + part[16:24] + part[24:32])

    partial = lax.fori_loop(0, 8, add_up, zero8, unroll=2)
    rounds = []
    for i, (got, at, targets) in enumerate(((sum_z, lon, along), (sum_y, lat, across), (sum_x, rad, through))):
        copies = [
            remote(summed.at[i], got.at[at], sum_send.at[i, k], sum_recv.at[i, k], target)
            for k, target in enumerate(targets)
        ]
        rounds.append((got, at, copies))

    def send_sum(i, value):
        got, at, copies = rounds[i]
        summed[i] = value
        got[at] = value
        for copy in copies:
            copy.start()

    def get_sum(i):
        got, _, copies = rounds[i]
        for copy in copies:
            copy.wait_recv()
            unsettled.append(copy.wait_send)
        total = got[0]
        for k in range(1, len(copies) + 1):
            total = total + got[k]
        return total

    send_sum(0, partial)
    inside(p)
    accs = rim_terms(p, finish(), STEPS[0])
    p = turn[0] % 2
    finish = exchange(accs)
    inside(p)
    send_sum(1, get_sum(0))

    def emit(afters, x):
        for c, after in enumerate(afters):
            adjoint[c, x] = after
            wide0[c, x + 1, own_rows, :] = after

    accs = rim_terms(p, finish(), STEPS[1], emit=emit)

    finish = exchange(accs, wide0)
    send_sum(2, get_sum(1))
    halo = finish()

    def outputs(x, carry):
        v = base[0, x + 1, own_rows, :]
        keep_x, keep_y = edge(x, 1, 8), edge_rows(1, 32)
        ga, us = [], []
        rims = rims_of(halo, 12, x)
        for c in range(3):
            u = wide0[c, x + 1, own_rows, :]
            low_z, high_z = shifted(u, rims[4 * c : 4 * c + 4])
            ga.append([
                wide0[c, x + 2, own_rows, :] * keep_x - u,
                wide0[c, x + 1, pl.ds(TOP + 1, 32), :] * keep_y - u,
                high_z - u,
            ])
            us.append((u, low_z))
        divergence = (
            us[0][0] - edge(x, 0, 8) * wide0[0, x, own_rows, :]
            + (us[1][0] - edge_rows(0, 32) * wide0[1, x + 1, pl.ds(TOP - 1, 32), :])
            + (us[2][0] - us[2][1])
        )
        pnext[x] = base[1, x + 1, own_rows, :] - v * divergence
        at = block(x, 32)
        total = strain[0, at, :] * ga[0][0] + strain[1, at, :] * ga[1][1] + strain[2, at, :] * ga[2][2]
        for i, (d, e) in enumerate(((0, 1), (0, 2), (1, 2))):
            total = total + strain[3 + i, at, :] * (ga[e][d] + ga[d][e])
        gradient[x] = total
        return carry

    lax.fori_loop(0, 8, outputs, 0, unroll=4)
    mean = jnp.sum(get_sum(2)) / CELLS
    settle()

    def shift(x, carry):
        pnext[x] = pnext[x] - mean
        return carry

    lax.fori_loop(0, 8, shift, 0)


def per_device(forcing, pressure, viscosity, forward, owner):
    vmem, anywhere = pl.BlockSpec(memory_space=pltpu.VMEM), pl.BlockSpec(memory_space=pl.ANY)
    f32 = lambda *shape: pltpu.VMEM(shape, F32)
    dma = lambda *shape: pltpu.SemaphoreType.DMA(shape)
    return pl.pallas_call(
        kernel,
        out_shape=(
            jax.ShapeDtypeStruct((3, 8, 32, 128), F32),
            jax.ShapeDtypeStruct((8, 32, 128), F32),
            jax.ShapeDtypeStruct((8, 32, 128), F32),
        ),
        in_specs=[anywhere] * 4 + [vmem],
        out_specs=(vmem, vmem, vmem),
        scratch_shapes=[
            f32(3, 8, 32, 128), f32(2, 10, 48, 128), f32(3, 10, 48, 128), f32(1, 8, 128), f32(2, 8, 128),
            f32(2, 3, 10, 48, 128), f32(2, 4, 8, 128), f32(6, 256, 128), f32(6, 64, 128), f32(6, 16, 128),
            f32(6, 256, 128), f32(256, 128), f32(256, 128), f32(3, 256, 128), f32(3, 256, 128), f32(3, 8, 32, 128),
            f32(3, 10, 48, 128), f32(4, 8, 128), f32(3, 256, 128), f32(3, 10, 48, 128), f32(4, 8, 128),
            f32(3, 10, 48, 128), f32(256, 128), f32(2, 2, 3, 32, 128), f32(2, 2, 3, 8, 8, 128), f32(6, 256, 128),
            f32(4, 13, 48, 128), f32(4, 12, 40, 128), f32(12, 48, 128), f32(12, 40, 128),
            f32(3, 12, 48, 128), f32(3, 12, 48, 128), f32(3, 12, 48, 128), f32(3, 12, 40, 128),
            f32(2, 3, 12, 48, 128), f32(2, 3, 12, 40, 128), f32(3, 12, 48, 128), f32(3, 12, 40, 128),
            f32(1, 2, 8, 128), f32(1, 3, 3, 2, 8, 128), f32(2, 4, 6, 8, 128), f32(2, 4, 3, 3, 3, 8, 128),
            f32(6, 48, 128), f32(6, 144, 128), f32(3, 8, 128), f32(1, 2, 8, 128),
            f32(1, 8, 8, 128), f32(1, 64, 128), f32(3, 8, 128), f32(4, 8, 128), f32(8, 8, 128), f32(8, 8, 128),
            dma(4), dma(2, 6), dma(2, 6), dma(3), dma(3), dma(1, 7), dma(1, 7), dma(1, 7), dma(1, 7), dma(3, 7), dma(3, 7),
            dma(1, 26), dma(1, 26), dma(35), dma(35), dma(6), dma(6), dma(6), dma(6), dma(2, 6), dma(2, 6), dma(7), dma(7),
        ],
        compiler_params=pltpu.CompilerParams(
            collective_id=0, has_side_effects=True, vmem_limit_bytes=60 * 1024 * 1024
        ),
    )(forcing, pressure, viscosity, forward, owner)


def solution(mesh):
    placed = (
        P(None, "rad", "lat", "lon"),
        P("rad", "lat", "lon"),
        P("rad", "lat", "lon"),
        P(None, "rad", "lat", "lon"),
        P("rad", "lat", "lon"),
    )
    return jax.shard_map(
        per_device,
        mesh=mesh,
        in_specs=placed,
        out_specs=(P(None, "rad", "lat", "lon"), P("rad", "lat", "lon"), P("rad", "lat", "lon")),
        check_vma=False,
    )
```
